128 devices in a mesh: rep: 8 (over z, y_hi), tp: 16 (over y_lo, x, core).
Axes of the slice: x: 4, y: 4 (y_hi: 2, y_lo: 2; y = y_hi * 2 + y_lo), z: 4, core: 2. Of those that a mesh axis runs over, the one named last changes fastest.
Arguments:
- tokens: bfloat16 [8192, 2560], P('rep', 'tp'), may hold values from -6 to 6
- output_grads: bfloat16 [8192, 14336], P('rep', 'tp'), may hold values from -6 to 6
- momentum: bfloat16 [8, 2560, 14336], P('rep', None, 'tp'), may hold values from -1.1953125 to 1.1953125
- component_picks: int32 [8, 40, 224, 32], P(None, None, 'tp'), may hold values from 0 to 4095, as said below
Outputs:
- new_momentum: bfloat16 [8, 2560, 14336], P('rep', None, 'tp')
- update: bfloat16 [2560, 14336], P(None, 'tp')
The draws below stay inside these ranges and needn't reach their ends.
Inputs may be any that keep to these rules, and one draw needn't show every extreme that they name: `component_picks`: pick k of each block lies in k * 128 to (k + 1) * 128 - 1, so the picks of one block are distinct.
All inputs are finite; a program needn't handle non-finite values.
Results may differ from the reference program's by a relative error of at most 0.001.
Values may be sent and summed in bfloat16 or wider, within the bound.
A program may use at most 256 MiB of HBM per device.

```python
import math
import jax
import jax.numpy as jnp
from jax import lax

D = 2560
FF = 14336
ROWS = 1024
BLOCK = 64
PICKS = 32
STRIDE = 128
DBLOCKS = 40
FBLOCKS = 224
ALL_ROWS = 8192
N_REP = 8


def draw_component_picks(key, part):
    key = jax.random.fold_in(key, 7)
    offsets = jax.random.randint(key, (N_REP, DBLOCKS, FBLOCKS, PICKS), 0, STRIDE, dtype=jnp.int32)
    return offsets + STRIDE * jnp.arange(PICKS, dtype=jnp.int32)


def steps_of(own_key, dims, shards, smallest, largest):
    def one(dim, shards_of):
        heights = jax.random.uniform(jax.random.fold_in(jax.random.fold_in(own_key, 6), dim), (shards_of,), jnp.float32, smallest / len(shards), largest / len(shards))
        return jnp.repeat(jnp.exp(heights), dims[dim] // shards_of).reshape((-1,) + (1,) * (len(dims) - dim - 1))

    level = one(*shards[0])
    for cut in shards[1:]:
        level = level * one(*cut)
    return level


def normal_values(stream_key, dims, deviation, limit, cuts=(), held_as=jnp.bfloat16):
    values = jax.random.normal(stream_key, dims, jnp.float32) * deviation
    if len(cuts) > 0:
        values = steps_of(stream_key, dims, cuts, -0.22, 0.18) * values
    return jnp.clip(values, min=-limit, max=limit).astype(held_as)


def setup_inputs(seed: int = 0) -> dict:
    streams_of = jax.random.split(jax.random.key(seed), 5)
    return {
        "tokens": normal_values(streams_of[0], (ALL_ROWS, D), 1.0, 6.0, ((0, 8), (1, 16))),
        "output_grads": normal_values(streams_of[1], (ALL_ROWS, FF), 1.0, 6.0, ((0, 8), (1, 16))),
        "momentum": normal_values(streams_of[2], (N_REP, D, FF), 0.2, 1.1953125, ((0, 8), (2, 16))),
        "component_picks": draw_component_picks(jax.random.fold_in(streams_of[4], 71), 0),
    }


DECAY = 0.9
EPSILON = 1e-06
PRECISE = lax.Precision.HIGHEST

def cosine_table():
    frequency = jnp.arange(BLOCK, dtype=jnp.float32)[:, None]
    position = jnp.arange(BLOCK, dtype=jnp.float32)[None, :]
    weights_norm = jnp.where(frequency == 0, math.sqrt(1.0 / BLOCK), math.sqrt(2.0 / BLOCK))
    return weights_norm * jnp.cos(math.pi * (2.0 * position + 1.0) * frequency / (2.0 * BLOCK))

def to_spectrum(grid_in, cosine):
    row_total, col_total = grid_in.shape
    stacked = grid_in.reshape(row_total // BLOCK, BLOCK, col_total)
    halfway = jnp.einsum('ai,pic->pac', cosine, stacked, precision=PRECISE)
    spread = halfway.reshape(row_total, col_total // BLOCK, BLOCK)
    result = jnp.einsum('rbj,cj->rbc', spread, cosine, precision=PRECISE)
    return result.reshape(row_total, col_total)

def from_spectrum(grid_in, cosine):
    row_total, col_total = grid_in.shape
    stacked = grid_in.reshape(row_total // BLOCK, BLOCK, col_total)
    halfway = jnp.einsum('ai,pac->pic', cosine, stacked, precision=PRECISE)
    spread = halfway.reshape(row_total, col_total // BLOCK, BLOCK)
    result = jnp.einsum('rbc,cj->rbj', spread, cosine, precision=PRECISE)
    return result.reshape(row_total, col_total)

def pick_positions(pick_index, col_count):
    freq_row = pick_index // BLOCK
    freq_col = pick_index % BLOCK
    row_block = jnp.arange(pick_index.shape[-3], dtype=jnp.int32)[:, None, None]
    col_block = jnp.arange(pick_index.shape[-2], dtype=jnp.int32)[None, :, None]
    return (row_block * BLOCK + freq_row) * col_count + col_block * BLOCK + freq_col

def block_rescale(summed):
    row_total, col_total = summed.shape
    tiles = summed.reshape(row_total // BLOCK, BLOCK, col_total // BLOCK, BLOCK)
    mean_square = lax.optimization_barrier(jnp.mean(tiles * tiles, axis=(1, 3), keepdims=True))
    return (tiles * lax.rsqrt(mean_square + EPSILON)).reshape(row_total, col_total)

def reference(tokens, output_grads, momentum, component_picks):
    cosine = cosine_table()
    dense_sum = jnp.zeros((D * FF,), jnp.float32)
    results = []
    for group_index in range(N_REP):
        token_rows = tokens[group_index * ROWS:(group_index + 1) * ROWS]
        grad_rows = output_grads[group_index * ROWS:(group_index + 1) * ROWS]
        gradient = lax.dot_general(token_rows, grad_rows, (((0,), (0,)), ((), ())), preferred_element_type=jnp.float32)
        moved = DECAY * momentum[group_index].astype(jnp.float32) + gradient * (1.0 / math.sqrt(ROWS))
        spectrum = to_spectrum(moved, cosine).reshape(-1)
        positions = pick_positions(component_picks[group_index], FF).reshape(-1)
        values = jnp.take(spectrum, positions)
        remaining = spectrum.at[positions].set(0.0)
        results.append(from_spectrum(remaining.reshape(D, FF), cosine).astype(jnp.bfloat16))
        dense_sum = dense_sum.at[positions].add(values)
    summed = from_spectrum(dense_sum.reshape(D, FF), cosine)
    update = block_rescale(summed).astype(jnp.bfloat16)
    return (jnp.stack(results), update)
```

```python
import functools
import math

import jax
import jax.numpy as jnp
import ml_dtypes
import numpy as np
from jax import lax
from jax.experimental import pallas as pl
from jax.experimental.pallas import tpu as pltpu
from jax.sharding import PartitionSpec as P

ROWS = 1024
BLOCK = 64
HALF = 32
FIVE = 5
CHUNK = FIVE * BLOCK
LANES = 128
DECAY = 0.9
EPSILON = 1e-06
BF = jnp.bfloat16
F32 = jnp.float32


def split_table(table):
    high = table.astype(ml_dtypes.bfloat16)
    low = (table - high.astype(np.float64)).astype(ml_dtypes.bfloat16)
    return high, low


def tables(width):
    frequency = np.arange(BLOCK, dtype=np.float64)[:, None]
    position = np.arange(BLOCK, dtype=np.float64)[None, :]
    norm = np.where(frequency == 0, math.sqrt(1.0 / BLOCK), math.sqrt(2.0 / BLOCK))
    cosine = norm * np.cos(math.pi * (2.0 * position + 1.0) * frequency / (2.0 * BLOCK))
    ordered = np.concatenate([cosine[0::2], cosine[1::2]])

    def rows_table(matrix):
        high, low = split_table(matrix)
        return np.concatenate([high, high, low], axis=1)

    def lanes_table(matrix):
        pair = np.zeros((LANES, LANES))
        pair[:BLOCK, :BLOCK] = matrix
        pair[BLOCK:, BLOCK:] = matrix
        high, low = split_table(pair)
        return np.concatenate(
            [np.concatenate([high, low], axis=1), np.concatenate([high, np.zeros_like(low)], axis=1)]
        )

    slot = np.arange(LANES)[:, None] % 16
    block = np.arange(width)[None, :] // BLOCK
    expand = (slot == block).astype(ml_dtypes.bfloat16)
    same = (np.arange(LANES)[:, None] // BLOCK == np.arange(LANES)[None, :] // BLOCK).astype(ml_dtypes.bfloat16)
    return {
        "row_fwd": rows_table(ordered),
        "row_inv": rows_table(ordered.T),
        "lane_fwd": lanes_table(cosine.T),
        "lane_inv": lanes_table(cosine),
        "expand": expand,
        "expand2": np.concatenate([expand, expand]),
        "compress": np.ascontiguousarray(expand.T),
        "same": same,
    }


def dot(a, b):
    return jnp.dot(a, b, preferred_element_type=F32)


def split(value):
    high = value.astype(BF)
    return high, (value - high.astype(F32)).astype(BF)


def lane_transform(high, low, weights):
    groups = high.shape[1] // LANES
    parts = []
    for group in range(groups):
        cut = slice(group * LANES, (group + 1) * LANES)
        both = dot(jnp.concatenate([high[:, cut], low[:, cut]], axis=1), weights)
        parts.append(both[:, :LANES] + both[:, LANES:])
    return jnp.concatenate(parts, axis=1)


def own_slots(shape):
    row = lax.broadcasted_iota(jnp.int32, shape, 0) // HALF
    lane = lax.broadcasted_iota(jnp.int32, shape, 1) // 16
    return lane == row


def lane_in_block(shape):
    return (lax.broadcasted_iota(jnp.int32, shape, 1) % BLOCK).astype(F32)


def grad_kernel(xt_ref, g_ref, mom_ref, off_ref, rowf_ref, rowi_ref, lanef_ref, lanei_ref, exp_ref, comp_ref, new_ref, val_ref, moved_ref):
    moved_ref[...] = dot(xt_ref[...], g_ref[...]) + DECAY * mom_ref[...].astype(F32)
    off = jnp.concatenate([off_ref[0]] * FIVE, axis=0)
    slots = own_slots((FIVE * HALF, LANES))
    off = jnp.where(slots, off, 0.0).astype(BF)
    offsets = dot(off, exp_ref[...])
    odd = offsets >= BLOCK
    picked_rows = []
    for p in range(FIVE):
        high, low = split(moved_ref[p * BLOCK:(p + 1) * BLOCK, :])
        freq = dot(rowf_ref[...], jnp.concatenate([high, low, high], axis=0))
        cut = slice(p * HALF, (p + 1) * HALF)
        picked_rows.append(jnp.where(odd[cut], freq[HALF:], freq[:HALF]))
    high, low = split(jnp.concatenate(picked_rows, axis=0))
    spectrum = lane_transform(high, low, lanef_ref[...])
    column = jnp.where(odd, offsets - BLOCK, offsets)
    picked = jnp.where(column == lane_in_block(offsets.shape), spectrum, 0.0)
    high, low = split(picked)
    values = dot(high, comp_ref[...]) + dot(low, comp_ref[...])
    values = jnp.where(slots, values, 0.0)
    val_ref[0] = sum(values[p * HALF:(p + 1) * HALF] for p in range(FIVE))
    spread = lane_transform(high, low, lanei_ref[...])
    for p in range(FIVE):
        cut = slice(p * HALF, (p + 1) * HALF)
        part = spread[cut]
        high, low = split(jnp.concatenate([jnp.where(odd[cut], 0.0, part), jnp.where(odd[cut], part, 0.0)], axis=0))
        taken = dot(rowi_ref[...], jnp.concatenate([high, low, high], axis=0))
        rows = slice(p * BLOCK, (p + 1) * BLOCK)
        new_ref[rows, :] = (moved_ref[rows, :] - taken).astype(BF)


def update_kernel(val_ref, off_ref, rowi_ref, lanei_ref, exp_ref, exp2_ref, same_ref, up_ref, even_ref, odd_ref):
    groups = val_ref.shape[0]
    slots = own_slots((FIVE * HALF, LANES))
    even_ref[...] = jnp.zeros_like(even_ref)
    odd_ref[...] = jnp.zeros_like(odd_ref)
    lane = lane_in_block(even_ref.shape)

    def add_group(r, carry):
        off = jnp.concatenate([off_ref[r, 0]] * FIVE, axis=0)
        off = jnp.where(slots, off, 0.0).astype(BF)
        offsets = dot(off, exp_ref[...])
        val = jnp.where(slots, jnp.concatenate([val_ref[r, 0]] * FIVE, axis=0), 0.0)
        high, low = split(val)
        values = dot(jnp.concatenate([high, low], axis=1), exp2_ref[...])
        even_ref[...] += jnp.where(offsets == lane, values, 0.0)
        odd_ref[...] += jnp.where(offsets == lane + BLOCK, values, 0.0)
        return carry

    lax.fori_loop(0, groups, add_group, 0)
    even, odd = even_ref[...], odd_ref[...]
    squares = even * even + odd * odd
    high, low = split(even)
    spread_even = lane_transform(high, low, lanei_ref[...])
    high, low = split(odd)
    spread_odd = lane_transform(high, low, lanei_ref[...])
    for p in range(FIVE):
        cut = slice(p * HALF, (p + 1) * HALF)
        high, low = split(jnp.concatenate([spread_even[cut], spread_odd[cut]], axis=0))
        field = dot(rowi_ref[...], jnp.concatenate([high, low, high], axis=0))
        total = jnp.broadcast_to(jnp.sum(squares[cut], axis=0, keepdims=True), (8, squares.shape[1]))
        scales = []
        for q in range(squares.shape[1] // LANES):
            high, low = split(total[:, q * LANES:(q + 1) * LANES])
            scales.append(dot(high, same_ref[...]) + dot(low, same_ref[...]))
        power = jnp.concatenate(scales, axis=1)[:1]
        scale = lax.rsqrt(power * (1.0 / (BLOCK * BLOCK)) + EPSILON)
        up_ref[p * BLOCK:(p + 1) * BLOCK, :] = (field * scale).astype(BF)


def whole(shape):
    return pl.BlockSpec(shape, lambda i: (0,) * len(shape))


def grad_call(xt, g, mom, off, t):
    features, width = mom.shape
    chunks = features // CHUNK
    return pl.pallas_call(
        grad_kernel,
        grid=(chunks,),
        in_specs=[
            pl.BlockSpec((CHUNK, ROWS), lambda i: (i, 0)),
            whole(g.shape),
            pl.BlockSpec((CHUNK, width), lambda i: (i, 0)),
            pl.BlockSpec((1, HALF, LANES), lambda i: (i, 0, 0)),
        ] + [whole(t[n].shape) for n in ("row_fwd", "row_inv", "lane_fwd", "lane_inv", "expand", "compress")],
        out_specs=[
            pl.BlockSpec((CHUNK, width), lambda i: (i, 0)),
            pl.BlockSpec((1, HALF, LANES), lambda i: (i, 0, 0)),
        ],
        out_shape=[
            jax.ShapeDtypeStruct((features, width), BF),
            jax.ShapeDtypeStruct((chunks, HALF, LANES), F32),
        ],
        scratch_shapes=[pltpu.VMEM((CHUNK, width), F32)],
        compiler_params=pltpu.CompilerParams(vmem_limit_bytes=50 * 2**20),
    )(xt, g, mom, off, *(t[n] for n in ("row_fwd", "row_inv", "lane_fwd", "lane_inv", "expand", "compress")))


def update_call(values, off, t, width):
    groups, chunks = values.shape[:2]
    names = ("row_inv", "lane_inv", "expand", "expand2", "same")
    return pl.pallas_call(
        update_kernel,
        grid=(chunks,),
        in_specs=[
            pl.BlockSpec((groups, 1, HALF, LANES), lambda i: (0, i, 0, 0)),
            pl.BlockSpec((groups, 1, HALF, LANES), lambda i: (0, i, 0, 0)),
        ] + [whole(t[n].shape) for n in names],
        out_specs=pl.BlockSpec((CHUNK, width), lambda i: (i, 0)),
        out_shape=jax.ShapeDtypeStruct((chunks * CHUNK, width), BF),
        scratch_shapes=[pltpu.VMEM((FIVE * HALF, width), F32), pltpu.VMEM((FIVE * HALF, width), F32)],
        compiler_params=pltpu.CompilerParams(vmem_limit_bytes=50 * 2**20),
    )(values, off, *(t[n] for n in names))


def slot_offsets(picks):
    groups, block_rows, block_cols, count = picks.shape
    off = (picks % LANES).astype(F32)
    off = jnp.pad(off, ((0, 0), (0, 0), (0, 16 - block_cols), (0, 0)))
    off = off.reshape(groups, block_rows // FIVE, FIVE * 16, count)
    off = jnp.transpose(off, (0, 1, 3, 2))
    return jnp.pad(off, ((0, 0), (0, 0), (0, 0), (0, LANES - FIVE * 16)))


def body(tokens, output_grads, momentum, component_picks):
    width = momentum.shape[2]
    t = {name: jnp.asarray(table) for name, table in tables(width).items()}
    xt = lax.all_gather((tokens * BF(1.0 / math.sqrt(ROWS))).T, "tp", axis=0, tiled=True)
    off = slot_offsets(component_picks)
    own = lax.dynamic_index_in_dim(off, lax.axis_index("rep"), 0, keepdims=False)
    new_momentum, values = grad_call(xt, output_grads, momentum[0], own, t)
    gathered = lax.all_gather(values, "rep", axis=0)
    update = update_call(gathered, off, t, width)
    return (new_momentum[None], update)


def solution(mesh):
    return jax.shard_map(
        body,
        mesh=mesh,
        in_specs=(P("rep", "tp"), P("rep", "tp"), P("rep", None, "tp"), P(None, None, "tp", None)),
        out_specs=(P("rep", None, "tp"), P(None, "tp")),
        check_vma=False,
    )
```

```python
import functools
import math

import jax
import jax.numpy as jnp
import ml_dtypes
import numpy as np
from jax import lax
from jax.experimental import pallas as pl
from jax.experimental.pallas import tpu as pltpu
from jax.sharding import PartitionSpec as P

ROWS = 1024
BLOCK = 64
HALF = 32
FIVE = 5
CHUNK = FIVE * BLOCK
LANES = 128
DECAY = 0.9
EPSILON = 1e-06
BF = jnp.bfloat16
F32 = jnp.float32


def split_table(table):
    high = table.astype(ml_dtypes.bfloat16)
    low = (table - high.astype(np.float64)).astype(ml_dtypes.bfloat16)
    return high, low


def tables(width):
    frequency = np.arange(BLOCK, dtype=np.float64)[:, None]
    position = np.arange(BLOCK, dtype=np.float64)[None, :]
    norm = np.where(frequency == 0, math.sqrt(1.0 / BLOCK), math.sqrt(2.0 / BLOCK))
    cosine = norm * np.cos(math.pi * (2.0 * position + 1.0) * frequency / (2.0 * BLOCK))
    ordered = np.concatenate([cosine[0::2], cosine[1::2]])

    def rows_table(matrix):
        high, low = split_table(matrix)
        return np.concatenate([high, high, low], axis=1)

    def lanes_table(matrix):
        pair = np.zeros((LANES, LANES))
        pair[:BLOCK, :BLOCK] = matrix
        pair[BLOCK:, BLOCK:] = matrix
        high, low = split_table(pair)
        return np.concatenate(
            [np.concatenate([high, low], axis=1), np.concatenate([high, np.zeros_like(low)], axis=1)]
        )

    slot = np.arange(LANES)[:, None] % 16
    block = np.arange(width)[None, :] // BLOCK
    expand = (slot == block).astype(ml_dtypes.bfloat16)
    same = (np.arange(LANES)[:, None] // BLOCK == np.arange(LANES)[None, :] // BLOCK).astype(ml_dtypes.bfloat16)
    return {
        "row_fwd": rows_table(ordered),
        "row_inv": rows_table(ordered.T),
        "lane_fwd": lanes_table(cosine.T),
        "lane_inv": lanes_table(cosine),
        "expand": expand,
        "expand2": np.concatenate([expand, expand]),
        "compress": np.ascontiguousarray(expand.T),
        "same": same,
    }


def dot(a, b):
    return jnp.dot(a, b, preferred_element_type=F32)


def split(value):
    high = value.astype(BF)
    return high, (value - high.astype(F32)).astype(BF)


def lane_transform(high, low, weights):
    groups = high.shape[1] // LANES
    parts = []
    for group in range(groups):
        cut = slice(group * LANES, (group + 1) * LANES)
        both = dot(jnp.concatenate([high[:, cut], low[:, cut]], axis=1), weights)
        parts.append(both[:, :LANES] + both[:, LANES:])
    return jnp.concatenate(parts, axis=1)


def own_slots(shape):
    row = lax.broadcasted_iota(jnp.int32, shape, 0) // HALF
    lane = lax.broadcasted_iota(jnp.int32, shape, 1) // 16
    return lane == row


def lane_in_block(shape):
    return (lax.broadcasted_iota(jnp.int32, shape, 1) % BLOCK).astype(F32)


def gather_kernel(xt_ref, g_hbm, mom_hbm, picks_ref, rowf_ref, rowi_ref, lanef_ref, lanei_ref, exp_ref, comp_ref,
                  new_hbm, val_hbm, off_hbm,
                  xt, g, mom, new, moved, turned, off_all, val_all,
                  g_sem, mom_sem, new_sem, out_sem, own_sem, send_sem, recv_sem, pass_sem, sib_sem, vsend_sem, vrecv_sem):
    share = xt_ref.shape[0]
    chips = mom.shape[0] // CHUNK
    line = chips // 2
    reps = val_all.shape[0]
    rep, tp = lax.axis_index("rep"), lax.axis_index("tp")
    core, chip = lax.rem(tp, 2), lax.div(tp, 2)
    x, y = lax.rem(chip, line), lax.div(chip, line)

    def chip_at(dx, dy):
        return lax.rem(y + dy, 2) * line + lax.rem(x + dx, line)

    def device_at(dx, dy):
        return {"tp": chip_at(dx, dy) * 2 + core}

    left, right, across, sibling = device_at(line - 1, 0), device_at(1, 0), device_at(0, 1), {"tp": chip * 2 + 1 - core}

    def chip_of(step):
        dy = jnp.where((step == 3) | (step >= 5), 1, 0)
        dx = jnp.where((step == 1) | (step == 5), line - 1, jnp.where((step == 2) | (step == 6), 1, jnp.where((step == 4) | (step == 7), 2, 0)))
        return chip_at(dx, dy)

    def rows_of(step, first, count):
        start = (chip_of(step) * 2 + core) * share + first
        return xt.at[pl.ds(pl.multiple_of(start, 16), count), :]

    half = share // 2

    def push(index, recv, step, first, count, target, source=None):
        rows = rows_of(step, first, count)
        return pltpu.make_async_remote_copy(
            src_ref=rows if source is None else source, dst_ref=rows,
            send_sem=send_sem.at[index], recv_sem=recv_sem.at[recv],
            device_id=target, device_id_type=pl.DeviceIdType.MESH)

    def arrive(recv, step, first, count):
        push(0, recv, step, first, count, left).wait_recv()

    def to_sibling(step, source=None):
        rows = rows_of(step, 0, share)
        return pltpu.make_async_remote_copy(
            src_ref=rows if source is None else source, dst_ref=rows,
            send_sem=pass_sem.at[step], recv_sem=sib_sem.at[step],
            device_id=sibling, device_id_type=pl.DeviceIdType.MESH)

    def from_sibling(step):
        start = (chip_of(step) * 2 + 1 - core) * share
        rows = xt.at[pl.ds(pl.multiple_of(start, 16), share), :]
        pltpu.make_async_remote_copy(
            src_ref=rows, dst_ref=rows, send_sem=pass_sem.at[step], recv_sem=sib_sem.at[step],
            device_id=sibling, device_id_type=pl.DeviceIdType.MESH).wait_recv()

    def mom_copy(step):
        rows = pl.ds(pl.multiple_of(chip_of(step) * CHUNK, CHUNK), CHUNK)
        return pltpu.make_async_copy(mom_hbm.at[rows, :], mom.at[rows, :], mom_sem.at[step])

    def new_copy(step):
        rows = pl.ds(pl.multiple_of(chip_of(step) * CHUNK, CHUNK), CHUNK)
        return pltpu.make_async_copy(new.at[rows, :], new_hbm.at[rows, :], new_sem.at[step])

    def send_values(part, first, count, ahead):
        slab = val_all.at[rep, pl.ds(first, count)]
        return pltpu.make_async_remote_copy(
            src_ref=slab, dst_ref=slab,
            send_sem=vsend_sem.at[part, ahead], recv_sem=vrecv_sem.at[part, ahead],
            device_id={"rep": lax.rem(rep + ahead, reps)}, device_id_type=pl.DeviceIdType.MESH)

    def take_values(part, first, count, behind):
        slab = val_all.at[lax.rem(rep + reps - behind, reps), pl.ds(first, count)]
        return pltpu.make_async_remote_copy(
            src_ref=slab, dst_ref=slab,
            send_sem=vsend_sem.at[part, behind], recv_sem=vrecv_sem.at[part, behind],
            device_id={"rep": lax.rem(rep + behind, reps)}, device_id_type=pl.DeviceIdType.MESH)

    g_copy = pltpu.make_async_copy(g_hbm, g, g_sem)
    g_copy.start()
    own_rows = rows_of(0, 0, share)
    own_copy = pltpu.make_async_copy(xt_ref, own_rows, own_sem)
    own_copy.start()
    mom_copy(0).start()

    barrier = pltpu.get_barrier_semaphore()
    for target in (left, right, across, sibling):
        pl.semaphore_signal(barrier, inc=1, device_id=target, device_id_type=pl.DeviceIdType.MESH)
    for ahead in range(1, reps):
        pl.semaphore_signal(barrier, inc=1, device_id={"rep": lax.rem(rep + ahead, reps)}, device_id_type=pl.DeviceIdType.MESH)
    pl.semaphore_wait(barrier, 4 + reps - 1)

    first_pushes = [push(0, 0, 0, 0, share, right, xt_ref), push(1, 1, 0, 0, share, left, xt_ref), push(2, 2, 0, 0, share, across, xt_ref)]
    to_sibling(0, xt_ref).start()
    for copy in first_pushes:
        copy.start()
    for step in range(1, chips):
        mom_copy(step).start()

    turned[...] = jnp.zeros_like(turned)

    def turn(index, carry):
        part, quad = lax.div(index, 2), lax.rem(index, 2)
        for p in range(FIVE):
            for r in range(4):
                picks = picks_ref[quad * 4 + r, part * FIVE + p]
                turned[p * 16:p * 16 + picks.shape[0], r * HALF:(r + 1) * HALF] = (picks & (LANES - 1)).astype(F32)
        flat = turned[...].T
        for r in range(4):
            off_all[quad * 4 + r, part] = flat[r * HALF:(r + 1) * HALF]
        return carry

    lax.fori_loop(0, chips * 2, turn, 0)
    off_copy = pltpu.make_async_copy(off_all, off_hbm, out_sem.at[0])
    off_copy.start()
    own_copy.wait()
    g_copy.wait()

    second_pushes = [
        push(3, 3, 1, 0, half, right), push(4, 4, 2, half, half, left),
        push(5, 5, 3, 0, share, right), push(6, 6, 3, 0, share, left)]
    third_pushes = [push(7, 7, 4, 0, half, across), push(8, 8, 4, half, half, across)]

    def one(step, carry):
        @pl.when(step == 1)
        def _():
            arrive(0, 1, 0, share)
            arrive(1, 2, 0, share)
            arrive(2, 3, 0, share)
            for copy in second_pushes:
                copy.start()
            for s in (1, 2, 3):
                to_sibling(s).start()

        @pl.when(step == 2)
        def _():
            arrive(3, 4, 0, half)
            arrive(4, 4, half, half)
            for copy in third_pushes:
                copy.start()
            to_sibling(4).start()

        @pl.when(step == 5)
        def _():
            arrive(5, 5, 0, share)
            to_sibling(5).start()
            arrive(6, 6, 0, share)
            to_sibling(6).start()
            arrive(7, 7, 0, half)
            arrive(8, 7, half, half)
            to_sibling(7).start()

        from_sibling(step)
        mom_copy(step).wait()
        chunk = chip_of(step)
        base = pl.multiple_of(chunk * CHUNK, CHUNK)
        values = grad_chunk(xt, g, mom, off_all[rep, chunk], rowf_ref, rowi_ref, lanef_ref, lanei_ref, exp_ref, comp_ref, new, moved, base)
        val_all[rep, step] = values
        new_copy(step).start()

        @pl.when(step == 3)
        def _():
            for ahead in range(1, reps):
                send_values(0, 0, 4, ahead).start()

        @pl.when(step == 6)
        def _():
            for ahead in range(1, reps):
                send_values(1, 4, 3, ahead).start()

        return carry

    lax.fori_loop(0, chips, one, 0)
    for ahead in range(1, reps):
        send_values(2, 7, 1, ahead).start()
    for copy in first_pushes + second_pushes + third_pushes:
        copy.wait_send()
    for step in range(chips):
        to_sibling(step).wait_send()
        new_copy(step).wait()
    off_copy.wait()
    parts = ((0, 0, 4), (1, 4, 3), (2, 7, 1))
    for part, first, count in parts:
        for behind in range(1, reps):
            take_values(part, first, count, behind).wait_recv()
    outs = [pltpu.make_async_copy(val_all.at[:, step], val_hbm.at[:, chip_of(step)], out_sem.at[1 + step]) for step in range(chips)]
    for copy in outs:
        copy.start()
    for part, first, count in parts:
        for ahead in range(1, reps):
            send_values(part, first, count, ahead).wait_send()
    for copy in outs:
        copy.wait()


def grad_chunk(xt, g, mom, off, rowf_ref, rowi_ref, lanef_ref, lanei_ref, exp_ref, comp_ref, new, moved_ref, base):
    rows = pl.ds(base, CHUNK)
    moved_ref[...] = dot(xt[rows, :], g[...]) + DECAY * mom[rows, :].astype(F32)
    off = jnp.concatenate([off] * FIVE, axis=0)
    slots = own_slots((FIVE * HALF, LANES))
    off = jnp.where(slots, off, 0.0).astype(BF)
    offsets = dot(off, exp_ref[...])
    odd = offsets >= BLOCK
    picked_rows = []
    for p in range(FIVE):
        high, low = split(moved_ref[p * BLOCK:(p + 1) * BLOCK, :])
        freq = dot(rowf_ref[...], jnp.concatenate([high, low, high], axis=0))
        cut = slice(p * HALF, (p + 1) * HALF)
        picked_rows.append(jnp.where(odd[cut], freq[HALF:], freq[:HALF]))
    high, low = split(jnp.concatenate(picked_rows, axis=0))
    spectrum = lane_transform(high, low, lanef_ref[...])
    column = jnp.where(odd, offsets - BLOCK, offsets)
    picked = jnp.where(column == lane_in_block(offsets.shape), spectrum, 0.0)
    high, low = split(picked)
    values = dot(high, comp_ref[...]) + dot(low, comp_ref[...])
    values = jnp.where(slots, values, 0.0)
    spread = lane_transform(high, low, lanei_ref[...])
    for p in range(FIVE):
        cut = slice(p * HALF, (p + 1) * HALF)
        part = spread[cut]
        high, low = split(jnp.concatenate([jnp.where(odd[cut], 0.0, part), jnp.where(odd[cut], part, 0.0)], axis=0))
        taken = dot(rowi_ref[...], jnp.concatenate([high, low, high], axis=0))
        new[pl.ds(base + p * BLOCK, BLOCK), :] = (moved_ref[p * BLOCK:(p + 1) * BLOCK, :] - taken).astype(BF)
    return sum(values[p * HALF:(p + 1) * HALF] for p in range(FIVE))


def update_kernel(val_ref, off_ref, rowi_ref, lanei_ref, exp_ref, exp2_ref, same_ref, new_in, up_ref, new_out, even_ref, odd_ref, sem):
    keep = pltpu.make_async_copy(new_in, new_out, sem)

    @pl.when(pl.program_id(0) == 0)
    def _():
        keep.start()

    groups = val_ref.shape[0]
    slots = own_slots((FIVE * HALF, LANES))
    even_ref[...] = jnp.zeros_like(even_ref)
    odd_ref[...] = jnp.zeros_like(odd_ref)
    lane = lane_in_block(even_ref.shape)

    def add_group(r, carry):
        off = jnp.concatenate([off_ref[r, 0]] * FIVE, axis=0)
        off = jnp.where(slots, off, 0.0).astype(BF)
        offsets = dot(off, exp_ref[...])
        val = jnp.where(slots, jnp.concatenate([val_ref[r, 0]] * FIVE, axis=0), 0.0)
        high, low = split(val)
        values = dot(jnp.concatenate([high, low], axis=1), exp2_ref[...])
        even_ref[...] += jnp.where(offsets == lane, values, 0.0)
        odd_ref[...] += jnp.where(offsets == lane + BLOCK, values, 0.0)
        return carry

    lax.fori_loop(0, groups, add_group, 0)
    even, odd = even_ref[...], odd_ref[...]
    squares = even * even + odd * odd
    high, low = split(even)
    spread_even = lane_transform(high, low, lanei_ref[...])
    high, low = split(odd)
    spread_odd = lane_transform(high, low, lanei_ref[...])
    for p in range(FIVE):
        cut = slice(p * HALF, (p + 1) * HALF)
        high, low = split(jnp.concatenate([spread_even[cut], spread_odd[cut]], axis=0))
        field = dot(rowi_ref[...], jnp.concatenate([high, low, high], axis=0))
        total = jnp.broadcast_to(jnp.sum(squares[cut], axis=0, keepdims=True), (8, squares.shape[1]))
        scales = []
        for q in range(squares.shape[1] // LANES):
            high, low = split(total[:, q * LANES:(q + 1) * LANES])
            scales.append(dot(high, same_ref[...]) + dot(low, same_ref[...]))
        power = jnp.concatenate(scales, axis=1)[:1]
        scale = lax.rsqrt(power * (1.0 / (BLOCK * BLOCK)) + EPSILON)
        up_ref[p * BLOCK:(p + 1) * BLOCK, :] = (field * scale).astype(BF)

    @pl.when(pl.program_id(0) == pl.num_programs(0) - 1)
    def _():
        keep.wait()


def whole(shape):
    return pl.BlockSpec(shape, lambda i: (0,) * len(shape))


def gather_call(xt, g, mom, picks, t):
    features, width = mom.shape
    reps = picks.shape[0]
    chunks = features // CHUNK
    names = ("row_fwd", "row_inv", "lane_fwd", "lane_inv", "expand", "compress")
    vmem, any_space = pl.BlockSpec(memory_space=pltpu.VMEM), pl.BlockSpec(memory_space=pl.ANY)
    dma = pltpu.SemaphoreType.DMA
    return pl.pallas_call(
        gather_kernel,
        in_specs=[any_space, any_space, any_space] + [vmem] * (1 + len(names)),
        out_specs=[any_space] * 3,
        out_shape=[
            jax.ShapeDtypeStruct((features, width), BF),
            jax.ShapeDtypeStruct((reps, chunks, HALF, LANES), F32),
            jax.ShapeDtypeStruct((reps, chunks, HALF, LANES), F32),
        ],
        scratch_shapes=[
            pltpu.VMEM((features, ROWS), BF),
            pltpu.VMEM(g.shape, BF),
            pltpu.VMEM((features, width), BF),
            pltpu.VMEM((features, width), BF),
            pltpu.VMEM((CHUNK, width), F32),
            pltpu.VMEM((LANES, LANES), F32),
            pltpu.VMEM((reps, chunks, HALF, LANES), F32),
            pltpu.VMEM((reps, chunks, HALF, LANES), F32),
            dma, dma((chunks,)), dma((chunks,)), dma((1 + chunks,)), dma, dma((9,)), dma((9,)), dma((chunks,)), dma((chunks,)), dma((3, reps)), dma((3, reps)),
        ],
        compiler_params=pltpu.CompilerParams(vmem_limit_bytes=56 * 2**20, collective_id=0, has_side_effects=True),
    )(xt, g, mom, picks, *(t[n] for n in names))


def update_call(values, off, new, t, width):
    groups, chunks = values.shape[:2]
    names = ("row_inv", "lane_inv", "expand", "expand2", "same")
    return pl.pallas_call(
        update_kernel,
        grid=(chunks,),
        in_specs=[
            pl.BlockSpec((groups, 1, HALF, LANES), lambda i: (0, i, 0, 0)),
            pl.BlockSpec((groups, 1, HALF, LANES), lambda i: (0, i, 0, 0)),
        ] + [whole(t[n].shape) for n in names] + [pl.BlockSpec(memory_space=pl.ANY)],
        out_specs=[pl.BlockSpec((CHUNK, width), lambda i: (i, 0)), pl.BlockSpec(memory_space=pl.ANY)],
        out_shape=[jax.ShapeDtypeStruct((chunks * CHUNK, width), BF), jax.ShapeDtypeStruct(new.shape, BF)],
        scratch_shapes=[pltpu.VMEM((FIVE * HALF, width), F32), pltpu.VMEM((FIVE * HALF, width), F32), pltpu.SemaphoreType.DMA],
        compiler_params=pltpu.CompilerParams(vmem_limit_bytes=50 * 2**20),
    )(values, off, *(t[n] for n in names), new)


def body(tokens, output_grads, momentum, component_picks):
    width = momentum.shape[2]
    t = {name: jnp.asarray(table) for name, table in tables(width).items()}
    xt = (tokens * BF(1.0 / math.sqrt(ROWS))).T
    new_momentum, values, off = gather_call(xt, output_grads, momentum[0], component_picks, t)
    update, new_momentum = update_call(values, off, new_momentum, t, width)
    return (new_momentum[None], update)


def solution(mesh):
    return jax.shard_map(
        body,
        mesh=mesh,
        in_specs=(P("rep", "tp"), P("rep", "tp"), P("rep", None, "tp"), P(None, None, "tp", None)),
        out_specs=(P("rep", None, "tp"), P(None, "tp")),
        check_vma=False,
    )
```

```python
import functools
import math

import jax
import jax.numpy as jnp
import ml_dtypes
import numpy as np
from jax import lax
from jax.experimental import pallas as pl
from jax.experimental.pallas import tpu as pltpu
from jax.sharding import PartitionSpec as P

ROWS = 1024
BLOCK = 64
HALF = 32
FIVE = 5
CHUNK = FIVE * BLOCK
LANES = 128
SLOT = 8
DECAY = 0.9
EPSILON = 1e-06
NAMES = ("select", "row_fwd", "row_inv", "lane_fwd", "lane_inv", "expand", "compress")
BF = jnp.bfloat16
F32 = jnp.float32


def split_table(table):
    high = table.astype(ml_dtypes.bfloat16)
    low = (table - high.astype(np.float64)).astype(ml_dtypes.bfloat16)
    return high, low


def tables(width, width_rows):
    frequency = np.arange(BLOCK, dtype=np.float64)[:, None]
    position = np.arange(BLOCK, dtype=np.float64)[None, :]
    norm = np.where(frequency == 0, math.sqrt(1.0 / BLOCK), math.sqrt(2.0 / BLOCK))
    cosine = norm * np.cos(math.pi * (2.0 * position + 1.0) * frequency / (2.0 * BLOCK))
    ordered = np.concatenate([cosine[0::2], cosine[1::2]])

    def rows_table(matrix):
        high, low = split_table(matrix)
        return np.concatenate([high, high, low], axis=1)

    def lanes_table(matrix):
        pair = np.zeros((LANES, LANES))
        pair[:BLOCK, :BLOCK] = matrix
        pair[BLOCK:, BLOCK:] = matrix
        high, low = split_table(pair)
        return np.concatenate(
            [np.concatenate([high, low], axis=1), np.concatenate([high, np.zeros_like(low)], axis=1)]
        )

    slot = np.arange(LANES)[:, None] // SLOT
    block = np.arange(width)[None, :] // BLOCK
    expand = (slot == block).astype(ml_dtypes.bfloat16)
    same = (np.arange(LANES)[:, None] // BLOCK == np.arange(LANES)[None, :] // BLOCK).astype(ml_dtypes.bfloat16)
    rows = width_rows
    select = np.zeros((width // BLOCK, rows, rows // FIVE * LANES), ml_dtypes.bfloat16)
    for b in range(width // BLOCK):
        for p in range(rows):
            select[b, p, p // FIVE * LANES + b * SLOT + p % FIVE] = 1.0
    return {
        "select": select,
        "row_fwd": rows_table(ordered),
        "row_inv": rows_table(ordered.T),
        "lane_fwd": lanes_table(cosine.T),
        "lane_inv": lanes_table(cosine),
        "expand": expand,
        "expand2": np.concatenate([expand, expand]),
        "compress": np.ascontiguousarray(expand.T),
        "same": same,
    }


def dot(a, b):
    return jnp.dot(a, b, preferred_element_type=F32)


def split(value):
    high = value.astype(BF)
    return high, (value - high.astype(F32)).astype(BF)


def lane_transform(high, low, weights):
    groups = high.shape[1] // LANES
    parts = []
    for group in range(groups):
        cut = slice(group * LANES, (group + 1) * LANES)
        both = dot(jnp.concatenate([high[:, cut], low[:, cut]], axis=1), weights)
        parts.append(both[:, :LANES] + both[:, LANES:])
    return jnp.concatenate(parts, axis=1)


def own_slots(shape):
    row = lax.broadcasted_iota(jnp.int32, shape, 0) // HALF
    lane = lax.broadcasted_iota(jnp.int32, shape, 1) % SLOT
    return lane == row


def lane_in_block(shape):
    return (lax.broadcasted_iota(jnp.int32, shape, 1) % BLOCK).astype(F32)


def gather_kernel(xt_ref, g_hbm, mom_hbm, *refs):
    count = len(NAMES) + 1
    small_hbm, refs = refs[:count], refs[count:]
    new_hbm, val_hbm, off_hbm = refs[:3]
    small, refs = refs[3:3 + count], refs[3 + count:]
    picks_ref, select_ref, rowf_ref, rowi_ref, lanef_ref, lanei_ref, exp_ref, comp_ref = small
    (xt, g, mom, new, moved, off_all, val_all,
                  small_sem, g_sem, mom_sem, new_sem, out_sem, own_sem, send_sem, recv_sem, pass_sem, sib_sem, vsend_sem, vrecv_sem) = refs
    share = xt_ref.shape[0]
    chips = mom.shape[0] // CHUNK
    line = chips // 2
    reps = val_all.shape[0]
    rep, tp = lax.axis_index("rep"), lax.axis_index("tp")
    core, chip = lax.rem(tp, 2), lax.div(tp, 2)
    x, y = lax.rem(chip, line), lax.div(chip, line)

    def chip_at(dx, dy):
        return lax.rem(y + dy, 2) * line + lax.rem(x + dx, line)

    def device_at(dx, dy):
        return {"tp": chip_at(dx, dy) * 2 + core}

    left, right, across, sibling = device_at(line - 1, 0), device_at(1, 0), device_at(0, 1), {"tp": chip * 2 + 1 - core}

    def chip_of(step):
        dy = jnp.where((step == 3) | (step >= 5), 1, 0)
        dx = jnp.where((step == 1) | (step == 5), line - 1, jnp.where((step == 2) | (step == 6), 1, jnp.where((step == 4) | (step == 7), 2, 0)))
        return chip_at(dx, dy)

    def rows_of(step, first, count):
        start = (chip_of(step) * 2 + core) * share + first
        return xt.at[pl.ds(pl.multiple_of(start, 16), count), :]

    half = share // 2

    def push(index, recv, step, first, count, target, source=None):
        rows = rows_of(step, first, count)
        return pltpu.make_async_remote_copy(
            src_ref=rows if source is None else source, dst_ref=rows,
            send_sem=send_sem.at[index], recv_sem=recv_sem.at[recv],
            device_id=target, device_id_type=pl.DeviceIdType.MESH)

    def arrive(recv, step, first, count):
        push(0, recv, step, first, count, left).wait_recv()

    def to_sibling(step, source=None):
        rows = rows_of(step, 0, share)
        return pltpu.make_async_remote_copy(
            src_ref=rows if source is None else source, dst_ref=rows,
            send_sem=pass_sem.at[step], recv_sem=sib_sem.at[step],
            device_id=sibling, device_id_type=pl.DeviceIdType.MESH)

    def from_sibling(step):
        start = (chip_of(step) * 2 + 1 - core) * share
        rows = xt.at[pl.ds(pl.multiple_of(start, 16), share), :]
        pltpu.make_async_remote_copy(
            src_ref=rows, dst_ref=rows, send_sem=pass_sem.at[step], recv_sem=sib_sem.at[step],
            device_id=sibling, device_id_type=pl.DeviceIdType.MESH).wait_recv()

    def mom_copy(step):
        rows = pl.ds(pl.multiple_of(chip_of(step) * CHUNK, CHUNK), CHUNK)
        return pltpu.make_async_copy(mom_hbm.at[rows, :], mom.at[rows, :], mom_sem.at[step])

    def new_copy(step):
        rows = pl.ds(pl.multiple_of(chip_of(step) * CHUNK, CHUNK), CHUNK)
        return pltpu.make_async_copy(new.at[rows, :], new_hbm.at[rows, :], new_sem.at[step])

    def send_values(part, first, count, ahead):
        slab = val_all.at[rep, pl.ds(first, count)]
        return pltpu.make_async_remote_copy(
            src_ref=slab, dst_ref=slab,
            send_sem=vsend_sem.at[part, ahead], recv_sem=vrecv_sem.at[part, ahead],
            device_id={"rep": lax.rem(rep + ahead, reps)}, device_id_type=pl.DeviceIdType.MESH)

    def take_values(part, first, count, behind):
        slab = val_all.at[lax.rem(rep + reps - behind, reps), pl.ds(first, count)]
        return pltpu.make_async_remote_copy(
            src_ref=slab, dst_ref=slab,
            send_sem=vsend_sem.at[part, behind], recv_sem=vrecv_sem.at[part, behind],
            device_id={"rep": lax.rem(rep + behind, reps)}, device_id_type=pl.DeviceIdType.MESH)

    own_rows = rows_of(0, 0, share)
    own_copy = pltpu.make_async_copy(xt_ref, own_rows, own_sem)
    own_copy.start()
    small_copies = [pltpu.make_async_copy(small_hbm[n], small[n], small_sem.at[n]) for n in range(count)]
    for copy in small_copies:
        copy.start()
    g_copy = pltpu.make_async_copy(g_hbm, g, g_sem)
    g_copy.start()
    mom_copy(0).start()

    barrier = pltpu.get_barrier_semaphore()
    for target in (left, right, across, sibling):
        pl.semaphore_signal(barrier, inc=1, device_id=target, device_id_type=pl.DeviceIdType.MESH)
    for ahead in range(1, reps):
        pl.semaphore_signal(barrier, inc=1, device_id={"rep": lax.rem(rep + ahead, reps)}, device_id_type=pl.DeviceIdType.MESH)
    small_copies[0].wait()
    small_copies[1].wait()
    flat = jnp.zeros((reps * HALF, chips * LANES), F32)
    for b in range(picks_ref.shape[1]):
        low_bits = (picks_ref[:, b] & (LANES - 1)).astype(F32).astype(BF)
        flat = flat + dot(low_bits.reshape(reps * HALF, low_bits.shape[2]), select_ref[b])
    for r in range(reps):
        for part in range(chips):
            off_all[r, part] = flat[r * HALF:(r + 1) * HALF, part * LANES:(part + 1) * LANES]

    pl.semaphore_wait(barrier, 4 + reps - 1)

    first_pushes = [push(0, 0, 0, 0, share, right, xt_ref), push(1, 1, 0, 0, share, left, xt_ref), push(2, 2, 0, 0, share, across, xt_ref)]
    to_sibling(0, xt_ref).start()
    for copy in first_pushes:
        copy.start()
    for step in range(1, chips):
        mom_copy(step).start()

    off_copy = pltpu.make_async_copy(off_all, off_hbm, out_sem.at[0])
    off_copy.start()
    own_copy.wait()
    g_copy.wait()
    for copy in small_copies[2:]:
        copy.wait()

    second_pushes = [
        push(3, 3, 1, 0, half, right), push(4, 4, 2, half, half, left),
        push(5, 5, 3, 0, share, right), push(6, 6, 3, 0, share, left)]
    third_pushes = [push(7, 7, 4, 0, half, across), push(8, 8, 4, half, half, across)]

    def one(step, carry):
        @pl.when(step == 1)
        def _():
            arrive(0, 1, 0, share)
            arrive(1, 2, 0, share)
            arrive(2, 3, 0, share)
            for copy in second_pushes:
                copy.start()
            for s in (1, 2, 3):
                to_sibling(s).start()

        @pl.when(step == 2)
        def _():
            arrive(3, 4, 0, half)
            arrive(4, 4, half, half)
            for copy in third_pushes:
                copy.start()
            to_sibling(4).start()

        @pl.when(step == 5)
        def _():
            arrive(5, 5, 0, share)
            to_sibling(5).start()
            arrive(6, 6, 0, share)
            to_sibling(6).start()
            arrive(7, 7, 0, half)
            arrive(8, 7, half, half)
            to_sibling(7).start()

        from_sibling(step)
        mom_copy(step).wait()
        chunk = chip_of(step)
        base = pl.multiple_of(chunk * CHUNK, CHUNK)
        values = grad_chunk(xt, g, mom, off_all[rep, chunk], rowf_ref, rowi_ref, lanef_ref, lanei_ref, exp_ref, comp_ref, new, moved, base)
        val_all[rep, step] = values
        new_copy(step).start()

        @pl.when(step == 3)
        def _():
            for ahead in range(1, reps):
                send_values(0, 0, 4, ahead).start()

        @pl.when(step == 6)
        def _():
            for ahead in range(1, reps):
                send_values(1, 4, 3, ahead).start()

        return carry

    lax.fori_loop(0, chips, one, 0)
    for ahead in range(1, reps):
        send_values(2, 7, 1, ahead).start()
    for copy in first_pushes + second_pushes + third_pushes:
        copy.wait_send()
    for step in range(chips):
        to_sibling(step).wait_send()
        new_copy(step).wait()
    off_copy.wait()
    parts = ((0, 0, 4), (1, 4, 3), (2, 7, 1))
    for part, first, count in parts:
        for behind in range(1, reps):
            take_values(part, first, count, behind).wait_recv()
    outs = [pltpu.make_async_copy(val_all.at[:, step], val_hbm.at[:, chip_of(step)], out_sem.at[1 + step]) for step in range(chips)]
    for copy in outs:
        copy.start()
    for part, first, count in parts:
        for ahead in range(1, reps):
            send_values(part, first, count, ahead).wait_send()
    for copy in outs:
        copy.wait()


def grad_chunk(xt, g, mom, off, rowf_ref, rowi_ref, lanef_ref, lanei_ref, exp_ref, comp_ref, new, moved_ref, base):
    rows = pl.ds(base, CHUNK)
    moved_ref[...] = dot(xt[rows, :], g[...]) * (1.0 / math.sqrt(ROWS)) + DECAY * mom[rows, :].astype(F32)
    off = jnp.concatenate([off] * FIVE, axis=0)
    slots = own_slots((FIVE * HALF, LANES))
    off = jnp.where(slots, off, 0.0).astype(BF)
    offsets = dot(off, exp_ref[...])
    odd = offsets >= BLOCK
    picked_rows = []
    for p in range(FIVE):
        high, low = split(moved_ref[p * BLOCK:(p + 1) * BLOCK, :])
        freq = dot(rowf_ref[...], jnp.concatenate([high, low, high], axis=0))
        cut = slice(p * HALF, (p + 1) * HALF)
        picked_rows.append(jnp.where(odd[cut], freq[HALF:], freq[:HALF]))
    high, low = split(jnp.concatenate(picked_rows, axis=0))
    spectrum = lane_transform(high, low, lanef_ref[...])
    column = jnp.where(odd, offsets - BLOCK, offsets)
    picked = jnp.where(column == lane_in_block(offsets.shape), spectrum, 0.0)
    high, low = split(picked)
    values = dot(high, comp_ref[...]) + dot(low, comp_ref[...])
    values = jnp.where(slots, values, 0.0)
    spread = lane_transform(high, low, lanei_ref[...])
    for p in range(FIVE):
        cut = slice(p * HALF, (p + 1) * HALF)
        part = spread[cut]
        high, low = split(jnp.concatenate([jnp.where(odd[cut], 0.0, part), jnp.where(odd[cut], part, 0.0)], axis=0))
        taken = dot(rowi_ref[...], jnp.concatenate([high, low, high], axis=0))
        new[pl.ds(base + p * BLOCK, BLOCK), :] = (moved_ref[p * BLOCK:(p + 1) * BLOCK, :] - taken).astype(BF)
    return sum(values[p * HALF:(p + 1) * HALF] for p in range(FIVE))


def update_kernel(val_ref, off_ref, rowi_ref, lanei_ref, exp_ref, exp2_ref, same_ref, new_in, up_ref, new_out, even_ref, odd_ref, offs_ref, vals_ref):
    new_out[...] = new_in[...]
    groups = val_ref.shape[0]
    width = even_ref.shape[1]
    rows = FIVE * HALF
    slots = own_slots((rows, LANES))
    for r in range(groups):
        cut = slice(r * rows, (r + 1) * rows)
        off = jnp.concatenate([off_ref[r, 0]] * FIVE, axis=0)
        offs_ref[cut, :] = jnp.where(slots, off, 0.0).astype(BF)
        high, low = split(jnp.where(slots, jnp.concatenate([val_ref[r, 0]] * FIVE, axis=0), 0.0))
        vals_ref[cut, :LANES] = high
        vals_ref[cut, LANES:] = low
    for start in range(0, width, 2 * LANES):
        lanes = slice(start, min(start + 2 * LANES, width))
        offsets = dot(offs_ref[...], exp_ref[:, lanes])
        values = dot(vals_ref[...], exp2_ref[:, lanes])
        lane = lane_in_block((rows, offsets.shape[1]))
        even = odd = jnp.zeros(lane.shape, F32)
        for r in range(groups):
            off, val = offsets[r * rows:(r + 1) * rows], values[r * rows:(r + 1) * rows]
            even = even + jnp.where(off == lane, val, 0.0)
            odd = odd + jnp.where(off == lane + BLOCK, val, 0.0)
        even_ref[:, lanes] = even
        odd_ref[:, lanes] = odd
    even, odd = even_ref[...], odd_ref[...]
    squares = even * even + odd * odd
    high, low = split(even)
    spread_even = lane_transform(high, low, lanei_ref[...])
    high, low = split(odd)
    spread_odd = lane_transform(high, low, lanei_ref[...])
    for p in range(FIVE):
        cut = slice(p * HALF, (p + 1) * HALF)
        high, low = split(jnp.concatenate([spread_even[cut], spread_odd[cut]], axis=0))
        field = dot(rowi_ref[...], jnp.concatenate([high, low, high], axis=0))
        total = jnp.broadcast_to(jnp.sum(squares[cut], axis=0, keepdims=True), (8, squares.shape[1]))
        scales = []
        for q in range(squares.shape[1] // LANES):
            high, low = split(total[:, q * LANES:(q + 1) * LANES])
            scales.append(dot(high, same_ref[...]) + dot(low, same_ref[...]))
        power = jnp.concatenate(scales, axis=1)[:1]
        scale = lax.rsqrt(power * (1.0 / (BLOCK * BLOCK)) + EPSILON)
        up_ref[p * BLOCK:(p + 1) * BLOCK, :] = (field * scale).astype(BF)


def whole(shape):
    return pl.BlockSpec(shape, lambda i: (0,) * len(shape))


def gather_call(xt, g, mom, picks, t):
    features, width = mom.shape
    reps = picks.shape[0]
    chunks = features // CHUNK
    small = [picks] + [t[n] for n in NAMES]
    any_space = pl.BlockSpec(memory_space=pl.ANY)
    dma = pltpu.SemaphoreType.DMA
    return pl.pallas_call(
        gather_kernel,
        in_specs=[any_space] * (3 + len(small)),
        out_specs=[any_space] * 3,
        out_shape=[
            jax.ShapeDtypeStruct((features, width), BF),
            jax.ShapeDtypeStruct((reps, chunks, HALF, LANES), F32),
            jax.ShapeDtypeStruct((reps, chunks, HALF, LANES), F32),
        ],
        scratch_shapes=[pltpu.VMEM(a.shape, a.dtype) for a in small] + [
            pltpu.VMEM((features, ROWS), BF),
            pltpu.VMEM(g.shape, BF),
            pltpu.VMEM((features, width), BF),
            pltpu.VMEM((features, width), BF),
            pltpu.VMEM((CHUNK, width), F32),
            pltpu.VMEM((reps, chunks, HALF, LANES), F32),
            pltpu.VMEM((reps, chunks, HALF, LANES), F32),
            dma((len(small),)), dma, dma((chunks,)), dma((chunks,)), dma((1 + chunks,)), dma, dma((9,)), dma((9,)), dma((chunks,)), dma((chunks,)), dma((3, reps)), dma((3, reps)),
        ],
        compiler_params=pltpu.CompilerParams(vmem_limit_bytes=56 * 2**20, collective_id=0, has_side_effects=True),
    )(xt, g, mom, *small)


def update_call(values, off, new, t, width):
    groups, chunks = values.shape[:2]
    names = ("row_inv", "lane_inv", "expand", "expand2", "same")
    return pl.pallas_call(
        update_kernel,
        grid=(chunks,),
        in_specs=[
            pl.BlockSpec((groups, 1, HALF, LANES), lambda i: (0, i, 0, 0)),
            pl.BlockSpec((groups, 1, HALF, LANES), lambda i: (0, i, 0, 0)),
        ] + [whole(t[n].shape) for n in names] + [pl.BlockSpec((CHUNK, width), lambda i: (i, 0))],
        out_specs=[pl.BlockSpec((CHUNK, width), lambda i: (i, 0))] * 2,
        out_shape=[jax.ShapeDtypeStruct((chunks * CHUNK, width), BF), jax.ShapeDtypeStruct(new.shape, BF)],
        scratch_shapes=[pltpu.VMEM((FIVE * HALF, width), F32), pltpu.VMEM((FIVE * HALF, width), F32), pltpu.VMEM((groups * FIVE * HALF, LANES), BF), pltpu.VMEM((groups * FIVE * HALF, 2 * LANES), BF)],
        compiler_params=pltpu.CompilerParams(vmem_limit_bytes=50 * 2**20),
    )(values, off, *(t[n] for n in names), new)


def body(tokens, output_grads, momentum, component_picks):
    width = momentum.shape[2]
    t = {name: jnp.asarray(table) for name, table in tables(width, component_picks.shape[1]).items()}
    picks = jnp.transpose(component_picks, (0, 2, 3, 1))
    new_momentum, values, off = gather_call(tokens.T, output_grads, momentum[0], picks, t)
    update, new_momentum = update_call(values, off, new_momentum, t, width)
    return (new_momentum[None], update)


def solution(mesh):
    return jax.shard_map(
        body,
        mesh=mesh,
        in_specs=(P("rep", "tp"), P("rep", "tp"), P("rep", None, "tp"), P(None, None, "tp", None)),
        out_specs=(P("rep", None, "tp"), P(None, "tp")),
        check_vma=False,
    )
```

```python
import functools
import math

import jax
import jax.numpy as jnp
import ml_dtypes
import numpy as np
from jax import lax
from jax.experimental import pallas as pl
from jax.experimental.pallas import tpu as pltpu
from jax.sharding import PartitionSpec as P

ROWS = 1024
BLOCK = 64
HALF = 32
FIVE = 5
CHUNK = FIVE * BLOCK
LANES = 128
SLOT = 8
QUAD = 4
LISTED = 16
DECAY = 0.9
EPSILON = 1e-06
NAMES = ("select", "row_fwd", "row_inv", "lane_fwd", "lane_inv", "expand", "compress")
BF = jnp.bfloat16
F32 = jnp.float32


def split_table(table):
    high = table.astype(ml_dtypes.bfloat16)
    low = (table - high.astype(np.float64)).astype(ml_dtypes.bfloat16)
    return high, low


def tables(width, width_rows):
    frequency = np.arange(BLOCK, dtype=np.float64)[:, None]
    position = np.arange(BLOCK, dtype=np.float64)[None, :]
    norm = np.where(frequency == 0, math.sqrt(1.0 / BLOCK), math.sqrt(2.0 / BLOCK))
    cosine = norm * np.cos(math.pi * (2.0 * position + 1.0) * frequency / (2.0 * BLOCK))
    ordered = np.concatenate([cosine[0::2], cosine[1::2]])

    def rows_table(matrix):
        high, low = split_table(matrix)
        return np.concatenate([high, high, low], axis=1)

    def lanes_table(matrix):
        pair = np.zeros((LANES, LANES))
        pair[:BLOCK, :BLOCK] = matrix
        pair[BLOCK:, BLOCK:] = matrix
        high, low = split_table(pair)
        return np.concatenate(
            [np.concatenate([high, low], axis=1), np.concatenate([high, np.zeros_like(low)], axis=1)]
        )

    slot = np.arange(LANES)[:, None] // SLOT
    block = np.arange(width)[None, :] // BLOCK
    expand = (slot == block).astype(ml_dtypes.bfloat16)
    rows = width_rows
    select = np.zeros((width // BLOCK, rows, rows // FIVE * LANES), ml_dtypes.bfloat16)
    for b in range(width // BLOCK):
        for p in range(rows):
            select[b, p, p // FIVE * LANES + b * SLOT + p % FIVE] = 1.0
    high, low = split_table(cosine.T)
    columns = np.concatenate([high, high, low], axis=1)
    spread = np.zeros((QUAD, BLOCK, 2, QUAD, HALF))
    for p in range(QUAD):
        for parity in range(2):
            spread[p, :, parity, p, :] = cosine[parity::2].T
    high, low = split_table(spread.reshape(QUAD * BLOCK, 2 * QUAD * HALF))
    segment = (np.arange(LANES)[:, None] // HALF == np.arange(LANES)[None, :] // HALF).astype(ml_dtypes.bfloat16)
    return {
        "select": select,
        "row_fwd": rows_table(ordered),
        "row_inv": rows_table(ordered.T),
        "lane_fwd": lanes_table(cosine.T),
        "lane_inv": lanes_table(cosine),
        "expand": expand,
        "compress": (np.arange(LISTED)[:, None] == block).astype(ml_dtypes.bfloat16),
        "columns": columns,
        "spread": np.concatenate([high, low]),
        "segment": np.concatenate([segment, segment]),
    }


def dot(a, b):
    return jnp.dot(a, b, preferred_element_type=F32)


def dot_t(a, b):
    return lax.dot_general(a, b, (((1,), (1,)), ((), ())), preferred_element_type=F32)


def split(value):
    high = value.astype(BF)
    return high, (value - high.astype(F32)).astype(BF)


def lane_transform(high, low, weights):
    groups = high.shape[1] // LANES
    parts = []
    for group in range(groups):
        cut = slice(group * LANES, (group + 1) * LANES)
        both = dot(jnp.concatenate([high[:, cut], low[:, cut]], axis=1), weights)
        parts.append(both[:, :LANES] + both[:, LANES:])
    return jnp.concatenate(parts, axis=1)


def own_slots(shape):
    row = lax.broadcasted_iota(jnp.int32, shape, 0) // HALF
    lane = lax.broadcasted_iota(jnp.int32, shape, 1) % SLOT
    return lane == row


def lane_in_block(shape):
    return (lax.broadcasted_iota(jnp.int32, shape, 1) % BLOCK).astype(F32)


def gather_kernel(xt_ref, g_hbm, mom_hbm, *refs):
    count = len(NAMES) + 1
    small_hbm, refs = refs[:count], refs[count:]
    new_hbm, val_hbm, off_hbm = refs[:3]
    small, refs = refs[3:3 + count], refs[3 + count:]
    picks_ref, select_ref, rowf_ref, rowi_ref, lanef_ref, lanei_ref, exp_ref, comp_ref = small
    (xt, g, mom, new, moved, picked_high, picked_low, turned, flipped, off_own, off_all, val_all,
                  small_sem, g_sem, mom_sem, new_sem, out_sem, own_sem, send_sem, recv_sem, pass_sem, sib_sem, vsend_sem, vrecv_sem) = refs
    share = xt_ref.shape[0]
    chips = mom.shape[0] // CHUNK
    line = chips // 2
    reps = val_all.shape[0]
    rep, tp = lax.axis_index("rep"), lax.axis_index("tp")
    core, chip = lax.rem(tp, 2), lax.div(tp, 2)
    x, y = lax.rem(chip, line), lax.div(chip, line)

    def chip_at(dx, dy):
        return lax.rem(y + dy, 2) * line + lax.rem(x + dx, line)

    def device_at(dx, dy):
        return {"tp": chip_at(dx, dy) * 2 + core}

    left, right, across, sibling = device_at(line - 1, 0), device_at(1, 0), device_at(0, 1), {"tp": chip * 2 + 1 - core}

    def chip_of(step):
        dy = jnp.where((step == 3) | (step >= 5), 1, 0)
        dx = jnp.where((step == 1) | (step == 5), line - 1, jnp.where((step == 2) | (step == 6), 1, jnp.where((step == 4) | (step == 7), 2, 0)))
        return chip_at(dx, dy)

    def rows_of(step, first, count):
        start = (chip_of(step) * 2 + core) * share + first
        return xt.at[pl.ds(pl.multiple_of(start, 16), count), :]

    half = share // 2

    def push(index, recv, step, first, count, target, source=None):
        rows = rows_of(step, first, count)
        return pltpu.make_async_remote_copy(
            src_ref=rows if source is None else source, dst_ref=rows,
            send_sem=send_sem.at[index], recv_sem=recv_sem.at[recv],
            device_id=target, device_id_type=pl.DeviceIdType.MESH)

    def arrive(recv, step, first, count):
        push(0, recv, step, first, count, left).wait_recv()

    def to_sibling(step, source=None):
        rows = rows_of(step, 0, share)
        return pltpu.make_async_remote_copy(
            src_ref=rows if source is None else source, dst_ref=rows,
            send_sem=pass_sem.at[step], recv_sem=sib_sem.at[step],
            device_id=sibling, device_id_type=pl.DeviceIdType.MESH)

    def from_sibling(step):
        start = (chip_of(step) * 2 + 1 - core) * share
        rows = xt.at[pl.ds(pl.multiple_of(start, 16), share), :]
        pltpu.make_async_remote_copy(
            src_ref=rows, dst_ref=rows, send_sem=pass_sem.at[step], recv_sem=sib_sem.at[step],
            device_id=sibling, device_id_type=pl.DeviceIdType.MESH).wait_recv()

    def mom_copy(step):
        rows = pl.ds(pl.multiple_of(chip_of(step) * CHUNK, CHUNK), CHUNK)
        return pltpu.make_async_copy(mom_hbm.at[rows, :], mom.at[rows, :], mom_sem.at[step])

    def new_copy(step):
        rows = pl.ds(pl.multiple_of(chip_of(step) * CHUNK, CHUNK), CHUNK)
        return pltpu.make_async_copy(new.at[rows, :], new_hbm.at[rows, :], new_sem.at[step])

    def send_values(step, ahead):
        slab = val_all.at[rep, step]
        return pltpu.make_async_remote_copy(
            src_ref=slab, dst_ref=slab,
            send_sem=vsend_sem.at[step, ahead], recv_sem=vrecv_sem.at[step, ahead],
            device_id={"rep": lax.rem(rep + ahead, reps)}, device_id_type=pl.DeviceIdType.MESH)

    def take_values(step, behind):
        slab = val_all.at[lax.rem(rep + reps - behind, reps), step]
        return pltpu.make_async_remote_copy(
            src_ref=slab, dst_ref=slab,
            send_sem=vsend_sem.at[step, behind], recv_sem=vrecv_sem.at[step, behind],
            device_id={"rep": lax.rem(rep + behind, reps)}, device_id_type=pl.DeviceIdType.MESH)

    own_rows = rows_of(0, 0, share)
    own_copy = pltpu.make_async_copy(xt_ref, own_rows, own_sem)
    own_copy.start()
    small_copies = [pltpu.make_async_copy(small_hbm[n], small[n], small_sem.at[n]) for n in range(count)]
    for copy in small_copies:
        copy.start()
    g_copy = pltpu.make_async_copy(g_hbm, g, g_sem)
    g_copy.start()
    mom_copy(0).start()

    barrier = pltpu.get_barrier_semaphore()
    for target in (left, right, across, sibling):
        pl.semaphore_signal(barrier, inc=1, device_id=target, device_id_type=pl.DeviceIdType.MESH)
    for ahead in range(1, reps):
        pl.semaphore_signal(barrier, inc=1, device_id={"rep": lax.rem(rep + ahead, reps)}, device_id_type=pl.DeviceIdType.MESH)
    pl.semaphore_wait(barrier, 4 + reps - 1)

    own_low, own_high = xt_ref.at[pl.ds(0, half), :], xt_ref.at[pl.ds(half, half), :]
    first_pushes = [
        push(0, 0, 0, 0, half, right, own_low), push(1, 1, 0, half, half, left, own_high), push(2, 2, 0, 0, half, across, own_low),
        push(3, 3, 0, half, half, right, own_high), push(4, 4, 0, 0, half, left, own_low), push(5, 5, 0, half, half, across, own_high)]
    to_sibling(0, xt_ref).start()
    for copy in first_pushes:
        copy.start()
    for step in range(1, chips):
        mom_copy(step).start()

    small_copies[0].wait()
    small_copies[1].wait()
    blocks = picks_ref.shape[1]
    flat = jnp.zeros((HALF, chips * LANES), F32)
    for b in range(blocks):
        low_bits = (picks_ref[rep, b] & (LANES - 1)).astype(F32).astype(BF)
        flat = flat + dot(low_bits, select_ref[b])
    for part in range(chips):
        off_own[part] = flat[:, part * LANES:(part + 1) * LANES]
    own_copy.wait()
    g_copy.wait()
    for copy in small_copies[2:]:
        copy.wait()

    turned[...] = jnp.zeros_like(turned)

    def turn(r, carry):
        for first in range(0, blocks, QUAD):
            for place in range(min(QUAD, blocks - first)):
                turned[place * HALF:(place + 1) * HALF, :picks_ref.shape[3]] = (picks_ref[r, first + place] & (LANES - 1)).astype(F32)
            flipped[...] = turned[...].T
            for p in range(QUAD):
                lines = flipped[pl.ds(p, off_all.shape[2], stride=QUAD), :]
                for place in range(min(QUAD, blocks - first)):
                    off_all[r, first + place, :, p * HALF:(p + 1) * HALF] = lines[:, place * HALF:(place + 1) * HALF]
        return carry

    second_pushes = [
        push(6, 6, 1, 0, half, right), push(7, 7, 2, half, half, left),
        push(8, 8, 3, 0, share, right), push(9, 9, 3, 0, share, left)]
    third_pushes = [push(10, 10, 4, 0, half, across), push(11, 11, 4, half, half, across)]

    def forward(step):
        chunk = chip_of(step)
        grad_chunk(xt, g, mom, off_own[chunk], rowf_ref, lanef_ref, exp_ref, comp_ref, moved, picked_high, picked_low,
                   val_all.at[rep, step], chunk)

    def backward(step):
        chunk = chip_of(step)
        back_chunk(off_own[chunk], rowi_ref, lanei_ref, exp_ref, moved, picked_high, picked_low, new, chunk)
        new_copy(step).start()

    def backward_step(step, carry):
        backward(step)
        return carry

    def one(step, carry):
        @pl.when(step == 1)
        def _():
            arrive(0, 1, 0, half)
            second_pushes[0].start()
            arrive(1, 2, half, half)
            second_pushes[1].start()
            lax.fori_loop(0, reps, turn, 0)
            pltpu.make_async_copy(off_all, off_hbm, out_sem.at[0]).start()
            arrive(2, 3, 0, half)
            arrive(5, 3, half, half)
            second_pushes[2].start()
            second_pushes[3].start()
            arrive(3, 1, half, half)
            to_sibling(1).start()
            arrive(4, 2, 0, half)
            to_sibling(2).start()
            to_sibling(3).start()

        @pl.when(step == 2)
        def _():
            arrive(6, 4, 0, half)
            third_pushes[0].start()
            arrive(7, 4, half, half)
            third_pushes[1].start()
            to_sibling(4).start()

        @pl.when(step == 5)
        def _():
            lax.fori_loop(0, 4, backward_step, 0)
            arrive(8, 5, 0, share)
            to_sibling(5).start()
            arrive(9, 6, 0, share)
            to_sibling(6).start()
            arrive(10, 7, 0, half)
            arrive(11, 7, half, half)
            to_sibling(7).start()
            lax.fori_loop(4, 5, backward_step, 0)

        from_sibling(step)
        mom_copy(step).wait()
        forward(step)
        for ahead in range(1, reps):
            send_values(step, ahead).start()
        return carry

    lax.fori_loop(0, chips, one, 0)
    lax.fori_loop(5, chips, backward_step, 0)
    for copy in first_pushes + second_pushes + third_pushes:
        copy.wait_send()

    def settle(step, carry):
        to_sibling(step).wait_send()
        for behind in range(1, reps):
            take_values(step, behind).wait_recv()
        pltpu.make_async_copy(val_all.at[:, step], val_hbm.at[:, chip_of(step)], out_sem.at[1 + step]).start()
        return carry

    def finish(step, carry):
        for ahead in range(1, reps):
            send_values(step, ahead).wait_send()
        new_copy(step).wait()
        pltpu.make_async_copy(val_all.at[:, step], val_hbm.at[:, chip_of(step)], out_sem.at[1 + step]).wait()
        return carry

    lax.fori_loop(0, chips, settle, 0)
    lax.fori_loop(0, chips, finish, 0)
    pltpu.make_async_copy(off_all, off_hbm, out_sem.at[0]).wait()


def spread_offsets(off, exp_ref):
    off = jnp.where(own_slots((FIVE * HALF, LANES)), jnp.concatenate([off] * FIVE, axis=0), 0.0).astype(BF)
    return dot(off, exp_ref[...])


def grad_chunk(xt, g, mom, off, rowf_ref, lanef_ref, exp_ref, comp_ref, moved_ref, high_ref, low_ref, val_ref, chunk):
    rows = pl.ds(pl.multiple_of(chunk * CHUNK, CHUNK), CHUNK)
    half_rows = pl.ds(pl.multiple_of(chunk * (CHUNK // 2), CHUNK // 2), CHUNK // 2)
    moved = moved_ref.at[rows, :]
    moved[...] = dot(xt[rows, :], g[...]) * (1.0 / math.sqrt(ROWS)) + DECAY * mom[rows, :].astype(F32)
    offsets = spread_offsets(off, exp_ref)
    odd = offsets >= BLOCK
    picked_rows = []
    for p in range(FIVE):
        high, low = split(moved[p * BLOCK:(p + 1) * BLOCK, :])
        freq = dot(rowf_ref[...], jnp.concatenate([high, low, high], axis=0))
        cut = slice(p * HALF, (p + 1) * HALF)
        picked_rows.append(jnp.where(odd[cut], freq[HALF:], freq[:HALF]))
    high, low = split(jnp.concatenate(picked_rows, axis=0))
    spectrum = lane_transform(high, low, lanef_ref[...])
    column = jnp.where(odd, offsets - BLOCK, offsets)
    high, low = split(jnp.where(column == lane_in_block(offsets.shape), spectrum, 0.0))
    high_ref[half_rows, :] = high
    low_ref[half_rows, :] = low
    val_ref[:, :FIVE * HALF] = dot_t(comp_ref[...], high) + dot_t(comp_ref[...], low)


def back_chunk(off, rowi_ref, lanei_ref, exp_ref, moved_ref, high_ref, low_ref, new, chunk):
    base = pl.multiple_of(chunk * CHUNK, CHUNK)
    half_rows = pl.ds(pl.multiple_of(chunk * (CHUNK // 2), CHUNK // 2), CHUNK // 2)
    odd = spread_offsets(off, exp_ref) >= BLOCK
    spread = lane_transform(high_ref[half_rows, :], low_ref[half_rows, :], lanei_ref[...])
    for p in range(FIVE):
        cut = slice(p * HALF, (p + 1) * HALF)
        part = spread[cut]
        high, low = split(jnp.concatenate([jnp.where(odd[cut], 0.0, part), jnp.where(odd[cut], part, 0.0)], axis=0))
        taken = dot(rowi_ref[...], jnp.concatenate([high, low, high], axis=0))
        rows = pl.ds(base + p * BLOCK, BLOCK)
        new[rows, :] = (moved_ref[rows, :] - taken).astype(BF)


def update_kernel(val_ref, off_ref, col_ref, spread_ref, seg_ref, new_in, up_ref, new_out, vals, sums, high_ref, low_ref):
    step = pl.program_id(0)
    groups, blocks = off_ref.shape[:2]
    chips = val_ref.shape[1]
    new_out[...] = new_in[...]

    @pl.when(step == 0)
    def _():
        for r in range(groups):
            line = jnp.concatenate([val_ref[r, c][:, :FIVE * HALF] for c in range(chips)], axis=1)
            for i in range(line.shape[1] // LANES):
                vals[i, r] = line[:, i * LANES:(i + 1) * LANES]

    column = lax.broadcasted_iota(jnp.int32, (BLOCK, LANES), 0).astype(F32)
    powers = []
    for b in range(blocks):
        even = odd = jnp.zeros((BLOCK, LANES), F32)
        for r in range(groups):
            line = off_ref[r, b, pl.ds(step, 1), :]
            val = jnp.broadcast_to(vals[step, r, b:b + 1, :], (BLOCK, LANES))
            even = even + jnp.where(jnp.broadcast_to(line, (BLOCK, LANES)) == column, val, 0.0)
            odd = odd + jnp.where(jnp.broadcast_to(line - BLOCK, (BLOCK, LANES)) == column, val, 0.0)
        sums[b, :, :LANES] = even
        sums[b, :, LANES:] = odd
        powers.append(jnp.sum(even * even + odd * odd, axis=0, keepdims=True))
    powers = jnp.concatenate(powers + [jnp.zeros((16 - blocks, LANES), F32)], axis=0)
    high, low = split(powers)
    power = dot(jnp.concatenate([high, low], axis=1), seg_ref[...])
    scale = lax.rsqrt(power * (1.0 / (BLOCK * BLOCK)) + EPSILON)
    for b in range(blocks):
        row = jnp.concatenate([scale[b:b + 1]] * 2, axis=1)
        high, low = split(sums[b] * row)
        half = dot(col_ref[...], jnp.concatenate([high, low, high], axis=0))
        high, low = split(half)
        high_ref[b * BLOCK:(b + 1) * BLOCK, :] = high
        low_ref[b * BLOCK:(b + 1) * BLOCK, :] = low
    rows = QUAD * BLOCK
    width = high_ref.shape[0]
    for start in range(0, width, 256):
        cut = slice(start, min(start + 256, width))
        field = dot_t(spread_ref[:rows], high_ref[cut]) + dot_t(spread_ref[rows:], high_ref[cut]) + dot_t(spread_ref[:rows], low_ref[cut])
        up_ref[:, cut] = field.astype(BF)


def whole(shape):
    return pl.BlockSpec(shape, lambda i: (0,) * len(shape))


def gather_call(xt, g, mom, picks, t):
    features, width = mom.shape
    reps = picks.shape[0]
    chunks = features // CHUNK
    values = (reps, chunks, LISTED, 2 * LANES)
    offsets = (reps, picks.shape[1], features // (QUAD * BLOCK), LANES)
    small = [picks] + [t[n] for n in NAMES]
    any_space = pl.BlockSpec(memory_space=pl.ANY)
    dma = pltpu.SemaphoreType.DMA
    return pl.pallas_call(
        gather_kernel,
        in_specs=[any_space] * (3 + len(small)),
        out_specs=[any_space] * 3,
        out_shape=[
            jax.ShapeDtypeStruct((features, width), BF),
            jax.ShapeDtypeStruct(values, F32),
            jax.ShapeDtypeStruct(offsets, F32),
        ],
        scratch_shapes=[pltpu.VMEM(a.shape, a.dtype) for a in small] + [
            pltpu.VMEM((features, ROWS), BF),
            pltpu.VMEM(g.shape, BF),
            pltpu.VMEM((features, width), BF),
            pltpu.VMEM((features, width), BF),
            pltpu.VMEM((features, width), F32),
            pltpu.VMEM((features // 2, width), BF),
            pltpu.VMEM((features // 2, width), BF),
            pltpu.VMEM((LANES, LANES), F32),
            pltpu.VMEM((LANES, LANES), F32),
            pltpu.VMEM((chunks, HALF, LANES), F32),
            pltpu.VMEM(offsets, F32),
            pltpu.VMEM(values, F32),
            dma((len(small),)), dma, dma((chunks,)), dma((chunks,)), dma((1 + chunks,)), dma, dma((12,)), dma((12,)), dma((chunks,)), dma((chunks,)), dma((chunks, reps)), dma((chunks, reps)),
        ],
        compiler_params=pltpu.CompilerParams(vmem_limit_bytes=56 * 2**20, collective_id=0, has_side_effects=True),
    )(xt, g, mom, *small)


def update_call(values, off, new, t):
    groups, chips = values.shape[:2]
    blocks, steps = off.shape[1:3]
    rows, width = QUAD * BLOCK, blocks * BLOCK
    names = ("columns", "spread", "segment")
    return pl.pallas_call(
        update_kernel, grid=(new.shape[0] // rows,),
        in_specs=[whole(values.shape), whole(off.shape)] + [whole(t[n].shape) for n in names] + [pl.BlockSpec((rows, width), lambda i: (i, 0))],
        out_specs=[pl.BlockSpec((rows, width), lambda i: (i, 0))] * 2,
        out_shape=[jax.ShapeDtypeStruct(new.shape, BF), jax.ShapeDtypeStruct(new.shape, BF)],
        scratch_shapes=[pltpu.VMEM((new.shape[0] // rows, groups, values.shape[2], LANES), F32),
            pltpu.VMEM((blocks, BLOCK, 2 * LANES), F32), pltpu.VMEM((width, 2 * LANES), BF), pltpu.VMEM((width, 2 * LANES), BF)],
        compiler_params=pltpu.CompilerParams(vmem_limit_bytes=60 * 2**20),
    )(values, off, *(t[n] for n in names), new)


def body(tokens, output_grads, momentum, component_picks):
    width = momentum.shape[2]
    t = {name: jnp.asarray(table) for name, table in tables(width, component_picks.shape[1]).items()}
    picks = jnp.transpose(component_picks, (0, 2, 3, 1))
    new_momentum, values, off = gather_call(tokens.T, output_grads, momentum[0], picks, t)
    update, new_momentum = update_call(values, off, new_momentum, t)
    return (new_momentum[None], update)


def solution(mesh):
    return jax.shard_map(
        body,
        mesh=mesh,
        in_specs=(P("rep", "tp"), P("rep", "tp"), P("rep", None, "tp"), P(None, None, "tp", None)),
        out_specs=(P("rep", None, "tp"), P(None, "tp")),
        check_vma=False,
    )
```

```python
import functools
import math

import jax
import jax.numpy as jnp
import ml_dtypes
import numpy as np
from jax import lax
from jax.experimental import pallas as pl
from jax.experimental.pallas import tpu as pltpu
from jax.sharding import PartitionSpec as P

ROWS = 1024
BLOCK = 64
HALF = 32
FIVE = 5
CHUNK = FIVE * BLOCK
LANES = 128
SLOT = 8
QUAD = 4
LISTED = 16
DECAY = 0.9
EPSILON = 1e-06
NAMES = ("select", "row_fwd", "row_inv", "lane_fwd", "lane_inv", "expand", "compress")
BF = jnp.bfloat16
F32 = jnp.float32


def split_table(table):
    high = table.astype(ml_dtypes.bfloat16)
    low = (table - high.astype(np.float64)).astype(ml_dtypes.bfloat16)
    return high, low


def tables(width, width_rows):
    frequency = np.arange(BLOCK, dtype=np.float64)[:, None]
    position = np.arange(BLOCK, dtype=np.float64)[None, :]
    norm = np.where(frequency == 0, math.sqrt(1.0 / BLOCK), math.sqrt(2.0 / BLOCK))
    cosine = norm * np.cos(math.pi * (2.0 * position + 1.0) * frequency / (2.0 * BLOCK))
    ordered = np.concatenate([cosine[0::2], cosine[1::2]])

    def rows_table(matrix):
        high, low = split_table(matrix)
        return np.concatenate([high, high, low], axis=1)

    def lanes_table(matrix):
        pair = np.zeros((LANES, LANES))
        pair[:BLOCK, :BLOCK] = matrix
        pair[BLOCK:, BLOCK:] = matrix
        high, low = split_table(pair)
        return np.concatenate(
            [np.concatenate([high, low], axis=1), np.concatenate([high, np.zeros_like(low)], axis=1)]
        )

    slot = np.arange(LANES)[:, None] // SLOT
    block = np.arange(width)[None, :] // BLOCK
    expand = (slot == block).astype(ml_dtypes.bfloat16)
    rows = width_rows
    select = np.zeros((width // BLOCK, rows, rows // FIVE * LANES), ml_dtypes.bfloat16)
    for b in range(width // BLOCK):
        for p in range(rows):
            select[b, p, p // FIVE * LANES + b * SLOT + p % FIVE] = 1.0
    high, low = split_table(cosine.T)
    columns = np.concatenate([high, high, low], axis=1)
    spread = np.zeros((QUAD, BLOCK, 2, QUAD, HALF))
    for p in range(QUAD):
        for parity in range(2):
            spread[p, :, parity, p, :] = cosine[parity::2].T
    high, low = split_table(spread.reshape(QUAD * BLOCK, 2 * QUAD * HALF))
    segment = (np.arange(LANES)[:, None] // HALF == np.arange(LANES)[None, :] // HALF).astype(ml_dtypes.bfloat16)
    return {
        "select": select,
        "row_fwd": rows_table(ordered),
        "row_inv": rows_table(ordered.T),
        "lane_fwd": lanes_table(cosine.T),
        "lane_inv": lanes_table(cosine),
        "expand": expand,
        "compress": (np.arange(LISTED)[:, None] == block).astype(ml_dtypes.bfloat16),
        "columns": columns,
        "spread": np.concatenate([high, low]),
        "segment": np.concatenate([segment, segment]),
    }


def dot(a, b):
    return jnp.dot(a, b, preferred_element_type=F32)


def dot_t(a, b):
    return lax.dot_general(a, b, (((1,), (1,)), ((), ())), preferred_element_type=F32)


def split(value):
    high = value.astype(BF)
    return high, (value - high.astype(F32)).astype(BF)


def lane_transform(high, low, weights):
    groups = high.shape[1] // LANES
    parts = []
    for group in range(groups):
        cut = slice(group * LANES, (group + 1) * LANES)
        both = dot(jnp.concatenate([high[:, cut], low[:, cut]], axis=1), weights)
        parts.append(both[:, :LANES] + both[:, LANES:])
    return jnp.concatenate(parts, axis=1)


def own_slots(shape):
    row = lax.broadcasted_iota(jnp.int32, shape, 0) // HALF
    lane = lax.broadcasted_iota(jnp.int32, shape, 1) % SLOT
    return lane == row


def lane_in_block(shape):
    return (lax.broadcasted_iota(jnp.int32, shape, 1) % BLOCK).astype(F32)


def gather_kernel(xt_ref, g_hbm, mom_hbm, *refs):
    count = len(NAMES) + 1
    small_hbm, refs = refs[:count], refs[count:]
    new_hbm, val_hbm, off_hbm = refs[:3]
    small, refs = refs[3:3 + count], refs[3 + count:]
    picks_ref, select_ref, rowf_ref, rowi_ref, lanef_ref, lanei_ref, exp_ref, comp_ref = small
    (xt, g, mom, new, moved, picked_high, picked_low, turned, flipped, off_own, off_all, val_all,
                  small_sem, g_sem, mom_sem, new_sem, out_sem, own_sem, send_sem, recv_sem, pass_sem, sib_sem, vsend_sem, vrecv_sem) = refs
    share = xt_ref.shape[0]
    chips = mom.shape[0] // CHUNK
    line = chips // 2
    reps = val_all.shape[0]
    rep, tp = lax.axis_index("rep"), lax.axis_index("tp")
    core, chip = lax.rem(tp, 2), lax.div(tp, 2)
    x, y = lax.rem(chip, line), lax.div(chip, line)

    def chip_at(dx, dy):
        return lax.rem(y + dy, 2) * line + lax.rem(x + dx, line)

    def device_at(dx, dy):
        return {"tp": chip_at(dx, dy) * 2 + core}

    left, right, across, sibling = device_at(line - 1, 0), device_at(1, 0), device_at(0, 1), {"tp": chip * 2 + 1 - core}

    def chip_of(step):
        dy = jnp.where((step == 3) | (step >= 5), 1, 0)
        dx = jnp.where((step == 1) | (step == 5), line - 1, jnp.where((step == 2) | (step == 6), 1, jnp.where((step == 4) | (step == 7), 2, 0)))
        return chip_at(dx, dy)

    def rows_of(step, first, count):
        start = (chip_of(step) * 2 + core) * share + first
        return xt.at[pl.ds(pl.multiple_of(start, 16), count), :]

    half = share // 2

    def push(index, recv, step, first, count, target, source=None):
        rows = rows_of(step, first, count)
        return pltpu.make_async_remote_copy(
            src_ref=rows if source is None else source, dst_ref=rows,
            send_sem=send_sem.at[index], recv_sem=recv_sem.at[recv],
            device_id=target, device_id_type=pl.DeviceIdType.MESH)

    def arrive(recv, step, first, count):
        push(0, recv, step, first, count, left).wait_recv()

    def to_sibling(step, part, source=None):
        rows = rows_of(step, part * half, half)
        return pltpu.make_async_remote_copy(
            src_ref=rows if source is None else source, dst_ref=rows,
            send_sem=pass_sem.at[step, part], recv_sem=sib_sem.at[step, part],
            device_id=sibling, device_id_type=pl.DeviceIdType.MESH)

    def from_sibling(step, part):
        start = (chip_of(step) * 2 + 1 - core) * share + part * half
        rows = xt.at[pl.ds(pl.multiple_of(start, 16), half), :]
        pltpu.make_async_remote_copy(
            src_ref=rows, dst_ref=rows, send_sem=pass_sem.at[step, part], recv_sem=sib_sem.at[step, part],
            device_id=sibling, device_id_type=pl.DeviceIdType.MESH).wait_recv()

    def mom_copy(step):
        rows = pl.ds(pl.multiple_of(chip_of(step) * CHUNK, CHUNK), CHUNK)
        return pltpu.make_async_copy(mom_hbm.at[rows, :], mom.at[rows, :], mom_sem.at[step])

    def new_copy(step):
        rows = pl.ds(pl.multiple_of(chip_of(step) * CHUNK, CHUNK), CHUNK)
        return pltpu.make_async_copy(new.at[rows, :], new_hbm.at[rows, :], new_sem.at[step])

    def send_values(step, ahead):
        slab = val_all.at[rep, step]
        return pltpu.make_async_remote_copy(
            src_ref=slab, dst_ref=slab,
            send_sem=vsend_sem.at[step, ahead], recv_sem=vrecv_sem.at[step, ahead],
            device_id={"rep": lax.rem(rep + ahead, reps)}, device_id_type=pl.DeviceIdType.MESH)

    def take_values(step, behind):
        slab = val_all.at[lax.rem(rep + reps - behind, reps), step]
        return pltpu.make_async_remote_copy(
            src_ref=slab, dst_ref=slab,
            send_sem=vsend_sem.at[step, behind], recv_sem=vrecv_sem.at[step, behind],
            device_id={"rep": lax.rem(rep + behind, reps)}, device_id_type=pl.DeviceIdType.MESH)

    barrier = pltpu.get_barrier_semaphore()
    for target in (left, right, across, sibling):
        pl.semaphore_signal(barrier, inc=1, device_id=target, device_id_type=pl.DeviceIdType.MESH)
    for ahead in range(1, reps):
        pl.semaphore_signal(barrier, inc=1, device_id={"rep": lax.rem(rep + ahead, reps)}, device_id_type=pl.DeviceIdType.MESH)
    own_rows = rows_of(0, 0, share)
    own_copy = pltpu.make_async_copy(xt_ref, own_rows, own_sem)
    own_copy.start()
    small_copies = [pltpu.make_async_copy(small_hbm[n], small[n], small_sem.at[n]) for n in range(count)]
    for copy in small_copies:
        copy.start()
    g_copy = pltpu.make_async_copy(g_hbm, g, g_sem)
    g_copy.start()
    mom_copy(0).start()

    pl.semaphore_wait(barrier, 4 + reps - 1)

    own_low, own_high = xt_ref.at[pl.ds(0, half), :], xt_ref.at[pl.ds(half, half), :]
    first_pushes = [
        push(0, 0, 0, 0, half, right, own_low), push(1, 1, 0, half, half, left, own_high), push(2, 2, 0, 0, half, across, own_low),
        push(3, 3, 0, half, half, right, own_high), push(4, 4, 0, 0, half, left, own_low), push(5, 5, 0, half, half, across, own_high)]
    to_sibling(0, 0, own_low).start()
    to_sibling(0, 1, own_high).start()
    for copy in first_pushes:
        copy.start()
    for step in range(1, chips):
        mom_copy(step).start()

    small_copies[0].wait()
    small_copies[1].wait()
    blocks = picks_ref.shape[1]
    flat = jnp.zeros((HALF, chips * LANES), F32)
    for b in range(blocks):
        low_bits = (picks_ref[rep, b] & (LANES - 1)).astype(F32).astype(BF)
        flat = flat + dot(low_bits, select_ref[b])
    for part in range(chips):
        off_own[part] = flat[:, part * LANES:(part + 1) * LANES]
    own_copy.wait()
    g_copy.wait()
    for copy in small_copies[2:]:
        copy.wait()

    turned[...] = jnp.zeros_like(turned)

    def turn(r, carry):
        for first in range(0, blocks, QUAD):
            for place in range(min(QUAD, blocks - first)):
                turned[place * HALF:(place + 1) * HALF, :picks_ref.shape[3]] = (picks_ref[r, first + place] & (LANES - 1)).astype(F32)
            flipped[...] = turned[...].T
            for p in range(QUAD):
                lines = flipped[pl.ds(p, off_all.shape[2], stride=QUAD), :]
                for place in range(min(QUAD, blocks - first)):
                    off_all[r, first + place, :, p * HALF:(p + 1) * HALF] = lines[:, place * HALF:(place + 1) * HALF]
        return carry

    later_pushes = {
        6: push(6, 6, 1, 0, half, right), 7: push(7, 7, 2, half, half, left), 8: push(8, 8, 1, 0, half, across),
        9: push(9, 9, 3, half, half, right), 10: push(10, 10, 3, 0, half, left), 11: push(11, 11, 2, half, half, across),
        12: push(12, 12, 4, 0, half, across), 13: push(13, 13, 5, half, half, right)}

    def forward(step):
        chunk = chip_of(step)
        grad_chunk(xt, g, mom, off_own[chunk], rowf_ref, lanef_ref, exp_ref, comp_ref, moved, picked_high, picked_low,
                   val_all.at[rep, step], chunk)

    def backward(step):
        chunk = chip_of(step)
        back_chunk(off_own[chunk], rowi_ref, lanei_ref, exp_ref, moved, picked_high, picked_low, new, chunk)
        new_copy(step).start()

    def backward_step(step, carry):
        backward(step)
        return carry

    def one(step, carry):
        @pl.when(step == 1)
        def _():
            lax.fori_loop(0, reps, turn, 0)
            pltpu.make_async_copy(off_all, off_hbm, out_sem.at[0]).start()
            arrive(0, 1, 0, half)
            later_pushes[6].start()
            to_sibling(1, 0).start()
            arrive(1, 2, half, half)
            later_pushes[7].start()
            to_sibling(2, 1).start()
            arrive(2, 3, 0, half)
            to_sibling(3, 0).start()
            backward(0)
            arrive(3, 1, half, half)
            to_sibling(1, 1).start()
            later_pushes[8].start()
            arrive(4, 2, 0, half)
            later_pushes[10].start()
            to_sibling(2, 0).start()
            arrive(5, 3, half, half)
            later_pushes[9].start()
            later_pushes[11].start()
            to_sibling(3, 1).start()

        @pl.when(step == 2)
        def _():
            arrive(6, 4, 0, half)
            later_pushes[12].start()
            to_sibling(4, 0).start()
            arrive(7, 4, half, half)
            to_sibling(4, 1).start()

        @pl.when(step == 4)
        def _():
            arrive(8, 5, 0, half)
            to_sibling(5, 0).start()
            arrive(9, 5, half, half)
            later_pushes[13].start()
            to_sibling(5, 1).start()

        @pl.when(step == 5)
        def _():
            arrive(10, 6, 0, half)
            to_sibling(6, 0).start()
            arrive(11, 6, half, half)
            to_sibling(6, 1).start()

        @pl.when(step == 7)
        def _():
            arrive(12, 7, 0, half)
            to_sibling(7, 0).start()
            lax.fori_loop(1, 3, backward_step, 0)
            arrive(13, 7, half, half)
            to_sibling(7, 1).start()
            lax.fori_loop(3, 4, backward_step, 0)

        from_sibling(step, 0)
        from_sibling(step, 1)
        mom_copy(step).wait()
        forward(step)
        for ahead in range(1, reps):
            send_values(step, ahead).start()
        return carry

    lax.fori_loop(0, chips, one, 0)
    lax.fori_loop(4, chips, backward_step, 0)
    for copy in first_pushes + list(later_pushes.values()):
        copy.wait_send()

    def settle(step, carry):
        to_sibling(step, 0).wait_send()
        to_sibling(step, 1).wait_send()
        for behind in range(1, reps):
            take_values(step, behind).wait_recv()
        pltpu.make_async_copy(val_all.at[:, step], val_hbm.at[:, chip_of(step)], out_sem.at[1 + step]).start()
        return carry

    def finish(step, carry):
        for ahead in range(1, reps):
            send_values(step, ahead).wait_send()
        new_copy(step).wait()
        pltpu.make_async_copy(val_all.at[:, step], val_hbm.at[:, chip_of(step)], out_sem.at[1 + step]).wait()
        return carry

    lax.fori_loop(0, chips, settle, 0)
    lax.fori_loop(0, chips, finish, 0)
    pltpu.make_async_copy(off_all, off_hbm, out_sem.at[0]).wait()


def spread_offsets(off, exp_ref):
    off = jnp.where(own_slots((FIVE * HALF, LANES)), jnp.concatenate([off] * FIVE, axis=0), 0.0).astype(BF)
    return dot(off, exp_ref[...])


def grad_chunk(xt, g, mom, off, rowf_ref, lanef_ref, exp_ref, comp_ref, moved_ref, high_ref, low_ref, val_ref, chunk):
    rows = pl.ds(pl.multiple_of(chunk * CHUNK, CHUNK), CHUNK)
    half_rows = pl.ds(pl.multiple_of(chunk * (CHUNK // 2), CHUNK // 2), CHUNK // 2)
    moved = moved_ref.at[rows, :]
    moved[...] = dot(xt[rows, :], g[...]) * (1.0 / math.sqrt(ROWS)) + DECAY * mom[rows, :].astype(F32)
    offsets = spread_offsets(off, exp_ref)
    odd = offsets >= BLOCK
    picked_rows = []
    for p in range(FIVE):
        high, low = split(moved[p * BLOCK:(p + 1) * BLOCK, :])
        freq = dot(rowf_ref[...], jnp.concatenate([high, low, high], axis=0))
        cut = slice(p * HALF, (p + 1) * HALF)
        picked_rows.append(jnp.where(odd[cut], freq[HALF:], freq[:HALF]))
    high, low = split(jnp.concatenate(picked_rows, axis=0))
    spectrum = lane_transform(high, low, lanef_ref[...])
    column = jnp.where(odd, offsets - BLOCK, offsets)
    high, low = split(jnp.where(column == lane_in_block(offsets.shape), spectrum, 0.0))
    high_ref[half_rows, :] = high
    low_ref[half_rows, :] = low
    val_ref[:, :FIVE * HALF] = dot_t(comp_ref[...], high) + dot_t(comp_ref[...], low)


def back_chunk(off, rowi_ref, lanei_ref, exp_ref, moved_ref, high_ref, low_ref, new, chunk):
    base = pl.multiple_of(chunk * CHUNK, CHUNK)
    half_rows = pl.ds(pl.multiple_of(chunk * (CHUNK // 2), CHUNK // 2), CHUNK // 2)
    odd = spread_offsets(off, exp_ref) >= BLOCK
    spread = lane_transform(high_ref[half_rows, :], low_ref[half_rows, :], lanei_ref[...])
    for p in range(FIVE):
        cut = slice(p * HALF, (p + 1) * HALF)
        part = spread[cut]
        high, low = split(jnp.concatenate([jnp.where(odd[cut], 0.0, part), jnp.where(odd[cut], part, 0.0)], axis=0))
        taken = dot(rowi_ref[...], jnp.concatenate([high, low, high], axis=0))
        rows = pl.ds(base + p * BLOCK, BLOCK)
        new[rows, :] = (moved_ref[rows, :] - taken).astype(BF)


def update_kernel(val_hbm, off_hbm, col_hbm, spread_hbm, seg_hbm, new_in, up_hbm, new_out,
                  val_ref, off_ref, col_ref, spread_ref, seg_ref, new, up, vals, sums, high_ref, low_ref,
                  small_sem, in_sem, keep_sem, up_sem):
    groups, blocks = off_ref.shape[:2]
    chips = val_ref.shape[1]
    steps = vals.shape[0]
    rows = QUAD * BLOCK
    smalls = [pltpu.make_async_copy(a, b, small_sem.at[n]) for n, (a, b) in enumerate((
        (val_hbm, val_ref), (off_hbm, off_ref), (seg_hbm, seg_ref), (col_hbm, col_ref), (spread_hbm, spread_ref)))]
    for copy in smalls:
        copy.start()

    def piece(ref, step):
        return ref.at[pl.ds(pl.multiple_of(step * rows, rows), rows), :]

    def bring(step):
        return pltpu.make_async_copy(piece(new_in, step), piece(new, step), in_sem.at[step])

    def keep(step):
        return pltpu.make_async_copy(piece(new, step), piece(new_out, step), keep_sem.at[step])

    def hand_out(step):
        return pltpu.make_async_copy(piece(up, step), piece(up_hbm, step), up_sem.at[step])

    for step in range(steps):
        bring(step).start()
    smalls[0].wait()
    for r in range(groups):
        line = jnp.concatenate([val_ref[r, c][:, :FIVE * HALF] for c in range(chips)], axis=1)
        for i in range(steps):
            vals[i, r] = line[:, i * LANES:(i + 1) * LANES]
    for copy in smalls[1:]:
        copy.wait()

    def one(step, carry):
        bring(step).wait()
        keep(step).start()
        column = lax.broadcasted_iota(jnp.int32, (BLOCK, LANES), 0).astype(F32)
        powers = []
        for b in range(blocks):
            even = odd = jnp.zeros((BLOCK, LANES), F32)
            for r in range(groups):
                line = off_ref[r, b, pl.ds(step, 1), :]
                val = jnp.broadcast_to(vals[step, r, b:b + 1, :], (BLOCK, LANES))
                even = even + jnp.where(jnp.broadcast_to(line, (BLOCK, LANES)) == column, val, 0.0)
                odd = odd + jnp.where(jnp.broadcast_to(line - BLOCK, (BLOCK, LANES)) == column, val, 0.0)
            sums[b, :, :LANES] = even
            sums[b, :, LANES:] = odd
            powers.append(jnp.sum(even * even + odd * odd, axis=0, keepdims=True))
        powers = jnp.concatenate(powers + [jnp.zeros((16 - blocks, LANES), F32)], axis=0)
        high, low = split(powers)
        power = dot(jnp.concatenate([high, low], axis=1), seg_ref[...])
        scale = lax.rsqrt(power * (1.0 / (BLOCK * BLOCK)) + EPSILON)
        for b in range(blocks):
            row = jnp.concatenate([scale[b:b + 1]] * 2, axis=1)
            high, low = split(sums[b] * row)
            half = dot(col_ref[...], jnp.concatenate([high, low, high], axis=0))
            high, low = split(half)
            high_ref[b * BLOCK:(b + 1) * BLOCK, :] = high
            low_ref[b * BLOCK:(b + 1) * BLOCK, :] = low
        width = high_ref.shape[0]
        for start in range(0, width, 256):
            cut = slice(start, min(start + 256, width))
            field = dot_t(spread_ref[:rows], high_ref[cut]) + dot_t(spread_ref[rows:], high_ref[cut]) + dot_t(spread_ref[:rows], low_ref[cut])
            up[pl.ds(pl.multiple_of(step * rows, rows), rows), cut] = field.astype(BF)
        hand_out(step).start()
        return carry

    lax.fori_loop(0, steps, one, 0)
    for step in range(steps):
        keep(step).wait()
        hand_out(step).wait()


def gather_call(xt, g, mom, picks, t):
    features, width = mom.shape
    reps = picks.shape[0]
    chunks = features // CHUNK
    values = (reps, chunks, LISTED, 2 * LANES)
    offsets = (reps, picks.shape[1], features // (QUAD * BLOCK), LANES)
    small = [picks] + [t[n] for n in NAMES]
    any_space = pl.BlockSpec(memory_space=pl.ANY)
    dma = pltpu.SemaphoreType.DMA
    return pl.pallas_call(
        gather_kernel,
        in_specs=[any_space] * (3 + len(small)),
        out_specs=[any_space] * 3,
        out_shape=[
            jax.ShapeDtypeStruct((features, width), BF),
            jax.ShapeDtypeStruct(values, F32),
            jax.ShapeDtypeStruct(offsets, F32),
        ],
        scratch_shapes=[pltpu.VMEM(a.shape, a.dtype) for a in small] + [
            pltpu.VMEM((features, ROWS), BF),
            pltpu.VMEM(g.shape, BF),
            pltpu.VMEM((features, width), BF),
            pltpu.VMEM((features, width), BF),
            pltpu.VMEM((features, width), F32),
            pltpu.VMEM((features // 2, width), BF),
            pltpu.VMEM((features // 2, width), BF),
            pltpu.VMEM((LANES, LANES), F32),
            pltpu.VMEM((LANES, LANES), F32),
            pltpu.VMEM((chunks, HALF, LANES), F32),
            pltpu.VMEM(offsets, F32),
            pltpu.VMEM(values, F32),
            dma((len(small),)), dma, dma((chunks,)), dma((chunks,)), dma((1 + chunks,)), dma, dma((14,)), dma((14,)), dma((chunks, 2)), dma((chunks, 2)), dma((chunks, reps)), dma((chunks, reps)),
        ],
        compiler_params=pltpu.CompilerParams(vmem_limit_bytes=56 * 2**20, collective_id=0, has_side_effects=True),
    )(xt, g, mom, *small)


def update_call(values, off, new, t):
    groups, blocks, steps = off.shape[:3]
    width = blocks * BLOCK
    small = [values, off] + [t[n] for n in ("columns", "spread", "segment")]
    any_space, dma = pl.BlockSpec(memory_space=pl.ANY), pltpu.SemaphoreType.DMA
    return pl.pallas_call(
        update_kernel,
        in_specs=[any_space] * (len(small) + 1),
        out_specs=[any_space] * 2,
        out_shape=[jax.ShapeDtypeStruct(new.shape, BF)] * 2,
        scratch_shapes=[pltpu.VMEM(a.shape, a.dtype) for a in small] + [
            pltpu.VMEM(new.shape, BF),
            pltpu.VMEM(new.shape, BF),
            pltpu.VMEM((steps, groups, LISTED, LANES), F32),
            pltpu.VMEM((blocks, BLOCK, 2 * LANES), F32),
            pltpu.VMEM((width, 2 * LANES), BF),
            pltpu.VMEM((width, 2 * LANES), BF),
            dma((len(small),)), dma((steps,)), dma((steps,)), dma((steps,)),
        ],
        compiler_params=pltpu.CompilerParams(vmem_limit_bytes=60 * 2**20),
    )(*small, new)


def body(tokens, output_grads, momentum, component_picks):
    width = momentum.shape[2]
    t = {name: jnp.asarray(table) for name, table in tables(width, component_picks.shape[1]).items()}
    picks = jnp.transpose(component_picks, (0, 2, 3, 1))
    new_momentum, values, off = gather_call(tokens.T, output_grads, momentum[0], picks, t)
    update, new_momentum = update_call(values, off, new_momentum, t)
    return (new_momentum[None], update)


def solution(mesh):
    return jax.shard_map(
        body,
        mesh=mesh,
        in_specs=(P("rep", "tp"), P("rep", "tp"), P("rep", None, "tp"), P(None, None, "tp", None)),
        out_specs=(P("rep", None, "tp"), P(None, "tp")),
        check_vma=False,
    )
```

```python
import functools
import math

import jax
import jax.numpy as jnp
import ml_dtypes
import numpy as np
from jax import lax
from jax.experimental import pallas as pl
from jax.experimental.pallas import tpu as pltpu
from jax.sharding import PartitionSpec as P

ROWS = 1024
BLOCK = 64
HALF = 32
FIVE = 5
CHUNK = FIVE * BLOCK
LANES = 128
SLOT = 8
QUAD = 4
LISTED = 16
DECAY = 0.9
EPSILON = 1e-06
NAMES = ("select", "row_fwd", "row_inv", "lane_fwd", "lane_inv", "expand", "compress")
BF = jnp.bfloat16
F32 = jnp.float32


def split_table(table):
    high = table.astype(ml_dtypes.bfloat16)
    low = (table - high.astype(np.float64)).astype(ml_dtypes.bfloat16)
    return high, low


def tables(width, width_rows):
    frequency = np.arange(BLOCK, dtype=np.float64)[:, None]
    position = np.arange(BLOCK, dtype=np.float64)[None, :]
    norm = np.where(frequency == 0, math.sqrt(1.0 / BLOCK), math.sqrt(2.0 / BLOCK))
    cosine = norm * np.cos(math.pi * (2.0 * position + 1.0) * frequency / (2.0 * BLOCK))
    ordered = np.concatenate([cosine[0::2], cosine[1::2]])

    def rows_table(matrix):
        high, low = split_table(matrix)
        return np.concatenate([high, high, low], axis=1)

    def lanes_table(matrix):
        pair = np.zeros((LANES, LANES))
        pair[:BLOCK, :BLOCK] = matrix
        pair[BLOCK:, BLOCK:] = matrix
        high, low = split_table(pair)
        return np.concatenate(
            [np.concatenate([high, low], axis=1), np.concatenate([high, np.zeros_like(low)], axis=1)]
        )

    slot = np.arange(LANES)[:, None] // SLOT
    block = np.arange(width)[None, :] // BLOCK
    expand = (slot == block).astype(ml_dtypes.bfloat16)
    rows = width_rows
    select = np.zeros((width // BLOCK, rows, rows // FIVE * LANES), ml_dtypes.bfloat16)
    for b in range(width // BLOCK):
        for p in range(rows):
            select[b, p, p // FIVE * LANES + b * SLOT + p % FIVE] = 1.0
    high, low = split_table(cosine.T)
    columns = np.concatenate([high, high, low], axis=1)
    spread = np.zeros((QUAD, BLOCK, 2, QUAD, HALF))
    for p in range(QUAD):
        for parity in range(2):
            spread[p, :, parity, p, :] = 0.5 * (cosine[0::2] + (1 - 2 * parity) * cosine[1::2]).T
    high, low = split_table(spread.reshape(QUAD * BLOCK, 2 * QUAD * HALF))
    segment = (np.arange(LANES)[:, None] // HALF == np.arange(LANES)[None, :] // HALF).astype(ml_dtypes.bfloat16)
    return {
        "select": select,
        "row_fwd": rows_table(ordered),
        "row_inv": rows_table(ordered.T),
        "lane_fwd": lanes_table(cosine.T),
        "lane_inv": lanes_table(cosine),
        "expand": expand,
        "compress": (np.arange(LISTED)[:, None] == block).astype(ml_dtypes.bfloat16),
        "columns": columns,
        "spread": np.concatenate([high, high, low], axis=1),
        "segment": np.concatenate([segment, segment]),
    }


def dot(a, b):
    return jnp.dot(a, b, preferred_element_type=F32)


def dot_t(a, b):
    return lax.dot_general(a, b, (((1,), (1,)), ((), ())), preferred_element_type=F32)


def split(value):
    high = value.astype(BF)
    return high, (value - high.astype(F32)).astype(BF)


def lane_transform(high, low, weights):
    groups = high.shape[1] // LANES
    parts = []
    for group in range(groups):
        cut = slice(group * LANES, (group + 1) * LANES)
        both = dot(jnp.concatenate([high[:, cut], low[:, cut]], axis=1), weights)
        parts.append(both[:, :LANES] + both[:, LANES:])
    return jnp.concatenate(parts, axis=1)


def own_slots(shape):
    row = lax.broadcasted_iota(jnp.int32, shape, 0) // HALF
    lane = lax.broadcasted_iota(jnp.int32, shape, 1) % SLOT
    return lane == row


def lane_in_block(shape):
    return (lax.broadcasted_iota(jnp.int32, shape, 1) % BLOCK).astype(F32)


def gather_kernel(xt_ref, g_hbm, mom_hbm, *refs):
    count = len(NAMES) + 1
    small_hbm, refs = refs[:count], refs[count:]
    new_hbm, val_hbm, off_hbm = refs[:3]
    small, refs = refs[3:3 + count], refs[3 + count:]
    picks_ref, select_ref, rowf_ref, rowi_ref, lanef_ref, lanei_ref, exp_ref, comp_ref = small
    (xt, g, mom, new, moved, picked_high, picked_low, turned, flipped, off_own, off_all, val_all,
                  small_sem, g_sem, mom_sem, new_sem, out_sem, own_sem, send_sem, recv_sem, pass_sem, sib_sem, vsend_sem, vrecv_sem) = refs
    share = xt_ref.shape[0]
    chips = mom.shape[0] // CHUNK
    line = chips // 2
    reps = val_all.shape[0]
    rep, tp = lax.axis_index("rep"), lax.axis_index("tp")
    core, chip = lax.rem(tp, 2), lax.div(tp, 2)
    x, y = lax.rem(chip, line), lax.div(chip, line)

    def chip_at(dx, dy):
        return lax.rem(y + dy, 2) * line + lax.rem(x + dx, line)

    def device_at(dx, dy):
        return {"tp": chip_at(dx, dy) * 2 + core}

    left, right, across, sibling = device_at(line - 1, 0), device_at(1, 0), device_at(0, 1), {"tp": chip * 2 + 1 - core}

    def chip_of(step):
        dy = jnp.where((step == 3) | (step >= 5), 1, 0)
        dx = jnp.where((step == 1) | (step == 5), line - 1, jnp.where((step == 2) | (step == 6), 1, jnp.where((step == 4) | (step == 7), 2, 0)))
        return chip_at(dx, dy)

    def rows_of(step, first, count):
        start = (chip_of(step) * 2 + core) * share + first
        return xt.at[pl.ds(pl.multiple_of(start, 16), count), :]

    half = share // 2

    def push(index, recv, step, first, count, target, source=None):
        rows = rows_of(step, first, count)
        return pltpu.make_async_remote_copy(
            src_ref=rows if source is None else source, dst_ref=rows,
            send_sem=send_sem.at[index], recv_sem=recv_sem.at[recv],
            device_id=target, device_id_type=pl.DeviceIdType.MESH)

    def arrive(recv, step, first, count):
        push(0, recv, step, first, count, left).wait_recv()

    def to_sibling(step, part, source=None):
        rows = rows_of(step, part * half, half)
        return pltpu.make_async_remote_copy(
            src_ref=rows if source is None else source, dst_ref=rows,
            send_sem=pass_sem.at[step, part], recv_sem=sib_sem.at[step, part],
            device_id=sibling, device_id_type=pl.DeviceIdType.MESH)

    def from_sibling(step, part):
        start = (chip_of(step) * 2 + 1 - core) * share + part * half
        rows = xt.at[pl.ds(pl.multiple_of(start, 16), half), :]
        pltpu.make_async_remote_copy(
            src_ref=rows, dst_ref=rows, send_sem=pass_sem.at[step, part], recv_sem=sib_sem.at[step, part],
            device_id=sibling, device_id_type=pl.DeviceIdType.MESH).wait_recv()

    def mom_copy(step):
        rows = pl.ds(pl.multiple_of(chip_of(step) * CHUNK, CHUNK), CHUNK)
        return pltpu.make_async_copy(mom_hbm.at[rows, :], mom.at[rows, :], mom_sem.at[step])

    def new_copy(step):
        rows = pl.ds(pl.multiple_of(chip_of(step) * CHUNK, CHUNK), CHUNK)
        return pltpu.make_async_copy(new.at[rows, :], new_hbm.at[rows, :], new_sem.at[step])

    def send_values(step, ahead):
        slab = val_all.at[rep, step]
        return pltpu.make_async_remote_copy(
            src_ref=slab, dst_ref=slab,
            send_sem=vsend_sem.at[step, ahead], recv_sem=vrecv_sem.at[step, ahead],
            device_id={"rep": lax.rem(rep + ahead, reps)}, device_id_type=pl.DeviceIdType.MESH)

    def take_values(step, behind):
        slab = val_all.at[lax.rem(rep + reps - behind, reps), step]
        return pltpu.make_async_remote_copy(
            src_ref=slab, dst_ref=slab,
            send_sem=vsend_sem.at[step, behind], recv_sem=vrecv_sem.at[step, behind],
            device_id={"rep": lax.rem(rep + behind, reps)}, device_id_type=pl.DeviceIdType.MESH)

    barrier = pltpu.get_barrier_semaphore()
    for target in (left, right, across, sibling):
        pl.semaphore_signal(barrier, inc=1, device_id=target, device_id_type=pl.DeviceIdType.MESH)
    for ahead in range(1, reps):
        pl.semaphore_signal(barrier, inc=1, device_id={"rep": lax.rem(rep + ahead, reps)}, device_id_type=pl.DeviceIdType.MESH)
    own_rows = rows_of(0, 0, share)
    own_copy = pltpu.make_async_copy(xt_ref, own_rows, own_sem)
    own_copy.start()
    small_copies = [pltpu.make_async_copy(small_hbm[n], small[n], small_sem.at[n]) for n in range(count)]
    for copy in small_copies:
        copy.start()
    g_copy = pltpu.make_async_copy(g_hbm, g, g_sem)
    g_copy.start()
    mom_copy(0).start()

    pl.semaphore_wait(barrier, 4 + reps - 1)

    own_low, own_high = xt_ref.at[pl.ds(0, half), :], xt_ref.at[pl.ds(half, half), :]
    first_pushes = [
        push(0, 0, 0, 0, half, right, own_low), push(1, 1, 0, half, half, left, own_high), push(2, 2, 0, 0, half, across, own_low),
        push(3, 3, 0, half, half, right, own_high), push(4, 4, 0, 0, half, left, own_low), push(5, 5, 0, half, half, across, own_high)]
    to_sibling(0, 0, own_low).start()
    to_sibling(0, 1, own_high).start()
    for copy in first_pushes:
        copy.start()
    for step in range(1, chips):
        mom_copy(step).start()

    small_copies[0].wait()
    small_copies[1].wait()
    blocks = picks_ref.shape[1]
    flat = jnp.zeros((HALF, chips * LANES), F32)
    for b in range(blocks):
        low_bits = (picks_ref[rep, b] & (LANES - 1)).astype(F32).astype(BF)
        flat = flat + dot(low_bits, select_ref[b])
    for part in range(chips):
        off_own[part] = flat[:, part * LANES:(part + 1) * LANES]
    own_copy.wait()
    g_copy.wait()
    for copy in small_copies[2:]:
        copy.wait()

    turned[...] = jnp.zeros_like(turned)

    def turn(r, carry):
        for first in range(0, blocks, QUAD):
            for place in range(min(QUAD, blocks - first)):
                turned[place * HALF:(place + 1) * HALF, :picks_ref.shape[3]] = (picks_ref[r, first + place] & (LANES - 1)).astype(F32)
            flipped[...] = turned[...].T
            for p in range(QUAD):
                lines = flipped[pl.ds(p, off_all.shape[2], stride=QUAD), :]
                for place in range(min(QUAD, blocks - first)):
                    off_all[r, first + place, :, p * HALF:(p + 1) * HALF] = lines[:, place * HALF:(place + 1) * HALF]
        return carry

    later_pushes = {
        6: push(6, 6, 1, 0, half, right), 7: push(7, 7, 2, half, half, left), 8: push(8, 8, 1, 0, half, across),
        9: push(9, 9, 3, half, half, right), 10: push(10, 10, 3, 0, half, left), 11: push(11, 11, 2, half, half, across),
        12: push(12, 12, 4, 0, half, across), 13: push(13, 13, 5, half, half, right)}

    def forward(step):
        chunk = chip_of(step)
        grad_chunk(xt, g, mom, off_own[chunk], rowf_ref, lanef_ref, exp_ref, comp_ref, moved, picked_high, picked_low,
                   val_all.at[rep, step], chunk)

    def backward(step):
        chunk = chip_of(step)
        back_chunk(off_own[chunk], rowi_ref, lanei_ref, exp_ref, moved, picked_high, picked_low, new, chunk)
        new_copy(step).start()

    def backward_step(step, carry):
        backward(step)
        return carry

    def one(step, carry):
        @pl.when(step == 1)
        def _():
            lax.fori_loop(0, reps, turn, 0)
            pltpu.make_async_copy(off_all, off_hbm, out_sem.at[0]).start()
            arrive(0, 1, 0, half)
            later_pushes[6].start()
            to_sibling(1, 0).start()
            arrive(1, 2, half, half)
            later_pushes[7].start()
            to_sibling(2, 1).start()
            arrive(2, 3, 0, half)
            to_sibling(3, 0).start()
            backward(0)
            arrive(3, 1, half, half)
            to_sibling(1, 1).start()
            later_pushes[8].start()
            arrive(4, 2, 0, half)
            later_pushes[10].start()
            to_sibling(2, 0).start()
            arrive(5, 3, half, half)
            later_pushes[9].start()
            later_pushes[11].start()
            to_sibling(3, 1).start()

        @pl.when(step == 2)
        def _():
            arrive(6, 4, 0, half)
            later_pushes[12].start()
            to_sibling(4, 0).start()
            arrive(7, 4, half, half)
            to_sibling(4, 1).start()

        @pl.when(step == 4)
        def _():
            arrive(8, 5, 0, half)
            to_sibling(5, 0).start()
            arrive(9, 5, half, half)
            later_pushes[13].start()
            to_sibling(5, 1).start()

        @pl.when(step == 5)
        def _():
            arrive(10, 6, 0, half)
            to_sibling(6, 0).start()
            arrive(11, 6, half, half)
            to_sibling(6, 1).start()

        @pl.when(step == 7)
        def _():
            arrive(12, 7, 0, half)
            to_sibling(7, 0).start()
            lax.fori_loop(1, 3, backward_step, 0)
            arrive(13, 7, half, half)
            to_sibling(7, 1).start()
            lax.fori_loop(3, 4, backward_step, 0)

        from_sibling(step, 0)
        from_sibling(step, 1)
        mom_copy(step).wait()
        forward(step)
        for ahead in range(1, reps):
            send_values(step, ahead).start()
        return carry

    lax.fori_loop(0, chips, one, 0)
    lax.fori_loop(4, chips, backward_step, 0)
    for copy in first_pushes + list(later_pushes.values()):
        copy.wait_send()

    def settle(step, carry):
        to_sibling(step, 0).wait_send()
        to_sibling(step, 1).wait_send()
        for behind in range(1, reps):
            take_values(step, behind).wait_recv()
        pltpu.make_async_copy(val_all.at[:, step], val_hbm.at[:, chip_of(step)], out_sem.at[1 + step]).start()
        return carry

    def finish(step, carry):
        for ahead in range(1, reps):
            send_values(step, ahead).wait_send()
        new_copy(step).wait()
        pltpu.make_async_copy(val_all.at[:, step], val_hbm.at[:, chip_of(step)], out_sem.at[1 + step]).wait()
        return carry

    lax.fori_loop(0, chips, settle, 0)
    lax.fori_loop(0, chips, finish, 0)
    pltpu.make_async_copy(off_all, off_hbm, out_sem.at[0]).wait()


def spread_offsets(off, exp_ref):
    off = jnp.where(own_slots((FIVE * HALF, LANES)), jnp.concatenate([off] * FIVE, axis=0), 0.0).astype(BF)
    return dot(off, exp_ref[...])


def grad_chunk(xt, g, mom, off, rowf_ref, lanef_ref, exp_ref, comp_ref, moved_ref, high_ref, low_ref, val_ref, chunk):
    rows = pl.ds(pl.multiple_of(chunk * CHUNK, CHUNK), CHUNK)
    half_rows = pl.ds(pl.multiple_of(chunk * (CHUNK // 2), CHUNK // 2), CHUNK // 2)
    moved = moved_ref.at[rows, :]
    moved[...] = dot(xt[rows, :], g[...]) * (1.0 / math.sqrt(ROWS)) + DECAY * mom[rows, :].astype(F32)
    offsets = spread_offsets(off, exp_ref)
    odd = offsets >= BLOCK
    picked_rows = []
    for p in range(FIVE):
        high, low = split(moved[p * BLOCK:(p + 1) * BLOCK, :])
        freq = dot(rowf_ref[...], jnp.concatenate([high, low, high], axis=0))
        cut = slice(p * HALF, (p + 1) * HALF)
        picked_rows.append(jnp.where(odd[cut], freq[HALF:], freq[:HALF]))
    high, low = split(jnp.concatenate(picked_rows, axis=0))
    spectrum = lane_transform(high, low, lanef_ref[...])
    column = jnp.where(odd, offsets - BLOCK, offsets)
    high, low = split(jnp.where(column == lane_in_block(offsets.shape), spectrum, 0.0))
    high_ref[half_rows, :] = high
    low_ref[half_rows, :] = low
    val_ref[:, :FIVE * HALF] = dot_t(comp_ref[...], high) + dot_t(comp_ref[...], low)


def back_chunk(off, rowi_ref, lanei_ref, exp_ref, moved_ref, high_ref, low_ref, new, chunk):
    base = pl.multiple_of(chunk * CHUNK, CHUNK)
    half_rows = pl.ds(pl.multiple_of(chunk * (CHUNK // 2), CHUNK // 2), CHUNK // 2)
    odd = spread_offsets(off, exp_ref) >= BLOCK
    spread = lane_transform(high_ref[half_rows, :], low_ref[half_rows, :], lanei_ref[...])
    for p in range(FIVE):
        cut = slice(p * HALF, (p + 1) * HALF)
        part = spread[cut]
        high, low = split(jnp.concatenate([jnp.where(odd[cut], 0.0, part), jnp.where(odd[cut], part, 0.0)], axis=0))
        taken = dot(rowi_ref[...], jnp.concatenate([high, low, high], axis=0))
        rows = pl.ds(base + p * BLOCK, BLOCK)
        new[rows, :] = (moved_ref[rows, :] - taken).astype(BF)


def update_kernel(val_hbm, off_hbm, col_hbm, spread_hbm, seg_hbm, new_in, up_hbm, new_out,
                  val_ref, off_ref, col_ref, spread_ref, seg_ref, new, up, vals, sums, half_ref,
                  small_sem, in_sem, keep_sem, up_sem):
    groups, blocks = off_ref.shape[:2]
    chips = val_ref.shape[1]
    steps = vals.shape[0]
    rows = QUAD * BLOCK
    smalls = [pltpu.make_async_copy(a, b, small_sem.at[n]) for n, (a, b) in enumerate((
        (val_hbm, val_ref), (off_hbm, off_ref), (seg_hbm, seg_ref), (col_hbm, col_ref), (spread_hbm, spread_ref)))]
    for copy in smalls:
        copy.start()

    def piece(ref, step):
        return ref.at[pl.ds(pl.multiple_of(step * rows, rows), rows), :]

    def bring(step):
        return pltpu.make_async_copy(piece(new_in, step), piece(new, step), in_sem.at[step])

    def keep(step):
        return pltpu.make_async_copy(piece(new, step), piece(new_out, step), keep_sem.at[step])

    def hand_out(step):
        return pltpu.make_async_copy(piece(up, step), piece(up_hbm, step), up_sem.at[step])

    smalls[0].wait()
    for r in range(groups):
        line = jnp.concatenate([val_ref[r, c][:, :FIVE * HALF] for c in range(chips)], axis=1)
        for i in range(steps):
            vals[i, r] = line[:, i * LANES:(i + 1) * LANES]
    for copy in smalls[1:]:
        copy.wait()

    def one(step, carry):
        bring(step).start()
        shape = (BLOCK // 8, 8, LANES)
        column = (lax.broadcasted_iota(jnp.int32, shape, 0) * 8 + lax.broadcasted_iota(jnp.int32, shape, 1)).astype(F32)
        powers = []
        for b in range(blocks):
            total = signed = jnp.zeros(shape, F32)
            for r in range(groups):
                off = jnp.broadcast_to(off_ref[r, b, pl.ds(step, 1), :], (8, LANES))
                val = jnp.broadcast_to(vals[step, r, b:b + 1, :], (8, LANES))
                odd = off >= BLOCK
                place = jnp.where(odd, off - BLOCK, off)[None] == column
                total = total + jnp.where(place, val[None], 0.0)
                signed = signed + jnp.where(place, jnp.where(odd, -val, val)[None], 0.0)
            sums[b, :, :LANES] = total.reshape(BLOCK, LANES)
            sums[b, :, LANES:] = signed.reshape(BLOCK, LANES)
            powers.append(jnp.sum(jnp.sum(total * total + signed * signed, axis=0), axis=0, keepdims=True))
        powers = jnp.concatenate(powers + [jnp.zeros((16 - blocks, LANES), F32)], axis=0)
        high, low = split(powers)
        power = dot(jnp.concatenate([high, low], axis=1), seg_ref[...])
        scale = lax.rsqrt(power * (0.5 / (BLOCK * BLOCK)) + EPSILON)
        for b in range(blocks):
            row = jnp.concatenate([scale[b:b + 1]] * 2, axis=1)
            high, low = split(sums[b] * row)
            half = dot(col_ref[...], jnp.concatenate([high, low, high], axis=0))
            high, low = split(half)
            half_ref[b * BLOCK:(b + 1) * BLOCK, :] = jnp.concatenate([high, low, high], axis=1)
        width = half_ref.shape[0]
        for start in range(0, width, 256):
            cut = slice(start, min(start + 256, width))
            field = dot_t(spread_ref[...], half_ref[cut])
            up[pl.ds(pl.multiple_of(step * rows, rows), rows), cut] = field.astype(BF)
        bring(step).wait()
        keep(step).start()
        hand_out(step).start()
        return carry

    lax.fori_loop(0, steps, one, 0)
    for step in range(steps):
        keep(step).wait()
        hand_out(step).wait()


def gather_call(xt, g, mom, picks, t):
    features, width = mom.shape
    reps = picks.shape[0]
    chunks = features // CHUNK
    values = (reps, chunks, LISTED, 2 * LANES)
    offsets = (reps, picks.shape[1], features // (QUAD * BLOCK), LANES)
    small = [picks] + [t[n] for n in NAMES]
    any_space = pl.BlockSpec(memory_space=pl.ANY)
    dma = pltpu.SemaphoreType.DMA
    return pl.pallas_call(
        gather_kernel,
        in_specs=[any_space] * (3 + len(small)),
        out_specs=[any_space] * 3,
        out_shape=[
            jax.ShapeDtypeStruct((features, width), BF),
            jax.ShapeDtypeStruct(values, F32),
            jax.ShapeDtypeStruct(offsets, F32),
        ],
        scratch_shapes=[pltpu.VMEM(a.shape, a.dtype) for a in small] + [
            pltpu.VMEM((features, ROWS), BF),
            pltpu.VMEM(g.shape, BF),
            pltpu.VMEM((features, width), BF),
            pltpu.VMEM((features, width), BF),
            pltpu.VMEM((features, width), F32),
            pltpu.VMEM((features // 2, width), BF),
            pltpu.VMEM((features // 2, width), BF),
            pltpu.VMEM((LANES, LANES), F32),
            pltpu.VMEM((LANES, LANES), F32),
            pltpu.VMEM((chunks, HALF, LANES), F32),
            pltpu.VMEM(offsets, F32),
            pltpu.VMEM(values, F32),
            dma((len(small),)), dma, dma((chunks,)), dma((chunks,)), dma((1 + chunks,)), dma, dma((14,)), dma((14,)), dma((chunks, 2)), dma((chunks, 2)), dma((chunks, reps)), dma((chunks, reps)),
        ],
        compiler_params=pltpu.CompilerParams(vmem_limit_bytes=56 * 2**20, collective_id=0, has_side_effects=True),
    )(xt, g, mom, *small)


def update_call(values, off, new, t):
    groups, blocks, steps = off.shape[:3]
    width = blocks * BLOCK
    small = [values, off] + [t[n] for n in ("columns", "spread", "segment")]
    any_space, dma = pl.BlockSpec(memory_space=pl.ANY), pltpu.SemaphoreType.DMA
    return pl.pallas_call(
        update_kernel,
        in_specs=[any_space] * (len(small) + 1),
        out_specs=[any_space] * 2,
        out_shape=[jax.ShapeDtypeStruct(new.shape, BF)] * 2,
        scratch_shapes=[pltpu.VMEM(a.shape, a.dtype) for a in small] + [
            pltpu.VMEM(new.shape, BF),
            pltpu.VMEM(new.shape, BF),
            pltpu.VMEM((steps, groups, LISTED, LANES), F32),
            pltpu.VMEM((blocks, BLOCK, 2 * LANES), F32),
            pltpu.VMEM((width, 6 * LANES), BF),
            dma((len(small),)), dma((steps,)), dma((steps,)), dma((steps,)),
        ],
        compiler_params=pltpu.CompilerParams(vmem_limit_bytes=60 * 2**20),
    )(*small, new)


def body(tokens, output_grads, momentum, component_picks):
    width = momentum.shape[2]
    t = {name: jnp.asarray(table) for name, table in tables(width, component_picks.shape[1]).items()}
    picks = jnp.transpose(component_picks, (0, 2, 3, 1))
    new_momentum, values, off = gather_call(tokens.T, output_grads, momentum[0], picks, t)
    update, new_momentum = update_call(values, off, new_momentum, t)
    return (new_momentum[None], update)


def solution(mesh):
    return jax.shard_map(
        body,
        mesh=mesh,
        in_specs=(P("rep", "tp"), P("rep", "tp"), P("rep", None, "tp"), P(None, None, "tp", None)),
        out_specs=(P("rep", None, "tp"), P(None, "tp")),
        check_vma=False,
    )
```

```python
import functools
import math

import jax
import jax.numpy as jnp
import ml_dtypes
import numpy as np
from jax import lax
from jax.experimental import pallas as pl
from jax.experimental.pallas import tpu as pltpu
from jax.sharding import PartitionSpec as P

ROWS = 1024
BLOCK = 64
HALF = 32
FIVE = 5
CHUNK = FIVE * BLOCK
LANES = 128
SLOT = 8
QUAD = 4
LISTED = 16
DECAY = 0.9
EPSILON = 1e-06
NAMES = ("select", "row_fwd", "row_inv", "lane_fwd", "lane_inv", "expand", "compress")
BF = jnp.bfloat16
F32 = jnp.float32


def split_table(table):
    high = table.astype(ml_dtypes.bfloat16)
    low = (table - high.astype(np.float64)).astype(ml_dtypes.bfloat16)
    return high, low


def tables(width, width_rows):
    frequency = np.arange(BLOCK, dtype=np.float64)[:, None]
    position = np.arange(BLOCK, dtype=np.float64)[None, :]
    norm = np.where(frequency == 0, math.sqrt(1.0 / BLOCK), math.sqrt(2.0 / BLOCK))
    cosine = norm * np.cos(math.pi * (2.0 * position + 1.0) * frequency / (2.0 * BLOCK))
    ordered = np.concatenate([cosine[0::2], cosine[1::2]])

    def rows_table(matrix):
        high, low = split_table(matrix)
        return np.concatenate([high, high, low], axis=1)

    def lanes_table(matrix):
        pair = np.zeros((LANES, LANES))
        pair[:BLOCK, :BLOCK] = matrix
        pair[BLOCK:, BLOCK:] = matrix
        high, low = split_table(pair)
        return np.concatenate(
            [np.concatenate([high, low], axis=1), np.concatenate([high, np.zeros_like(low)], axis=1)]
        )

    slot = np.arange(LANES)[:, None] // SLOT
    block = np.arange(width)[None, :] // BLOCK
    expand = (slot == block).astype(ml_dtypes.bfloat16)
    rows = width_rows
    select = np.zeros((width // BLOCK, rows, rows // FIVE * LANES), ml_dtypes.bfloat16)
    for b in range(width // BLOCK):
        for p in range(rows):
            select[b, p, p // FIVE * LANES + b * SLOT + p % FIVE] = 1.0
    high, low = split_table(cosine.T)
    columns = np.concatenate([high, high, low], axis=1)
    spread = np.zeros((QUAD, BLOCK, 2, QUAD, HALF))
    for p in range(QUAD):
        for parity in range(2):
            spread[p, :, parity, p, :] = 0.5 * (cosine[0::2] + (1 - 2 * parity) * cosine[1::2]).T
    high, low = split_table(spread.reshape(QUAD * BLOCK, 2 * QUAD * HALF))
    segment = (np.arange(LANES)[:, None] // HALF == np.arange(LANES)[None, :] // HALF).astype(ml_dtypes.bfloat16)
    return {
        "select": select,
        "row_fwd": rows_table(ordered),
        "row_inv": rows_table(ordered.T),
        "lane_fwd": lanes_table(cosine.T),
        "lane_inv": lanes_table(cosine),
        "expand": expand,
        "compress": (np.arange(LISTED)[:, None] == block).astype(ml_dtypes.bfloat16),
        "columns": columns,
        "spread": np.concatenate([high, high, low], axis=1),
        "segment": np.concatenate([segment, segment]),
    }


def dot(a, b):
    return jnp.dot(a, b, preferred_element_type=F32)


def dot_t(a, b):
    return lax.dot_general(a, b, (((1,), (1,)), ((), ())), preferred_element_type=F32)


def split(value):
    high = value.astype(BF)
    return high, (value - high.astype(F32)).astype(BF)


def lane_transform(high, low, weights):
    groups = high.shape[1] // LANES
    parts = []
    for group in range(groups):
        cut = slice(group * LANES, (group + 1) * LANES)
        both = dot(jnp.concatenate([high[:, cut], low[:, cut]], axis=1), weights)
        parts.append(both[:, :LANES] + both[:, LANES:])
    return jnp.concatenate(parts, axis=1)


def own_slots(shape):
    row = lax.broadcasted_iota(jnp.int32, shape, 0) // HALF
    lane = lax.broadcasted_iota(jnp.int32, shape, 1) % SLOT
    return lane == row


def lane_in_block(shape):
    return (lax.broadcasted_iota(jnp.int32, shape, 1) % BLOCK).astype(F32)


def gather_kernel(xt_ref, g_hbm, mom_hbm, *refs):
    count = len(NAMES) + 1
    small_hbm, refs = refs[:count], refs[count:]
    new_hbm, val_hbm, off_hbm = refs[:3]
    small, refs = refs[3:3 + count], refs[3 + count:]
    picks_ref, select_ref, rowf_ref, rowi_ref, lanef_ref, lanei_ref, exp_ref, comp_ref = small
    (xt, g, mom, new, moved, picked_high, picked_low, turned, flipped, off_own, off_all, val_all,
                  small_sem, g_sem, mom_sem, new_sem, out_sem, own_sem, send_sem, recv_sem, pass_sem, sib_sem, vsend_sem, vrecv_sem) = refs
    share = xt_ref.shape[0]
    chips = mom.shape[0] // CHUNK
    line = chips // 2
    reps = val_all.shape[0]
    rep, tp = lax.axis_index("rep"), lax.axis_index("tp")
    core, chip = lax.rem(tp, 2), lax.div(tp, 2)
    x, y = lax.rem(chip, line), lax.div(chip, line)

    def chip_at(dx, dy):
        return lax.rem(y + dy, 2) * line + lax.rem(x + dx, line)

    def device_at(dx, dy):
        return {"tp": chip_at(dx, dy) * 2 + core}

    left, right, across, sibling = device_at(line - 1, 0), device_at(1, 0), device_at(0, 1), {"tp": chip * 2 + 1 - core}

    def chip_of(step):
        dy = jnp.where((step == 3) | (step >= 5), 1, 0)
        dx = jnp.where((step == 1) | (step == 5), line - 1, jnp.where((step == 2) | (step == 6), 1, jnp.where((step == 4) | (step == 7), 2, 0)))
        return chip_at(dx, dy)

    def rows_of(step, first, count):
        start = (chip_of(step) * 2 + core) * share + first
        return xt.at[pl.ds(pl.multiple_of(start, 16), count), :]

    half = share // 2

    def push(index, recv, step, first, count, target, source=None):
        rows = rows_of(step, first, count)
        return pltpu.make_async_remote_copy(
            src_ref=rows if source is None else source, dst_ref=rows,
            send_sem=send_sem.at[index], recv_sem=recv_sem.at[recv],
            device_id=target, device_id_type=pl.DeviceIdType.MESH)

    def arrive(recv, step, first, count):
        push(0, recv, step, first, count, left).wait_recv()

    def to_sibling(step, part, source=None):
        rows = rows_of(step, part * half, half)
        return pltpu.make_async_remote_copy(
            src_ref=rows if source is None else source, dst_ref=rows,
            send_sem=pass_sem.at[step, part], recv_sem=sib_sem.at[step, part],
            device_id=sibling, device_id_type=pl.DeviceIdType.MESH)

    def from_sibling(step, part):
        start = (chip_of(step) * 2 + 1 - core) * share + part * half
        rows = xt.at[pl.ds(pl.multiple_of(start, 16), half), :]
        pltpu.make_async_remote_copy(
            src_ref=rows, dst_ref=rows, send_sem=pass_sem.at[step, part], recv_sem=sib_sem.at[step, part],
            device_id=sibling, device_id_type=pl.DeviceIdType.MESH).wait_recv()

    def mom_copy(step):
        rows = pl.ds(pl.multiple_of(chip_of(step) * CHUNK, CHUNK), CHUNK)
        return pltpu.make_async_copy(mom_hbm.at[rows, :], mom.at[rows, :], mom_sem.at[step])

    def new_copy(step):
        rows = pl.ds(pl.multiple_of(chip_of(step) * CHUNK, CHUNK), CHUNK)
        return pltpu.make_async_copy(new.at[rows, :], new_hbm.at[rows, :], new_sem.at[step])

    def send_values(step, ahead):
        slab = val_all.at[rep, step]
        return pltpu.make_async_remote_copy(
            src_ref=slab, dst_ref=slab,
            send_sem=vsend_sem.at[step, ahead], recv_sem=vrecv_sem.at[step, ahead],
            device_id={"rep": lax.rem(rep + ahead, reps)}, device_id_type=pl.DeviceIdType.MESH)

    def take_values(step, behind):
        slab = val_all.at[lax.rem(rep + reps - behind, reps), step]
        return pltpu.make_async_remote_copy(
            src_ref=slab, dst_ref=slab,
            send_sem=vsend_sem.at[step, behind], recv_sem=vrecv_sem.at[step, behind],
            device_id={"rep": lax.rem(rep + behind, reps)}, device_id_type=pl.DeviceIdType.MESH)

    barrier = pltpu.get_barrier_semaphore()
    for target in (left, right, across, sibling):
        pl.semaphore_signal(barrier, inc=1, device_id=target, device_id_type=pl.DeviceIdType.MESH)
    for ahead in range(1, reps):
        pl.semaphore_signal(barrier, inc=1, device_id={"rep": lax.rem(rep + ahead, reps)}, device_id_type=pl.DeviceIdType.MESH)
    own_rows = rows_of(0, 0, share)
    own_copy = pltpu.make_async_copy(xt_ref, own_rows, own_sem)
    own_copy.start()
    small_copies = [pltpu.make_async_copy(small_hbm[n], small[n], small_sem.at[n]) for n in range(count)]
    for copy in small_copies:
        copy.start()
    g_copy = pltpu.make_async_copy(g_hbm, g, g_sem)
    g_copy.start()
    mom_copy(0).start()

    pl.semaphore_wait(barrier, 4 + reps - 1)

    own_low, own_high = xt_ref.at[pl.ds(0, half), :], xt_ref.at[pl.ds(half, half), :]
    first_pushes = [
        push(0, 0, 0, 0, half, right, own_low), push(1, 1, 0, half, half, left, own_high), push(2, 2, 0, 0, half, across, own_low),
        push(3, 3, 0, half, half, right, own_high), push(4, 4, 0, 0, half, left, own_low), push(5, 5, 0, half, half, across, own_high)]
    to_sibling(0, 0, own_low).start()
    to_sibling(0, 1, own_high).start()
    for copy in first_pushes:
        copy.start()
    for step in range(1, chips):
        mom_copy(step).start()

    small_copies[0].wait()
    small_copies[1].wait()
    blocks = picks_ref.shape[1]
    flat = jnp.zeros((HALF, chips * LANES), F32)
    for b in range(blocks):
        low_bits = (picks_ref[rep, b] & (LANES - 1)).astype(F32).astype(BF)
        flat = flat + dot(low_bits, select_ref[b])
    for part in range(chips):
        off_own[part] = flat[:, part * LANES:(part + 1) * LANES]
    own_copy.wait()
    g_copy.wait()
    for copy in small_copies[2:]:
        copy.wait()

    turned[...] = jnp.zeros_like(turned)

    def turn(r, carry):
        for first in range(0, blocks, QUAD):
            for place in range(min(QUAD, blocks - first)):
                turned[place * HALF:(place + 1) * HALF, :picks_ref.shape[3]] = (picks_ref[r, first + place] & (LANES - 1)).astype(F32)
            flipped[...] = turned[...].T
            for p in range(QUAD):
                lines = flipped[pl.ds(p, off_all.shape[2], stride=QUAD), :]
                for place in range(min(QUAD, blocks - first)):
                    off_all[r, first + place, :, p * HALF:(p + 1) * HALF] = lines[:, place * HALF:(place + 1) * HALF]
        return carry

    later_pushes = {
        6: push(6, 6, 1, 0, half, right), 7: push(7, 7, 2, half, half, left), 8: push(8, 8, 1, 0, half, across),
        9: push(9, 9, 3, half, half, right), 10: push(10, 10, 3, 0, half, left), 11: push(11, 11, 2, half, half, across),
        12: push(12, 12, 4, 0, half, across), 13: push(13, 13, 5, half, half, right)}

    def forward(step):
        chunk = chip_of(step)
        grad_chunk(xt, g, mom, off_own[chunk], rowf_ref, lanef_ref, exp_ref, comp_ref, moved, picked_high, picked_low,
                   val_all.at[rep, step], chunk)

    def backward(step):
        chunk = chip_of(step)
        back_chunk(off_own[chunk], rowi_ref, lanei_ref, exp_ref, moved, picked_high, picked_low, new, chunk)
        new_copy(step).start()

    def backward_step(step, carry):
        backward(step)
        return carry

    def one(step, carry):
        @pl.when(step == 1)
        def _():
            arrive(0, 1, 0, half)
            to_sibling(1, 0).start()
            arrive(1, 2, half, half)
            to_sibling(2, 1).start()
            arrive(2, 3, 0, half)
            to_sibling(3, 0).start()
            lax.fori_loop(0, reps, turn, 0)
            pltpu.make_async_copy(off_all, off_hbm, out_sem.at[0]).start()
            later_pushes[6].start()
            later_pushes[7].start()
            arrive(3, 1, half, half)
            to_sibling(1, 1).start()
            later_pushes[8].start()
            arrive(4, 2, 0, half)
            to_sibling(2, 0).start()
            later_pushes[10].start()
            arrive(5, 3, half, half)
            to_sibling(3, 1).start()
            later_pushes[9].start()
            later_pushes[11].start()
            backward(0)

        @pl.when(step == 3)
        def _():
            arrive(6, 4, 0, half)
            later_pushes[12].start()
            to_sibling(4, 0).start()
            arrive(7, 4, half, half)
            to_sibling(4, 1).start()

        @pl.when(step == 4)
        def _():
            arrive(8, 5, 0, half)
            to_sibling(5, 0).start()

        @pl.when(step == 5)
        def _():
            arrive(9, 5, half, half)
            later_pushes[13].start()
            to_sibling(5, 1).start()
            arrive(10, 6, 0, half)
            to_sibling(6, 0).start()
            arrive(11, 6, half, half)
            to_sibling(6, 1).start()
            lax.fori_loop(1, 3, backward_step, 0)

        @pl.when(step == 7)
        def _():
            arrive(12, 7, 0, half)
            to_sibling(7, 0).start()
            lax.fori_loop(3, 4, backward_step, 0)
            arrive(13, 7, half, half)
            to_sibling(7, 1).start()
            lax.fori_loop(4, 5, backward_step, 0)

        from_sibling(step, 0)
        from_sibling(step, 1)
        mom_copy(step).wait()
        forward(step)
        for ahead in range(1, reps):
            send_values(step, ahead).start()
        return carry

    lax.fori_loop(0, chips, one, 0)
    lax.fori_loop(5, chips, backward_step, 0)
    for copy in first_pushes + list(later_pushes.values()):
        copy.wait_send()

    def settle(step, carry):
        to_sibling(step, 0).wait_send()
        to_sibling(step, 1).wait_send()
        for behind in range(1, reps):
            take_values(step, behind).wait_recv()
        pltpu.make_async_copy(val_all.at[:, step], val_hbm.at[:, chip_of(step)], out_sem.at[1 + step]).start()
        return carry

    def finish(step, carry):
        for ahead in range(1, reps):
            send_values(step, ahead).wait_send()
        new_copy(step).wait()
        pltpu.make_async_copy(val_all.at[:, step], val_hbm.at[:, chip_of(step)], out_sem.at[1 + step]).wait()
        return carry

    lax.fori_loop(0, chips, settle, 0)
    lax.fori_loop(0, chips, finish, 0)
    pltpu.make_async_copy(off_all, off_hbm, out_sem.at[0]).wait()


def spread_offsets(off, exp_ref):
    off = jnp.where(own_slots((FIVE * HALF, LANES)), jnp.concatenate([off] * FIVE, axis=0), 0.0).astype(BF)
    return dot(off, exp_ref[...])


def grad_chunk(xt, g, mom, off, rowf_ref, lanef_ref, exp_ref, comp_ref, moved_ref, high_ref, low_ref, val_ref, chunk):
    rows = pl.ds(pl.multiple_of(chunk * CHUNK, CHUNK), CHUNK)
    half_rows = pl.ds(pl.multiple_of(chunk * (CHUNK // 2), CHUNK // 2), CHUNK // 2)
    moved = moved_ref.at[rows, :]
    moved[...] = dot(xt[rows, :], g[...]) * (1.0 / math.sqrt(ROWS)) + DECAY * mom[rows, :].astype(F32)
    offsets = spread_offsets(off, exp_ref)
    odd = offsets >= BLOCK
    picked_rows = []
    for p in range(FIVE):
        high, low = split(moved[p * BLOCK:(p + 1) * BLOCK, :])
        freq = dot(rowf_ref[...], jnp.concatenate([high, low, high], axis=0))
        cut = slice(p * HALF, (p + 1) * HALF)
        picked_rows.append(jnp.where(odd[cut], freq[HALF:], freq[:HALF]))
    high, low = split(jnp.concatenate(picked_rows, axis=0))
    spectrum = lane_transform(high, low, lanef_ref[...])
    column = jnp.where(odd, offsets - BLOCK, offsets)
    high, low = split(jnp.where(column == lane_in_block(offsets.shape), spectrum, 0.0))
    high_ref[half_rows, :] = high
    low_ref[half_rows, :] = low
    val_ref[:, :FIVE * HALF] = dot_t(comp_ref[...], high) + dot_t(comp_ref[...], low)


def back_chunk(off, rowi_ref, lanei_ref, exp_ref, moved_ref, high_ref, low_ref, new, chunk):
    base = pl.multiple_of(chunk * CHUNK, CHUNK)
    half_rows = pl.ds(pl.multiple_of(chunk * (CHUNK // 2), CHUNK // 2), CHUNK // 2)
    odd = spread_offsets(off, exp_ref) >= BLOCK
    spread = lane_transform(high_ref[half_rows, :], low_ref[half_rows, :], lanei_ref[...])
    for p in range(FIVE):
        cut = slice(p * HALF, (p + 1) * HALF)
        part = spread[cut]
        high, low = split(jnp.concatenate([jnp.where(odd[cut], 0.0, part), jnp.where(odd[cut], part, 0.0)], axis=0))
        taken = dot(rowi_ref[...], jnp.concatenate([high, low, high], axis=0))
        rows = pl.ds(base + p * BLOCK, BLOCK)
        new[rows, :] = (moved_ref[rows, :] - taken).astype(BF)


def update_kernel(val_hbm, off_hbm, col_hbm, spread_hbm, seg_hbm, new_in, up_hbm, new_out,
                  val_ref, off_ref, col_ref, spread_ref, seg_ref, new, up, vals, sums, half_ref,
                  small_sem, in_sem, keep_sem, up_sem):
    groups, blocks = off_ref.shape[:2]
    chips = val_ref.shape[1]
    steps = vals.shape[0]
    rows = QUAD * BLOCK
    smalls = [pltpu.make_async_copy(a, b, small_sem.at[n]) for n, (a, b) in enumerate((
        (val_hbm, val_ref), (off_hbm, off_ref), (seg_hbm, seg_ref), (col_hbm, col_ref), (spread_hbm, spread_ref)))]
    for copy in smalls:
        copy.start()

    def piece(ref, step):
        return ref.at[pl.ds(pl.multiple_of(step * rows, rows), rows), :]

    def bring(step):
        return pltpu.make_async_copy(piece(new_in, step), piece(new, step), in_sem.at[step])

    def keep(step):
        return pltpu.make_async_copy(piece(new, step), piece(new_out, step), keep_sem.at[step])

    def hand_out(step):
        return pltpu.make_async_copy(piece(up, step), piece(up_hbm, step), up_sem.at[step])

    smalls[0].wait()
    for r in range(groups):
        line = jnp.concatenate([val_ref[r, c][:, :FIVE * HALF] for c in range(chips)], axis=1)
        for i in range(steps):
            vals[i, r] = line[:, i * LANES:(i + 1) * LANES]
    for copy in smalls[1:]:
        copy.wait()

    def one(step, carry):
        bring(step).start()
        shape = (BLOCK // 8, 8, LANES)
        column = (lax.broadcasted_iota(jnp.int32, shape, 0) * 8 + lax.broadcasted_iota(jnp.int32, shape, 1)).astype(F32)
        powers = []
        for b in range(blocks):
            total = signed = jnp.zeros(shape, F32)
            for r in range(groups):
                off = jnp.broadcast_to(off_ref[r, b, pl.ds(step, 1), :], (8, LANES))
                val = jnp.broadcast_to(vals[step, r, b:b + 1, :], (8, LANES))
                odd = off >= BLOCK
                place = jnp.where(odd, off - BLOCK, off)[None] == column
                total = total + jnp.where(place, val[None], 0.0)
                signed = signed + jnp.where(place, jnp.where(odd, -val, val)[None], 0.0)
            sums[b, :, :LANES] = total.reshape(BLOCK, LANES)
            sums[b, :, LANES:] = signed.reshape(BLOCK, LANES)
            powers.append(jnp.sum(jnp.sum(total * total + signed * signed, axis=0), axis=0, keepdims=True))
        powers = jnp.concatenate(powers + [jnp.zeros((16 - blocks, LANES), F32)], axis=0)
        high, low = split(powers)
        power = dot(jnp.concatenate([high, low], axis=1), seg_ref[...])
        scale = lax.rsqrt(power * (0.5 / (BLOCK * BLOCK)) + EPSILON)
        for b in range(blocks):
            row = jnp.concatenate([scale[b:b + 1]] * 2, axis=1)
            high, low = split(sums[b] * row)
            half = dot(col_ref[...], jnp.concatenate([high, low, high], axis=0))
            high, low = split(half)
            half_ref[b * BLOCK:(b + 1) * BLOCK, :] = jnp.concatenate([high, low, high], axis=1)
        width = half_ref.shape[0]
        for start in range(0, width, 256):
            cut = slice(start, min(start + 256, width))
            field = dot_t(spread_ref[...], half_ref[cut])
            up[pl.ds(pl.multiple_of(step * rows, rows), rows), cut] = field.astype(BF)
        bring(step).wait()
        keep(step).start()
        hand_out(step).start()
        return carry

    lax.fori_loop(0, steps, one, 0)
    for step in range(steps):
        keep(step).wait()
        hand_out(step).wait()


def gather_call(xt, g, mom, picks, t):
    features, width = mom.shape
    reps = picks.shape[0]
    chunks = features // CHUNK
    values = (reps, chunks, LISTED, 2 * LANES)
    offsets = (reps, picks.shape[1], features // (QUAD * BLOCK), LANES)
    small = [picks] + [t[n] for n in NAMES]
    any_space = pl.BlockSpec(memory_space=pl.ANY)
    dma = pltpu.SemaphoreType.DMA
    return pl.pallas_call(
        gather_kernel,
        in_specs=[any_space] * (3 + len(small)),
        out_specs=[any_space] * 3,
        out_shape=[
            jax.ShapeDtypeStruct((features, width), BF),
            jax.ShapeDtypeStruct(values, F32),
            jax.ShapeDtypeStruct(offsets, F32),
        ],
        scratch_shapes=[pltpu.VMEM(a.shape, a.dtype) for a in small] + [
            pltpu.VMEM((features, ROWS), BF),
            pltpu.VMEM(g.shape, BF),
            pltpu.VMEM((features, width), BF),
            pltpu.VMEM((features, width), BF),
            pltpu.VMEM((features, width), F32),
            pltpu.VMEM((features // 2, width), BF),
            pltpu.VMEM((features // 2, width), BF),
            pltpu.VMEM((LANES, LANES), F32),
            pltpu.VMEM((LANES, LANES), F32),
            pltpu.VMEM((chunks, HALF, LANES), F32),
            pltpu.VMEM(offsets, F32),
            pltpu.VMEM(values, F32),
            dma((len(small),)), dma, dma((chunks,)), dma((chunks,)), dma((1 + chunks,)), dma, dma((14,)), dma((14,)), dma((chunks, 2)), dma((chunks, 2)), dma((chunks, reps)), dma((chunks, reps)),
        ],
        compiler_params=pltpu.CompilerParams(vmem_limit_bytes=56 * 2**20, collective_id=0, has_side_effects=True),
    )(xt, g, mom, *small)


def update_call(values, off, new, t):
    groups, blocks, steps = off.shape[:3]
    width = blocks * BLOCK
    small = [values, off] + [t[n] for n in ("columns", "spread", "segment")]
    any_space, dma = pl.BlockSpec(memory_space=pl.ANY), pltpu.SemaphoreType.DMA
    return pl.pallas_call(
        update_kernel,
        in_specs=[any_space] * (len(small) + 1),
        out_specs=[any_space] * 2,
        out_shape=[jax.ShapeDtypeStruct(new.shape, BF)] * 2,
        scratch_shapes=[pltpu.VMEM(a.shape, a.dtype) for a in small] + [
            pltpu.VMEM(new.shape, BF),
            pltpu.VMEM(new.shape, BF),
            pltpu.VMEM((steps, groups, LISTED, LANES), F32),
            pltpu.VMEM((blocks, BLOCK, 2 * LANES), F32),
            pltpu.VMEM((width, 6 * LANES), BF),
            dma((len(small),)), dma((steps,)), dma((steps,)), dma((steps,)),
        ],
        compiler_params=pltpu.CompilerParams(vmem_limit_bytes=60 * 2**20),
    )(*small, new)


def body(tokens, output_grads, momentum, component_picks):
    width = momentum.shape[2]
    t = {name: jnp.asarray(table) for name, table in tables(width, component_picks.shape[1]).items()}
    picks = jnp.transpose(component_picks, (0, 2, 3, 1))
    new_momentum, values, off = gather_call(tokens.T, output_grads, momentum[0], picks, t)
    update, new_momentum = update_call(values, off, new_momentum, t)
    return (new_momentum[None], update)


def solution(mesh):
    return jax.shard_map(
        body,
        mesh=mesh,
        in_specs=(P("rep", "tp"), P("rep", "tp"), P("rep", None, "tp"), P(None, None, "tp", None)),
        out_specs=(P("rep", None, "tp"), P(None, "tp")),
        check_vma=False,
    )
```

```python
import functools
import math

import jax
import jax.numpy as jnp
import ml_dtypes
import numpy as np
from jax import lax
from jax.experimental import pallas as pl
from jax.experimental.pallas import tpu as pltpu
from jax.sharding import PartitionSpec as P

ROWS = 1024
BLOCK = 64
HALF = 32
FIVE = 5
CHUNK = FIVE * BLOCK
LANES = 128
SLOT = 8
QUAD = 4
LISTED = 16
DECAY = 0.9
EPSILON = 1e-06
NAMES = ("select", "row_fwd", "row_inv", "lane_fwd", "lane_inv", "expand", "compress")
BF = jnp.bfloat16
F32 = jnp.float32


def split_table(table):
    high = table.astype(ml_dtypes.bfloat16)
    low = (table - high.astype(np.float64)).astype(ml_dtypes.bfloat16)
    return high, low


def tables(width, width_rows):
    frequency = np.arange(BLOCK, dtype=np.float64)[:, None]
    position = np.arange(BLOCK, dtype=np.float64)[None, :]
    norm = np.where(frequency == 0, math.sqrt(1.0 / BLOCK), math.sqrt(2.0 / BLOCK))
    cosine = norm * np.cos(math.pi * (2.0 * position + 1.0) * frequency / (2.0 * BLOCK))
    ordered = np.concatenate([cosine[0::2], cosine[1::2]])

    def rows_table(matrix):
        high, low = split_table(matrix)
        return np.concatenate([high, high, low], axis=1)

    def lanes_table(matrix):
        pair = np.zeros((LANES, LANES))
        pair[:BLOCK, :BLOCK] = matrix
        pair[BLOCK:, BLOCK:] = matrix
        high, low = split_table(pair)
        return np.concatenate(
            [np.concatenate([high, low], axis=1), np.concatenate([high, np.zeros_like(low)], axis=1)]
        )

    slot = np.arange(LANES)[:, None] // SLOT
    block = np.arange(width)[None, :] // BLOCK
    expand = (slot == block).astype(ml_dtypes.bfloat16)
    rows = width_rows
    select = np.zeros((width // BLOCK, rows, rows // FIVE * LANES), ml_dtypes.bfloat16)
    for b in range(width // BLOCK):
        for p in range(rows):
            select[b, p, p // FIVE * LANES + b * SLOT + p % FIVE] = 1.0
    high, low = split_table(cosine.T)
    columns = np.concatenate([high, high, low], axis=1)
    spread = np.zeros((QUAD, BLOCK, 2, QUAD, HALF))
    for p in range(QUAD):
        for parity in range(2):
            spread[p, :, parity, p, :] = 0.5 * (cosine[0::2] + (1 - 2 * parity) * cosine[1::2]).T
    high, low = split_table(spread.reshape(QUAD * BLOCK, 2 * QUAD * HALF))
    segment = (np.arange(LANES)[:, None] // HALF == np.arange(LANES)[None, :] // HALF).astype(ml_dtypes.bfloat16)
    return {
        "select": select,
        "row_fwd": rows_table(ordered),
        "row_inv": rows_table(ordered.T),
        "lane_fwd": lanes_table(cosine.T),
        "lane_inv": lanes_table(cosine),
        "expand": expand,
        "compress": (np.arange(LISTED)[:, None] == block).astype(ml_dtypes.bfloat16),
        "columns": columns,
        "spread": np.concatenate([high, high, low], axis=1),
        "segment": np.concatenate([segment, segment]),
    }


def dot(a, b):
    return jnp.dot(a, b, preferred_element_type=F32)


def dot_t(a, b):
    return lax.dot_general(a, b, (((1,), (1,)), ((), ())), preferred_element_type=F32)


def split(value):
    high = value.astype(BF)
    return high, (value - high.astype(F32)).astype(BF)


def lane_transform(high, low, weights):
    groups = high.shape[1] // LANES
    parts = []
    for group in range(groups):
        cut = slice(group * LANES, (group + 1) * LANES)
        both = dot(jnp.concatenate([high[:, cut], low[:, cut]], axis=1), weights)
        parts.append(both[:, :LANES] + both[:, LANES:])
    return jnp.concatenate(parts, axis=1)


def own_slots(shape):
    row = lax.broadcasted_iota(jnp.int32, shape, 0) // HALF
    lane = lax.broadcasted_iota(jnp.int32, shape, 1) % SLOT
    return lane == row


def lane_in_block(shape):
    return (lax.broadcasted_iota(jnp.int32, shape, 1) % BLOCK).astype(F32)


def gather_kernel(xt_ref, g_hbm, mom_hbm, *refs):
    count = len(NAMES) + 1
    small_hbm, refs = refs[:count], refs[count:]
    new_hbm, val_hbm, off_hbm = refs[:3]
    small, refs = refs[3:3 + count], refs[3 + count:]
    picks_ref, select_ref, rowf_ref, rowi_ref, lanef_ref, lanei_ref, exp_ref, comp_ref = small
    (xt, g, mom, new, moved, picked_high, picked_low, turned, flipped, off_own, off_all, val_all,
                  small_sem, g_sem, mom_sem, new_sem, out_sem, own_sem, send_sem, recv_sem, pass_sem, sib_sem, vsend_sem, vrecv_sem) = refs
    share = xt_ref.shape[0]
    chips = mom.shape[0] // CHUNK
    line = chips // 2
    reps = val_all.shape[0]
    rep, tp = lax.axis_index("rep"), lax.axis_index("tp")
    core, chip = lax.rem(tp, 2), lax.div(tp, 2)
    x, y = lax.rem(chip, line), lax.div(chip, line)

    def chip_at(dx, dy):
        return lax.rem(y + dy, 2) * line + lax.rem(x + dx, line)

    def device_at(dx, dy):
        return {"tp": chip_at(dx, dy) * 2 + core}

    left, right, across, sibling = device_at(line - 1, 0), device_at(1, 0), device_at(0, 1), {"tp": chip * 2 + 1 - core}

    def chip_of(step):
        dy = jnp.where((step == 3) | (step >= 5), 1, 0)
        dx = jnp.where((step == 1) | (step == 5), line - 1, jnp.where((step == 2) | (step == 6), 1, jnp.where((step == 4) | (step == 7), 2, 0)))
        return chip_at(dx, dy)

    def rows_of(step, first, count):
        start = (chip_of(step) * 2 + core) * share + first
        return xt.at[pl.ds(pl.multiple_of(start, 16), count), :]

    half = share // 2

    def push(index, recv, step, first, count, target, source=None):
        rows = rows_of(step, first, count)
        return pltpu.make_async_remote_copy(
            src_ref=rows if source is None else source, dst_ref=rows,
            send_sem=send_sem.at[index], recv_sem=recv_sem.at[recv],
            device_id=target, device_id_type=pl.DeviceIdType.MESH)

    def arrive(recv, step, first, count):
        push(0, recv, step, first, count, left).wait_recv()

    def to_sibling(step, part, source=None):
        rows = rows_of(step, part * half, half)
        return pltpu.make_async_remote_copy(
            src_ref=rows if source is None else source, dst_ref=rows,
            send_sem=pass_sem.at[step, part], recv_sem=sib_sem.at[step, part],
            device_id=sibling, device_id_type=pl.DeviceIdType.MESH)

    def from_sibling(step, part):
        start = (chip_of(step) * 2 + 1 - core) * share + part * half
        rows = xt.at[pl.ds(pl.multiple_of(start, 16), half), :]
        pltpu.make_async_remote_copy(
            src_ref=rows, dst_ref=rows, send_sem=pass_sem.at[step, part], recv_sem=sib_sem.at[step, part],
            device_id=sibling, device_id_type=pl.DeviceIdType.MESH).wait_recv()

    def mom_copy(step):
        rows = pl.ds(pl.multiple_of(chip_of(step) * CHUNK, CHUNK), CHUNK)
        return pltpu.make_async_copy(mom_hbm.at[rows, :], mom.at[rows, :], mom_sem.at[step])

    def new_copy(step):
        rows = pl.ds(pl.multiple_of(chip_of(step) * CHUNK, CHUNK), CHUNK)
        return pltpu.make_async_copy(new.at[rows, :], new_hbm.at[rows, :], new_sem.at[step])

    def send_values(step, ahead):
        slab = val_all.at[rep, step]
        return pltpu.make_async_remote_copy(
            src_ref=slab, dst_ref=slab,
            send_sem=vsend_sem.at[step, ahead], recv_sem=vrecv_sem.at[step, ahead],
            device_id={"rep": lax.rem(rep + ahead, reps)}, device_id_type=pl.DeviceIdType.MESH)

    def take_values(step, behind):
        slab = val_all.at[lax.rem(rep + reps - behind, reps), step]
        return pltpu.make_async_remote_copy(
            src_ref=slab, dst_ref=slab,
            send_sem=vsend_sem.at[step, behind], recv_sem=vrecv_sem.at[step, behind],
            device_id={"rep": lax.rem(rep + behind, reps)}, device_id_type=pl.DeviceIdType.MESH)

    barrier = pltpu.get_barrier_semaphore()
    for target in (left, right, across, sibling):
        pl.semaphore_signal(barrier, inc=1, device_id=target, device_id_type=pl.DeviceIdType.MESH)
    for ahead in range(1, reps):
        pl.semaphore_signal(barrier, inc=1, device_id={"rep": lax.rem(rep + ahead, reps)}, device_id_type=pl.DeviceIdType.MESH)
    own_rows = rows_of(0, 0, share)
    own_copy = pltpu.make_async_copy(xt_ref, own_rows, own_sem)
    own_copy.start()
    small_copies = [pltpu.make_async_copy(small_hbm[n], small[n], small_sem.at[n]) for n in range(count)]
    for copy in small_copies:
        copy.start()
    g_copy = pltpu.make_async_copy(g_hbm, g, g_sem)
    g_copy.start()
    mom_copy(0).start()

    pl.semaphore_wait(barrier, 4 + reps - 1)

    own_low, own_high = xt_ref.at[pl.ds(0, half), :], xt_ref.at[pl.ds(half, half), :]
    first_pushes = [
        push(0, 0, 0, 0, half, right, own_low), push(1, 1, 0, half, half, left, own_high), push(2, 2, 0, 0, half, across, own_low),
        push(3, 3, 0, half, half, right, own_high), push(4, 4, 0, 0, half, left, own_low), push(5, 5, 0, half, half, across, own_high)]
    to_sibling(0, 0, own_low).start()
    to_sibling(0, 1, own_high).start()
    for copy in first_pushes:
        copy.start()
    for step in range(1, chips):
        mom_copy(step).start()

    small_copies[0].wait()
    small_copies[1].wait()
    blocks = picks_ref.shape[1]
    flat = jnp.zeros((HALF, chips * LANES), F32)
    for b in range(blocks):
        low_bits = (picks_ref[rep, b] & (LANES - 1)).astype(F32).astype(BF)
        flat = flat + dot(low_bits, select_ref[b])
    for part in range(chips):
        off_own[part] = flat[:, part * LANES:(part + 1) * LANES]
    own_copy.wait()
    g_copy.wait()
    for copy in small_copies[2:]:
        copy.wait()

    turned[...] = jnp.zeros_like(turned)

    def turn(r, carry):
        for first in range(0, blocks, QUAD):
            for place in range(min(QUAD, blocks - first)):
                turned[place * HALF:(place + 1) * HALF, :picks_ref.shape[3]] = (picks_ref[r, first + place] & (LANES - 1)).astype(F32)
            flipped[...] = turned[...].T
            for p in range(QUAD):
                lines = flipped[pl.ds(p, off_all.shape[2], stride=QUAD), :]
                for place in range(min(QUAD, blocks - first)):
                    off_all[r, first + place, :, p * HALF:(p + 1) * HALF] = lines[:, place * HALF:(place + 1) * HALF]
        return carry

    later_pushes = {
        6: push(6, 6, 1, 0, half, right), 7: push(7, 7, 2, half, half, left), 8: push(8, 8, 1, 0, half, across),
        9: push(9, 9, 3, half, half, right), 10: push(10, 10, 3, 0, half, left), 11: push(11, 11, 2, half, half, across),
        12: push(12, 12, 4, 0, half, across), 13: push(13, 13, 5, half, half, right)}

    def forward(step):
        chunk = chip_of(step)
        grad_chunk(xt, g, mom, off_own[chunk], rowf_ref, lanef_ref, exp_ref, comp_ref, moved, picked_high, picked_low,
                   val_all.at[rep, step], chunk)

    def backward(step):
        chunk = chip_of(step)
        back_chunk(off_own[chunk], rowi_ref, lanei_ref, exp_ref, moved, picked_high, picked_low, new, chunk)
        new_copy(step).start()

    def backward_step(step, carry):
        backward(step)
        return carry

    def one(step, carry):
        @pl.when(step == 1)
        def _():
            arrive(0, 1, 0, half)
            later_pushes[6].start()
            to_sibling(1, 0).start()
            arrive(1, 2, half, half)
            later_pushes[7].start()
            to_sibling(2, 1).start()
            arrive(2, 3, 0, half)
            to_sibling(3, 0).start()
            lax.fori_loop(0, reps, turn, 0)
            pltpu.make_async_copy(off_all, off_hbm, out_sem.at[0]).start()
            backward(0)
            arrive(3, 1, half, half)
            to_sibling(1, 1).start()
            later_pushes[8].start()
            arrive(4, 2, 0, half)
            later_pushes[10].start()
            to_sibling(2, 0).start()
            arrive(5, 3, half, half)
            later_pushes[9].start()
            later_pushes[11].start()
            to_sibling(3, 1).start()

        @pl.when(step == 2)
        def _():
            arrive(6, 4, 0, half)
            later_pushes[12].start()
            to_sibling(4, 0).start()
            arrive(7, 4, half, half)
            to_sibling(4, 1).start()

        @pl.when(step == 4)
        def _():
            arrive(8, 5, 0, half)
            to_sibling(5, 0).start()
            arrive(9, 5, half, half)
            later_pushes[13].start()
            to_sibling(5, 1).start()

        @pl.when(step == 5)
        def _():
            arrive(10, 6, 0, half)
            to_sibling(6, 0).start()
            arrive(11, 6, half, half)
            to_sibling(6, 1).start()

        @pl.when(step == 7)
        def _():
            arrive(12, 7, 0, half)
            to_sibling(7, 0).start()
            lax.fori_loop(1, 3, backward_step, 0)
            arrive(13, 7, half, half)
            to_sibling(7, 1).start()
            lax.fori_loop(3, 4, backward_step, 0)

        from_sibling(step, 0)
        from_sibling(step, 1)
        mom_copy(step).wait()
        forward(step)
        for ahead in range(1, reps):
            send_values(step, ahead).start()
        return carry

    lax.fori_loop(0, chips, one, 0)
    lax.fori_loop(4, chips, backward_step, 0)
    for copy in first_pushes + list(later_pushes.values()):
        copy.wait_send()

    def settle(step, carry):
        to_sibling(step, 0).wait_send()
        to_sibling(step, 1).wait_send()
        for behind in range(1, reps):
            take_values(step, behind).wait_recv()
        pltpu.make_async_copy(val_all.at[:, step], val_hbm.at[:, chip_of(step)], out_sem.at[1 + step]).start()
        return carry

    def finish(step, carry):
        for ahead in range(1, reps):
            send_values(step, ahead).wait_send()
        new_copy(step).wait()
        pltpu.make_async_copy(val_all.at[:, step], val_hbm.at[:, chip_of(step)], out_sem.at[1 + step]).wait()
        return carry

    lax.fori_loop(0, chips, settle, 0)
    lax.fori_loop(0, chips, finish, 0)
    pltpu.make_async_copy(off_all, off_hbm, out_sem.at[0]).wait()


def spread_offsets(off, exp_ref):
    off = jnp.where(own_slots((FIVE * HALF, LANES)), jnp.concatenate([off] * FIVE, axis=0), 0.0).astype(BF)
    return dot(off, exp_ref[...])


def grad_chunk(xt, g, mom, off, rowf_ref, lanef_ref, exp_ref, comp_ref, moved_ref, high_ref, low_ref, val_ref, chunk):
    rows = pl.ds(pl.multiple_of(chunk * CHUNK, CHUNK), CHUNK)
    half_rows = pl.ds(pl.multiple_of(chunk * (CHUNK // 2), CHUNK // 2), CHUNK // 2)
    moved = moved_ref.at[rows, :]
    moved[...] = dot(xt[rows, :], g[...]) * (1.0 / math.sqrt(ROWS)) + DECAY * mom[rows, :].astype(F32)
    offsets = spread_offsets(off, exp_ref)
    odd = offsets >= BLOCK
    picked_rows = []
    for p in range(FIVE):
        high, low = split(moved[p * BLOCK:(p + 1) * BLOCK, :])
        freq = dot(rowf_ref[...], jnp.concatenate([high, low, high], axis=0))
        cut = slice(p * HALF, (p + 1) * HALF)
        picked_rows.append(jnp.where(odd[cut], freq[HALF:], freq[:HALF]))
    high, low = split(jnp.concatenate(picked_rows, axis=0))
    spectrum = lane_transform(high, low, lanef_ref[...])
    column = jnp.where(odd, offsets - BLOCK, offsets)
    high, low = split(jnp.where(column == lane_in_block(offsets.shape), spectrum, 0.0))
    high_ref[half_rows, :] = high
    low_ref[half_rows, :] = low
    val_ref[:, :FIVE * HALF] = dot_t(comp_ref[...], high) + dot_t(comp_ref[...], low)


def back_chunk(off, rowi_ref, lanei_ref, exp_ref, moved_ref, high_ref, low_ref, new, chunk):
    base = pl.multiple_of(chunk * CHUNK, CHUNK)
    half_rows = pl.ds(pl.multiple_of(chunk * (CHUNK // 2), CHUNK // 2), CHUNK // 2)
    odd = spread_offsets(off, exp_ref) >= BLOCK
    spread = lane_transform(high_ref[half_rows, :], low_ref[half_rows, :], lanei_ref[...])
    for p in range(FIVE):
        cut = slice(p * HALF, (p + 1) * HALF)
        part = spread[cut]
        high, low = split(jnp.concatenate([jnp.where(odd[cut], 0.0, part), jnp.where(odd[cut], part, 0.0)], axis=0))
        taken = dot(rowi_ref[...], jnp.concatenate([high, low, high], axis=0))
        rows = pl.ds(base + p * BLOCK, BLOCK)
        new[rows, :] = (moved_ref[rows, :] - taken).astype(BF)


def update_kernel(val_hbm, off_hbm, col_hbm, spread_hbm, seg_hbm, new_in, up_hbm, new_out,
                  val_ref, off_ref, col_ref, spread_ref, seg_ref, new, up, vals, sums, half_ref,
                  small_sem, in_sem, keep_sem, up_sem):
    groups, blocks = off_ref.shape[:2]
    chips = val_ref.shape[1]
    steps = vals.shape[0]
    rows = QUAD * BLOCK
    smalls = [pltpu.make_async_copy(a, b, small_sem.at[n]) for n, (a, b) in enumerate((
        (val_hbm, val_ref), (off_hbm, off_ref), (seg_hbm, seg_ref), (col_hbm, col_ref), (spread_hbm, spread_ref)))]
    for copy in smalls:
        copy.start()

    def piece(ref, step):
        return ref.at[pl.ds(pl.multiple_of(step * rows, rows), rows), :]

    def bring(step):
        return pltpu.make_async_copy(piece(new_in, step), piece(new, step), in_sem.at[step])

    def keep(step):
        return pltpu.make_async_copy(piece(new, step), piece(new_out, step), keep_sem.at[step])

    def hand_out(step):
        return pltpu.make_async_copy(piece(up, step), piece(up_hbm, step), up_sem.at[step])

    smalls[0].wait()
    for r in range(groups):
        line = jnp.concatenate([val_ref[r, c][:, :FIVE * HALF] for c in range(chips)], axis=1)
        for i in range(steps):
            vals[i, r] = line[:, i * LANES:(i + 1) * LANES]
    for copy in smalls[1:]:
        copy.wait()

    def one(step, carry):
        bring(step).start()
        shape = (BLOCK // 8, 8, LANES)
        column = (lax.broadcasted_iota(jnp.int32, shape, 0) * 8 + lax.broadcasted_iota(jnp.int32, shape, 1)).astype(F32)
        powers = []
        for b in range(blocks):
            total = signed = jnp.zeros(shape, F32)
            for r in range(groups):
                off = jnp.broadcast_to(off_ref[r, b, pl.ds(step, 1), :], (8, LANES))
                val = jnp.broadcast_to(vals[step, r, b:b + 1, :], (8, LANES))
                odd = off >= BLOCK
                place = jnp.where(odd, off - BLOCK, off)[None] == column
                total = total + jnp.where(place, val[None], 0.0)
                signed = signed + jnp.where(place, jnp.where(odd, -val, val)[None], 0.0)
            sums[b, :, :LANES] = total.reshape(BLOCK, LANES)
            sums[b, :, LANES:] = signed.reshape(BLOCK, LANES)
            powers.append(jnp.sum(jnp.sum(total * total + signed * signed, axis=0), axis=0, keepdims=True))
        powers = jnp.concatenate(powers + [jnp.zeros((16 - blocks, LANES), F32)], axis=0)
        high, low = split(powers)
        power = dot(jnp.concatenate([high, low], axis=1), seg_ref[...])
        scale = lax.rsqrt(power * (0.5 / (BLOCK * BLOCK)) + EPSILON)
        for b in range(blocks):
            row = jnp.concatenate([scale[b:b + 1]] * 2, axis=1)
            high, low = split(sums[b] * row)
            half = dot(col_ref[...], jnp.concatenate([high, low, high], axis=0))
            high, low = split(half)
            half_ref[b * BLOCK:(b + 1) * BLOCK, :] = jnp.concatenate([high, low, high], axis=1)
        width = half_ref.shape[0]
        for start in range(0, width, 256):
            cut = slice(start, min(start + 256, width))
            field = dot_t(spread_ref[...], half_ref[cut])
            up[pl.ds(pl.multiple_of(step * rows, rows), rows), cut] = field.astype(BF)
        bring(step).wait()
        keep(step).start()
        hand_out(step).start()
        return carry

    lax.fori_loop(0, steps, one, 0)
    for step in range(steps):
        keep(step).wait()
        hand_out(step).wait()


def gather_call(xt, g, mom, picks, t):
    features, width = mom.shape
    reps = picks.shape[0]
    chunks = features // CHUNK
    values = (reps, chunks, LISTED, 2 * LANES)
    offsets = (reps, picks.shape[1], features // (QUAD * BLOCK), LANES)
    small = [picks] + [t[n] for n in NAMES]
    any_space = pl.BlockSpec(memory_space=pl.ANY)
    dma = pltpu.SemaphoreType.DMA
    return pl.pallas_call(
        gather_kernel,
        in_specs=[any_space] * (3 + len(small)),
        out_specs=[any_space] * 3,
        out_shape=[
            jax.ShapeDtypeStruct((features, width), BF),
            jax.ShapeDtypeStruct(values, F32),
            jax.ShapeDtypeStruct(offsets, F32),
        ],
        scratch_shapes=[pltpu.VMEM(a.shape, a.dtype) for a in small] + [
            pltpu.VMEM((features, ROWS), BF),
            pltpu.VMEM(g.shape, BF),
            pltpu.VMEM((features, width), BF),
            pltpu.VMEM((features, width), BF),
            pltpu.VMEM((features, width), F32),
            pltpu.VMEM((features // 2, width), BF),
            pltpu.VMEM((features // 2, width), BF),
            pltpu.VMEM((LANES, LANES), F32),
            pltpu.VMEM((LANES, LANES), F32),
            pltpu.VMEM((chunks, HALF, LANES), F32),
            pltpu.VMEM(offsets, F32),
            pltpu.VMEM(values, F32),
            dma((len(small),)), dma, dma((chunks,)), dma((chunks,)), dma((1 + chunks,)), dma, dma((14,)), dma((14,)), dma((chunks, 2)), dma((chunks, 2)), dma((chunks, reps)), dma((chunks, reps)),
        ],
        compiler_params=pltpu.CompilerParams(vmem_limit_bytes=56 * 2**20, collective_id=0, has_side_effects=True),
    )(xt, g, mom, *small)


def update_call(values, off, new, t):
    groups, blocks, steps = off.shape[:3]
    width = blocks * BLOCK
    small = [values, off] + [t[n] for n in ("columns", "spread", "segment")]
    any_space, dma = pl.BlockSpec(memory_space=pl.ANY), pltpu.SemaphoreType.DMA
    return pl.pallas_call(
        update_kernel,
        in_specs=[any_space] * (len(small) + 1),
        out_specs=[any_space] * 2,
        out_shape=[jax.ShapeDtypeStruct(new.shape, BF)] * 2,
        scratch_shapes=[pltpu.VMEM(a.shape, a.dtype) for a in small] + [
            pltpu.VMEM(new.shape, BF),
            pltpu.VMEM(new.shape, BF),
            pltpu.VMEM((steps, groups, LISTED, LANES), F32),
            pltpu.VMEM((blocks, BLOCK, 2 * LANES), F32),
            pltpu.VMEM((width, 6 * LANES), BF),
            dma((len(small),)), dma((steps,)), dma((steps,)), dma((steps,)),
        ],
        compiler_params=pltpu.CompilerParams(vmem_limit_bytes=60 * 2**20),
    )(*small, new)


def body(tokens, output_grads, momentum, component_picks):
    width = momentum.shape[2]
    t = {name: jnp.asarray(table) for name, table in tables(width, component_picks.shape[1]).items()}
    picks = jnp.transpose(component_picks, (0, 2, 3, 1))
    new_momentum, values, off = gather_call(tokens.T, output_grads, momentum[0], picks, t)
    update, new_momentum = update_call(values, off, new_momentum, t)
    return (new_momentum[None], update)


def solution(mesh):
    return jax.shard_map(
        body,
        mesh=mesh,
        in_specs=(P("rep", "tp"), P("rep", "tp"), P("rep", None, "tp"), P(None, None, "tp", None)),
        out_specs=(P("rep", None, "tp"), P(None, "tp")),
        check_vma=False,
    )
```

```python
import functools
import math

import jax
import jax.numpy as jnp
import ml_dtypes
import numpy as np
from jax import lax
from jax.experimental import pallas as pl
from jax.experimental.pallas import tpu as pltpu
from jax.sharding import PartitionSpec as P

ROWS = 1024
BLOCK = 64
HALF = 32
FIVE = 5
CHUNK = FIVE * BLOCK
LANES = 128
SLOT = 8
QUAD = 4
LISTED = 16
DECAY = 0.9
EPSILON = 1e-06
NAMES = ("select", "row_fwd", "row_inv", "lane_fwd", "lane_inv", "expand", "compress")
BF = jnp.bfloat16
F32 = jnp.float32


def split_table(table):
    high = table.astype(ml_dtypes.bfloat16)
    low = (table - high.astype(np.float64)).astype(ml_dtypes.bfloat16)
    return high, low


def tables(width, width_rows):
    frequency = np.arange(BLOCK, dtype=np.float64)[:, None]
    position = np.arange(BLOCK, dtype=np.float64)[None, :]
    norm = np.where(frequency == 0, math.sqrt(1.0 / BLOCK), math.sqrt(2.0 / BLOCK))
    cosine = norm * np.cos(math.pi * (2.0 * position + 1.0) * frequency / (2.0 * BLOCK))
    ordered = np.concatenate([cosine[0::2], cosine[1::2]])

    def rows_table(matrix):
        high, low = split_table(matrix)
        return np.concatenate([high, high, low], axis=1)

    def lanes_table(matrix):
        pair = np.zeros((LANES, LANES))
        pair[:BLOCK, :BLOCK] = matrix
        pair[BLOCK:, BLOCK:] = matrix
        high, low = split_table(pair)
        return np.concatenate(
            [np.concatenate([high, low], axis=1), np.concatenate([high, np.zeros_like(low)], axis=1)]
        )

    slot = np.arange(LANES)[:, None] // SLOT
    block = np.arange(width)[None, :] // BLOCK
    expand = (slot == block).astype(ml_dtypes.bfloat16)
    rows = width_rows
    select = np.zeros((width // BLOCK, rows, rows // FIVE * LANES), ml_dtypes.bfloat16)
    for b in range(width // BLOCK):
        for p in range(rows):
            select[b, p, p // FIVE * LANES + b * SLOT + p % FIVE] = 1.0
    high, low = split_table(cosine.T)
    columns = np.concatenate([high, high, low], axis=1)
    spread = np.zeros((QUAD, BLOCK, 2, QUAD, HALF))
    for p in range(QUAD):
        for parity in range(2):
            spread[p, :, parity, p, :] = 0.5 * (cosine[0::2] + (1 - 2 * parity) * cosine[1::2]).T
    high, low = split_table(spread.reshape(QUAD * BLOCK, 2 * QUAD * HALF))
    segment = (np.arange(LANES)[:, None] // HALF == np.arange(LANES)[None, :] // HALF).astype(ml_dtypes.bfloat16)
    return {
        "select": select,
        "row_fwd": rows_table(ordered),
        "row_inv": rows_table(ordered.T),
        "lane_fwd": lanes_table(cosine.T),
        "lane_inv": lanes_table(cosine),
        "expand": expand,
        "compress": (np.arange(LISTED)[:, None] == block).astype(ml_dtypes.bfloat16),
        "columns": columns,
        "spread": np.concatenate([high, high, low], axis=1),
        "segment": np.concatenate([segment, segment]),
    }


def dot(a, b):
    return jnp.dot(a, b, preferred_element_type=F32)


def dot_t(a, b):
    return lax.dot_general(a, b, (((1,), (1,)), ((), ())), preferred_element_type=F32)


def split(value):
    high = value.astype(BF)
    return high, (value - high.astype(F32)).astype(BF)


def lane_transform(high, low, weights):
    groups = high.shape[1] // LANES
    parts = []
    for group in range(groups):
        cut = slice(group * LANES, (group + 1) * LANES)
        both = dot(jnp.concatenate([high[:, cut], low[:, cut]], axis=1), weights)
        parts.append(both[:, :LANES] + both[:, LANES:])
    return jnp.concatenate(parts, axis=1)


def own_slots(shape):
    row = lax.broadcasted_iota(jnp.int32, shape, 0) // HALF
    lane = lax.broadcasted_iota(jnp.int32, shape, 1) % SLOT
    return lane == row


def lane_in_block(shape):
    return (lax.broadcasted_iota(jnp.int32, shape, 1) % BLOCK).astype(F32)


def gather_kernel(xt_ref, g_hbm, mom_hbm, *refs):
    count = len(NAMES) + 1
    small_hbm, refs = refs[:count], refs[count:]
    new_hbm, val_hbm, off_hbm = refs[:3]
    small, refs = refs[3:3 + count], refs[3 + count:]
    picks_ref, select_ref, rowf_ref, rowi_ref, lanef_ref, lanei_ref, exp_ref, comp_ref = small
    (xt, g, mom, new, moved, picked_high, picked_low, turned, flipped, off_own, off_all, val_all,
                  small_sem, g_sem, mom_sem, new_sem, out_sem, own_sem, send_sem, recv_sem, pass_sem, sib_sem, vsend_sem, vrecv_sem) = refs
    share = xt_ref.shape[0]
    chips = mom.shape[0] // CHUNK
    line = chips // 2
    reps = val_all.shape[0]
    rep, tp = lax.axis_index("rep"), lax.axis_index("tp")
    core, chip = lax.rem(tp, 2), lax.div(tp, 2)
    x, y = lax.rem(chip, line), lax.div(chip, line)

    def chip_at(dx, dy):
        return lax.rem(y + dy, 2) * line + lax.rem(x + dx, line)

    def device_at(dx, dy):
        return {"tp": chip_at(dx, dy) * 2 + core}

    left, right, across, sibling = device_at(line - 1, 0), device_at(1, 0), device_at(0, 1), {"tp": chip * 2 + 1 - core}

    def chip_of(step):
        dy = jnp.where((step == 3) | (step >= 5), 1, 0)
        dx = jnp.where((step == 1) | (step == 5), line - 1, jnp.where((step == 2) | (step == 6), 1, jnp.where((step == 4) | (step == 7), 2, 0)))
        return chip_at(dx, dy)

    def rows_of(step, first, count):
        start = (chip_of(step) * 2 + core) * share + first
        return xt.at[pl.ds(pl.multiple_of(start, 16), count), :]

    half = share // 2

    def push(index, recv, step, first, count, target, source=None):
        rows = rows_of(step, first, count)
        return pltpu.make_async_remote_copy(
            src_ref=rows if source is None else source, dst_ref=rows,
            send_sem=send_sem.at[index], recv_sem=recv_sem.at[recv],
            device_id=target, device_id_type=pl.DeviceIdType.MESH)

    def arrive(recv, step, first, count):
        push(0, recv, step, first, count, left).wait_recv()

    def to_sibling(step, part, source=None):
        rows = rows_of(step, part * half, half)
        return pltpu.make_async_remote_copy(
            src_ref=rows if source is None else source, dst_ref=rows,
            send_sem=pass_sem.at[step, part], recv_sem=sib_sem.at[step, part],
            device_id=sibling, device_id_type=pl.DeviceIdType.MESH)

    def from_sibling(step, part):
        start = (chip_of(step) * 2 + 1 - core) * share + part * half
        rows = xt.at[pl.ds(pl.multiple_of(start, 16), half), :]
        pltpu.make_async_remote_copy(
            src_ref=rows, dst_ref=rows, send_sem=pass_sem.at[step, part], recv_sem=sib_sem.at[step, part],
            device_id=sibling, device_id_type=pl.DeviceIdType.MESH).wait_recv()

    def mom_copy(step):
        rows = pl.ds(pl.multiple_of(chip_of(step) * CHUNK, CHUNK), CHUNK)
        return pltpu.make_async_copy(mom_hbm.at[rows, :], mom.at[rows, :], mom_sem.at[step])

    def new_copy(step):
        rows = pl.ds(pl.multiple_of(chip_of(step) * CHUNK, CHUNK), CHUNK)
        return pltpu.make_async_copy(new.at[rows, :], new_hbm.at[rows, :], new_sem.at[step])

    def send_values(step, ahead):
        slab = val_all.at[rep, step]
        return pltpu.make_async_remote_copy(
            src_ref=slab, dst_ref=slab,
            send_sem=vsend_sem.at[step, ahead], recv_sem=vrecv_sem.at[step, ahead],
            device_id={"rep": lax.rem(rep + ahead, reps)}, device_id_type=pl.DeviceIdType.MESH)

    def take_values(step, behind):
        slab = val_all.at[lax.rem(rep + reps - behind, reps), step]
        return pltpu.make_async_remote_copy(
            src_ref=slab, dst_ref=slab,
            send_sem=vsend_sem.at[step, behind], recv_sem=vrecv_sem.at[step, behind],
            device_id={"rep": lax.rem(rep + behind, reps)}, device_id_type=pl.DeviceIdType.MESH)

    barrier = pltpu.get_barrier_semaphore()
    for target in (left, right, across, sibling):
        pl.semaphore_signal(barrier, inc=1, device_id=target, device_id_type=pl.DeviceIdType.MESH)
    for ahead in range(1, reps):
        pl.semaphore_signal(barrier, inc=1, device_id={"rep": lax.rem(rep + ahead, reps)}, device_id_type=pl.DeviceIdType.MESH)
    own_rows = rows_of(0, 0, share)
    own_copy = pltpu.make_async_copy(xt_ref, own_rows, own_sem)
    own_copy.start()
    small_copies = [pltpu.make_async_copy(small_hbm[n], small[n], small_sem.at[n]) for n in range(count)]
    for copy in small_copies:
        copy.start()
    g_copy = pltpu.make_async_copy(g_hbm, g, g_sem)
    g_copy.start()
    mom_copy(0).start()

    pl.semaphore_wait(barrier, 4 + reps - 1)

    own_low, own_high = xt_ref.at[pl.ds(0, half), :], xt_ref.at[pl.ds(half, half), :]
    first_pushes = [
        push(0, 0, 0, 0, half, right, own_low), push(1, 1, 0, half, half, left, own_high), push(2, 2, 0, 0, half, across, own_low),
        push(3, 3, 0, half, half, right, own_high), push(4, 4, 0, 0, half, left, own_low), push(5, 5, 0, half, half, across, own_high)]
    to_sibling(0, 0, own_low).start()
    to_sibling(0, 1, own_high).start()
    for copy in first_pushes:
        copy.start()
    for step in range(1, chips):
        mom_copy(step).start()

    small_copies[0].wait()
    small_copies[1].wait()
    blocks = picks_ref.shape[1]
    flat = jnp.zeros((HALF, chips * LANES), F32)
    for b in range(blocks):
        low_bits = (picks_ref[rep, b] & (LANES - 1)).astype(F32).astype(BF)
        flat = flat + dot(low_bits, select_ref[b])
    for part in range(chips):
        off_own[part] = flat[:, part * LANES:(part + 1) * LANES]
    own_copy.wait()
    g_copy.wait()
    for copy in small_copies[2:]:
        copy.wait()

    turned[...] = jnp.zeros_like(turned)

    def turn(r, carry):
        for first in range(0, blocks, QUAD):
            for place in range(min(QUAD, blocks - first)):
                turned[place * HALF:(place + 1) * HALF, :picks_ref.shape[3]] = (picks_ref[r, first + place] & (LANES - 1)).astype(F32)
            flipped[...] = turned[...].T
            for p in range(QUAD):
                lines = flipped[pl.ds(p, off_all.shape[2], stride=QUAD), :]
                for place in range(min(QUAD, blocks - first)):
                    off_all[r, first + place, :, p * HALF:(p + 1) * HALF] = lines[:, place * HALF:(place + 1) * HALF]
        return carry

    later_pushes = {
        6: push(6, 6, 1, 0, half, right), 7: push(7, 7, 2, half, half, left), 8: push(8, 8, 1, 0, half, across),
        9: push(9, 9, 3, half, half, right), 10: push(10, 10, 3, 0, half, left), 11: push(11, 11, 2, half, half, across),
        12: push(12, 12, 4, 0, half, across), 13: push(13, 13, 5, half, half, right)}

    def forward(step):
        chunk = chip_of(step)
        grad_chunk(xt, g, mom, off_own[chunk], rowf_ref, lanef_ref, exp_ref, comp_ref, moved, picked_high, picked_low,
                   val_all.at[rep, step], chunk)

    def backward(step):
        chunk = chip_of(step)
        back_chunk(off_own[chunk], rowi_ref, lanei_ref, exp_ref, moved, picked_high, picked_low, new, chunk)
        new_copy(step).start()

    def backward_step(step, carry):
        backward(step)
        return carry

    def one(step, carry):
        @pl.when(step == 1)
        def _():
            lax.fori_loop(0, reps, turn, 0)
            pltpu.make_async_copy(off_all, off_hbm, out_sem.at[0]).start()
            arrive(0, 1, 0, half)
            later_pushes[6].start()
            to_sibling(1, 0).start()
            arrive(1, 2, half, half)
            later_pushes[7].start()
            to_sibling(2, 1).start()
            arrive(2, 3, 0, half)
            to_sibling(3, 0).start()
            arrive(3, 1, half, half)
            to_sibling(1, 1).start()
            later_pushes[8].start()
            arrive(4, 2, 0, half)
            later_pushes[10].start()
            to_sibling(2, 0).start()
            arrive(5, 3, half, half)
            later_pushes[9].start()
            later_pushes[11].start()
            to_sibling(3, 1).start()

        @pl.when(step == 2)
        def _():
            arrive(6, 4, 0, half)
            later_pushes[12].start()
            to_sibling(4, 0).start()
            arrive(7, 4, half, half)
            to_sibling(4, 1).start()

        @pl.when(step == 4)
        def _():
            arrive(8, 5, 0, half)
            to_sibling(5, 0).start()
            arrive(9, 5, half, half)
            later_pushes[13].start()
            to_sibling(5, 1).start()

        @pl.when(step == 5)
        def _():
            arrive(10, 6, 0, half)
            to_sibling(6, 0).start()
            arrive(11, 6, half, half)
            to_sibling(6, 1).start()

        @pl.when(step == 7)
        def _():
            arrive(12, 7, 0, half)
            to_sibling(7, 0).start()
            lax.fori_loop(0, 3, backward_step, 0)
            arrive(13, 7, half, half)
            to_sibling(7, 1).start()
            lax.fori_loop(3, 4, backward_step, 0)

        from_sibling(step, 0)
        from_sibling(step, 1)
        mom_copy(step).wait()
        forward(step)
        for ahead in range(1, reps):
            send_values(step, ahead).start()
        return carry

    lax.fori_loop(0, chips, one, 0)
    lax.fori_loop(4, chips, backward_step, 0)
    for copy in first_pushes + list(later_pushes.values()):
        copy.wait_send()

    def settle(step, carry):
        to_sibling(step, 0).wait_send()
        to_sibling(step, 1).wait_send()
        for behind in range(1, reps):
            take_values(step, behind).wait_recv()
        pltpu.make_async_copy(val_all.at[:, step], val_hbm.at[:, chip_of(step)], out_sem.at[1 + step]).start()
        return carry

    def finish(step, carry):
        for ahead in range(1, reps):
            send_values(step, ahead).wait_send()
        new_copy(step).wait()
        pltpu.make_async_copy(val_all.at[:, step], val_hbm.at[:, chip_of(step)], out_sem.at[1 + step]).wait()
        return carry

    lax.fori_loop(0, chips, settle, 0)
    lax.fori_loop(0, chips, finish, 0)
    pltpu.make_async_copy(off_all, off_hbm, out_sem.at[0]).wait()


def spread_offsets(off, exp_ref):
    off = jnp.where(own_slots((FIVE * HALF, LANES)), jnp.concatenate([off] * FIVE, axis=0), 0.0).astype(BF)
    return dot(off, exp_ref[...])


def grad_chunk(xt, g, mom, off, rowf_ref, lanef_ref, exp_ref, comp_ref, moved_ref, high_ref, low_ref, val_ref, chunk):
    rows = pl.ds(pl.multiple_of(chunk * CHUNK, CHUNK), CHUNK)
    half_rows = pl.ds(pl.multiple_of(chunk * (CHUNK // 2), CHUNK // 2), CHUNK // 2)
    moved = moved_ref.at[rows, :]
    moved[...] = dot(xt[rows, :], g[...]) * (1.0 / math.sqrt(ROWS)) + DECAY * mom[rows, :].astype(F32)
    offsets = spread_offsets(off, exp_ref)
    odd = offsets >= BLOCK
    picked_rows = []
    for p in range(FIVE):
        high, low = split(moved[p * BLOCK:(p + 1) * BLOCK, :])
        freq = dot(rowf_ref[...], jnp.concatenate([high, low, high], axis=0))
        cut = slice(p * HALF, (p + 1) * HALF)
        picked_rows.append(jnp.where(odd[cut], freq[HALF:], freq[:HALF]))
    high, low = split(jnp.concatenate(picked_rows, axis=0))
    spectrum = lane_transform(high, low, lanef_ref[...])
    column = jnp.where(odd, offsets - BLOCK, offsets)
    high, low = split(jnp.where(column == lane_in_block(offsets.shape), spectrum, 0.0))
    high_ref[half_rows, :] = high
    low_ref[half_rows, :] = low
    val_ref[:, :FIVE * HALF] = dot_t(comp_ref[...], high) + dot_t(comp_ref[...], low)


def back_chunk(off, rowi_ref, lanei_ref, exp_ref, moved_ref, high_ref, low_ref, new, chunk):
    base = pl.multiple_of(chunk * CHUNK, CHUNK)
    half_rows = pl.ds(pl.multiple_of(chunk * (CHUNK // 2), CHUNK // 2), CHUNK // 2)
    odd = spread_offsets(off, exp_ref) >= BLOCK
    spread = lane_transform(high_ref[half_rows, :], low_ref[half_rows, :], lanei_ref[...])
    for p in range(FIVE):
        cut = slice(p * HALF, (p + 1) * HALF)
        part = spread[cut]
        high, low = split(jnp.concatenate([jnp.where(odd[cut], 0.0, part), jnp.where(odd[cut], part, 0.0)], axis=0))
        taken = dot(rowi_ref[...], jnp.concatenate([high, low, high], axis=0))
        rows = pl.ds(base + p * BLOCK, BLOCK)
        new[rows, :] = (moved_ref[rows, :] - taken).astype(BF)


def update_kernel(val_hbm, off_hbm, col_hbm, spread_hbm, seg_hbm, new_in, up_hbm, new_out,
                  val_ref, off_ref, col_ref, spread_ref, seg_ref, new, up, vals, sums, half_ref,
                  small_sem, in_sem, keep_sem, up_sem):
    groups, blocks = off_ref.shape[:2]
    chips = val_ref.shape[1]
    steps = vals.shape[0]
    rows = QUAD * BLOCK
    smalls = [pltpu.make_async_copy(a, b, small_sem.at[n]) for n, (a, b) in enumerate((
        (val_hbm, val_ref), (off_hbm, off_ref), (seg_hbm, seg_ref), (col_hbm, col_ref), (spread_hbm, spread_ref)))]
    for copy in smalls:
        copy.start()

    def piece(ref, step):
        return ref.at[pl.ds(pl.multiple_of(step * rows, rows), rows), :]

    def bring(step):
        return pltpu.make_async_copy(piece(new_in, step), piece(new, step), in_sem.at[step])

    def keep(step):
        return pltpu.make_async_copy(piece(new, step), piece(new_out, step), keep_sem.at[step])

    def hand_out(step):
        return pltpu.make_async_copy(piece(up, step), piece(up_hbm, step), up_sem.at[step])

    smalls[0].wait()
    for r in range(groups):
        line = jnp.concatenate([val_ref[r, c][:, :FIVE * HALF] for c in range(chips)], axis=1)
        for i in range(steps):
            vals[i, r] = line[:, i * LANES:(i + 1) * LANES]
    for copy in smalls[1:]:
        copy.wait()

    def one(step, carry):
        bring(step).start()
        shape = (BLOCK // 8, 8, LANES)
        column = (lax.broadcasted_iota(jnp.int32, shape, 0) * 8 + lax.broadcasted_iota(jnp.int32, shape, 1)).astype(F32)
        powers = []
        for b in range(blocks):
            total = signed = jnp.zeros(shape, F32)
            for r in range(groups):
                off = jnp.broadcast_to(off_ref[r, b, pl.ds(step, 1), :], (8, LANES))
                val = jnp.broadcast_to(vals[step, r, b:b + 1, :], (8, LANES))
                odd = off >= BLOCK
                place = jnp.where(odd, off - BLOCK, off)[None] == column
                total = total + jnp.where(place, val[None], 0.0)
                signed = signed + jnp.where(place, jnp.where(odd, -val, val)[None], 0.0)
            sums[b, :, :LANES] = total.reshape(BLOCK, LANES)
            sums[b, :, LANES:] = signed.reshape(BLOCK, LANES)
            powers.append(jnp.sum(jnp.sum(total * total + signed * signed, axis=0), axis=0, keepdims=True))
        powers = jnp.concatenate(powers + [jnp.zeros((16 - blocks, LANES), F32)], axis=0)
        high, low = split(powers)
        power = dot(jnp.concatenate([high, low], axis=1), seg_ref[...])
        scale = lax.rsqrt(power * (0.5 / (BLOCK * BLOCK)) + EPSILON)
        for b in range(blocks):
            row = jnp.concatenate([scale[b:b + 1]] * 2, axis=1)
            high, low = split(sums[b] * row)
            half = dot(col_ref[...], jnp.concatenate([high, low, high], axis=0))
            high, low = split(half)
            half_ref[b * BLOCK:(b + 1) * BLOCK, :] = jnp.concatenate([high, low, high], axis=1)
        width = half_ref.shape[0]
        for start in range(0, width, 256):
            cut = slice(start, min(start + 256, width))
            field = dot_t(spread_ref[...], half_ref[cut])
            up[pl.ds(pl.multiple_of(step * rows, rows), rows), cut] = field.astype(BF)
        bring(step).wait()
        keep(step).start()
        hand_out(step).start()
        return carry

    lax.fori_loop(0, steps, one, 0)
    for step in range(steps):
        keep(step).wait()
        hand_out(step).wait()


def gather_call(xt, g, mom, picks, t):
    features, width = mom.shape
    reps = picks.shape[0]
    chunks = features // CHUNK
    values = (reps, chunks, LISTED, 2 * LANES)
    offsets = (reps, picks.shape[1], features // (QUAD * BLOCK), LANES)
    small = [picks] + [t[n] for n in NAMES]
    any_space = pl.BlockSpec(memory_space=pl.ANY)
    dma = pltpu.SemaphoreType.DMA
    return pl.pallas_call(
        gather_kernel,
        in_specs=[any_space] * (3 + len(small)),
        out_specs=[any_space] * 3,
        out_shape=[
            jax.ShapeDtypeStruct((features, width), BF),
            jax.ShapeDtypeStruct(values, F32),
            jax.ShapeDtypeStruct(offsets, F32),
        ],
        scratch_shapes=[pltpu.VMEM(a.shape, a.dtype) for a in small] + [
            pltpu.VMEM((features, ROWS), BF),
            pltpu.VMEM(g.shape, BF),
            pltpu.VMEM((features, width), BF),
            pltpu.VMEM((features, width), BF),
            pltpu.VMEM((features, width), F32),
            pltpu.VMEM((features // 2, width), BF),
            pltpu.VMEM((features // 2, width), BF),
            pltpu.VMEM((LANES, LANES), F32),
            pltpu.VMEM((LANES, LANES), F32),
            pltpu.VMEM((chunks, HALF, LANES), F32),
            pltpu.VMEM(offsets, F32),
            pltpu.VMEM(values, F32),
            dma((len(small),)), dma, dma((chunks,)), dma((chunks,)), dma((1 + chunks,)), dma, dma((14,)), dma((14,)), dma((chunks, 2)), dma((chunks, 2)), dma((chunks, reps)), dma((chunks, reps)),
        ],
        compiler_params=pltpu.CompilerParams(vmem_limit_bytes=56 * 2**20, collective_id=0, has_side_effects=True),
    )(xt, g, mom, *small)


def update_call(values, off, new, t):
    groups, blocks, steps = off.shape[:3]
    width = blocks * BLOCK
    small = [values, off] + [t[n] for n in ("columns", "spread", "segment")]
    any_space, dma = pl.BlockSpec(memory_space=pl.ANY), pltpu.SemaphoreType.DMA
    return pl.pallas_call(
        update_kernel,
        in_specs=[any_space] * (len(small) + 1),
        out_specs=[any_space] * 2,
        out_shape=[jax.ShapeDtypeStruct(new.shape, BF)] * 2,
        scratch_shapes=[pltpu.VMEM(a.shape, a.dtype) for a in small] + [
            pltpu.VMEM(new.shape, BF),
            pltpu.VMEM(new.shape, BF),
            pltpu.VMEM((steps, groups, LISTED, LANES), F32),
            pltpu.VMEM((blocks, BLOCK, 2 * LANES), F32),
            pltpu.VMEM((width, 6 * LANES), BF),
            dma((len(small),)), dma((steps,)), dma((steps,)), dma((steps,)),
        ],
        compiler_params=pltpu.CompilerParams(vmem_limit_bytes=60 * 2**20),
    )(*small, new)


def body(tokens, output_grads, momentum, component_picks):
    width = momentum.shape[2]
    t = {name: jnp.asarray(table) for name, table in tables(width, component_picks.shape[1]).items()}
    picks = jnp.transpose(component_picks, (0, 2, 3, 1))
    new_momentum, values, off = gather_call(tokens.T, output_grads, momentum[0], picks, t)
    update, new_momentum = update_call(values, off, new_momentum, t)
    return (new_momentum[None], update)


def solution(mesh):
    return jax.shard_map(
        body,
        mesh=mesh,
        in_specs=(P("rep", "tp"), P("rep", "tp"), P("rep", None, "tp"), P(None, None, "tp", None)),
        out_specs=(P("rep", None, "tp"), P(None, "tp")),
        check_vma=False,
    )
```
